32 devices in a mesh: seq: 8 (over z, y), tensor: 4 (over x, core).
Axes of the slice: x: 2, y: 2, z: 4, core: 2. Of those that a mesh axis runs over, the one named last changes fastest.
Arguments:
- layer_input: bfloat16 [4, 2048, 2048], P(None, 'seq'), may hold values from -6 to 6
- attn_norm: bfloat16 [2048], replicated, may hold values from 0.5 to 1.5
- query_weight: bfloat16 [2048, 2048], P(None, 'tensor'), may hold values from -0.125 to 0.125
- key_weight: bfloat16 [2048, 2048], P(None, 'tensor'), may hold values from -0.125 to 0.125
- value_weight: bfloat16 [2048, 2048], P(None, 'tensor'), may hold values from -0.125 to 0.125
- gate_weight: bfloat16 [2048, 2048], P(None, 'tensor'), may hold values from -0.125 to 0.125
- rank_down: bfloat16 [2048, 16], replicated, may hold values from -0.125 to 0.125
- rank_up: bfloat16 [16, 2048], P(None, 'tensor'), may hold values from -1.5 to 1.5
- decay_bias: bfloat16 [2048], P('tensor')
- head_gain: bfloat16 [2048], P('tensor'), may hold values from 0.5 to 1.5
- out_weight: bfloat16 [2048, 2048], P('tensor'), may hold values from -0.1875 to 0.1875
- mlp_norm: bfloat16 [2048], replicated, may hold values from 0.5 to 1.5
- swish_weight: bfloat16 [2048, 5632], P(None, 'tensor'), may hold values from -0.125 to 0.125
- up_weight: bfloat16 [2048, 5632], P(None, 'tensor'), may hold values from -0.125 to 0.125
- down_weight: bfloat16 [5632, 2048], P('tensor'), may hold values from -0.109375 to 0.109375
- cotangent: bfloat16 [4, 2048, 2048], P(None, 'seq'), may hold values from -6 to 6
Outputs:
- layer_output: bfloat16 [4, 2048, 2048], P(None, 'seq')
- input_grad: bfloat16 [4, 2048, 2048], P(None, 'seq')
- attn_norm_grad: float32 [2048], P('seq')
- query_grad: float32 [2048, 2048], P('seq', 'tensor')
- key_grad: float32 [2048, 2048], P('seq', 'tensor')
- value_grad: float32 [2048, 2048], P('seq', 'tensor')
- gate_grad: float32 [2048, 2048], P('seq', 'tensor')
- rank_down_grad: float32 [2048, 16], P('seq')
- rank_up_grad: float32 [16, 2048], P(None, 'tensor')
- decay_bias_grad: float32 [2048], P('tensor')
- head_gain_grad: float32 [2048], P('tensor')
- out_grad: float32 [2048, 2048], P('tensor', 'seq')
- mlp_norm_grad: float32 [2048], P('seq')
- swish_grad: float32 [2048, 5632], P('seq', 'tensor')
- up_grad: float32 [2048, 5632], P('seq', 'tensor')
- down_grad: float32 [5632, 2048], P('tensor', 'seq')
The draws below stay inside these ranges and needn't reach their ends.
All inputs are finite; a program needn't handle non-finite values.
Results may differ from the reference program's by a relative error of at most 0.025.
Values may be sent and summed in bfloat16 or wider, within the bound.
No kernel may reach another device: no remote copies, remote signals or barrier semaphores. Data moves between devices by JAX's collectives and lax.ppermute only.
A program may use at most 448 MiB of HBM per device.

```python
import math
import jax
import jax.numpy as jnp
from jax import lax

D = 2048
HEADS = 4
DK = 512
FF = 5632
RANK = 16
BLOCK = 64
SEQS = 4
LENGTH = 2048


def draw_decay_bias(key, part):
    key = jax.random.fold_in(key, 7)
    upper = math.log(LENGTH) + 1.0
    return jax.random.uniform(key, (D,), jnp.float32, -1.0, upper).astype(jnp.bfloat16)


def block_levels(key, dims, cuts, low, top_value):
    def one(dim, shards_of):
        steps = jax.random.uniform(jax.random.fold_in(jax.random.fold_in(key, 6), dim), (shards_of,), jnp.float32, low / len(cuts), top_value / len(cuts))
        return jnp.repeat(jnp.exp(steps), dims[dim] // shards_of).reshape((-1,) + (1,) * (len(dims) - dim - 1))

    factor_of = one(*cuts[0])
    for cut in cuts[1:]:
        factor_of = factor_of * one(*cut)
    return factor_of


def gaussian(stream_key, shape, spread, limit, cuts=(), dtype=jnp.bfloat16):
    values = spread * jax.random.normal(stream_key, shape, jnp.float32)
    if cuts:
        values = values * block_levels(stream_key, shape, cuts, -0.22, 0.18)
    return jnp.clip(values, -limit, limit).astype(dtype)


def setup_inputs(seed: int = 0) -> dict:
    seeds = jax.random.split(jax.random.key(seed), 17)
    return {
        "layer_input": gaussian(seeds[0], (SEQS, LENGTH, D), 1.0, 6.0, ((1, 8),)),
        "attn_norm": jnp.clip(1.0 + 0.1 * jax.random.normal(seeds[1], (D,), jnp.float32), 0.5, 1.5).astype(jnp.bfloat16),
        "query_weight": gaussian(seeds[2], (D, D), D ** -0.5, 0.125, ((1, 4),)),
        "key_weight": gaussian(seeds[3], (D, D), D ** -0.5, 0.125, ((1, 4),)),
        "value_weight": gaussian(seeds[4], (D, D), D ** -0.5, 0.125, ((1, 4),)),
        "gate_weight": gaussian(seeds[5], (D, D), D ** -0.5, 0.125, ((1, 4),)),
        "rank_down": gaussian(seeds[6], (D, RANK), D ** -0.5, 0.125),
        "rank_up": gaussian(seeds[7], (RANK, D), RANK ** -0.5, 1.5, ((1, 4),)),
        "decay_bias": draw_decay_bias(jax.random.fold_in(seeds[16], 71), 0),
        "head_gain": jnp.clip(1.0 + 0.1 * jax.random.normal(seeds[9], (D,), jnp.float32), 0.5, 1.5).astype(jnp.bfloat16),
        "out_weight": gaussian(seeds[10], (D, D), (D // 2) ** -0.5, 0.1875, ((0, 4),)),
        "mlp_norm": jnp.clip(1.0 + 0.1 * jax.random.normal(seeds[11], (D,), jnp.float32), 0.5, 1.5).astype(jnp.bfloat16),
        "swish_weight": gaussian(seeds[12], (D, FF), D ** -0.5, 0.125, ((1, 4),)),
        "up_weight": gaussian(seeds[13], (D, FF), D ** -0.5, 0.125, ((1, 4),)),
        "down_weight": gaussian(seeds[14], (FF, D), (FF // 2) ** -0.5, 0.109375, ((0, 4),)),
        "cotangent": gaussian(seeds[15], (SEQS, LENGTH, D), 1.0, 6.0, ((1, 8),)),
    }


@jax.custom_vjp
def low(v):
    return lax.optimization_barrier(v.astype(jnp.bfloat16)).astype(jnp.float32)

@jax.custom_vjp
def low_back(v):
    return v

def low_keep(v):
    return (low(v), None)

def low_pass(kept, grad):
    return (grad,)

def back_keep(v):
    return (v, None)

def back_low(kept, grad):
    return (low(grad),)
low.defvjp(low_keep, low_pass)
low_back.defvjp(back_keep, back_low)
highest_precision = lax.Precision.HIGHEST
epsilon = 1e-06

def matmul(left_rows, right_rows):
    return jnp.dot(left_rows, right_rows, precision=highest_precision)

def normed(values):
    return values * lax.rsqrt(lax.optimization_barrier(jnp.mean(values * values, axis=-1, keepdims=True)) + epsilon)

def block_step(state_matrix, pieces):
    query_rows, key_matrix, value_matrix, decays = pieces
    row_count = query_rows.shape[0]
    running_decay = jnp.cumsum(decays, axis=0)
    positions = jnp.arange(row_count)
    causal = (positions[None, :] <= positions[:, None]).astype(jnp.float32)
    center_decay = running_decay[row_count // 2]
    left_rows = query_rows * jnp.exp(running_decay - center_decay[None])
    right_rows = key_matrix * jnp.exp(center_decay[None] - running_decay)
    scores = jnp.einsum('thk,shk->hts', left_rows, right_rows, precision=highest_precision) * causal[None]
    inner_part = jnp.einsum('hts,shv->thv', scores, value_matrix, precision=highest_precision)
    carried_state = jnp.einsum('xwn,wnl->xwl', query_rows * jnp.exp(running_decay), state_matrix, precision=highest_precision)
    closing_decay = running_decay[-1]
    state_update = jnp.einsum('awy,awq->wyq', key_matrix * jnp.exp(closing_decay[None] - running_decay), value_matrix, precision=highest_precision)
    return (jnp.exp(closing_decay)[:, :, None] * state_matrix + state_update, inner_part + carried_state)

def mix_sequence(pieces):
    query_rows, key_matrix, value_matrix, decays = pieces
    seq_length, head_count, feature_count = query_rows.shape

    def to_blocks(values):
        return values.reshape(seq_length // BLOCK, BLOCK, head_count, feature_count)
    initial = jnp.zeros((head_count, feature_count, feature_count), jnp.float32)
    _, mixed_rows = lax.scan(jax.checkpoint(block_step), initial, (to_blocks(query_rows), to_blocks(key_matrix), to_blocks(value_matrix), to_blocks(decays)))
    return mixed_rows.reshape(seq_length, head_count, feature_count)

def forward(layer_input, attn_norm, query_weight, key_weight, value_weight, gate_weight, rank_down, rank_up, decay_bias, head_gain, out_weight, mlp_norm, swish_weight, up_weight, down_weight):
    seq_count, seq_length, feature_count = layer_input.shape
    row_count = seq_count * seq_length
    flat_input = layer_input.reshape(row_count, feature_count)
    first_norm = low(normed(flat_input) * attn_norm)
    query_rows = low_back(low(matmul(first_norm, query_weight)))
    key_matrix = low_back(low(matmul(first_norm, key_weight)))
    value_matrix = low_back(low(matmul(first_norm, value_weight)))
    rank_rows = low_back(low(matmul(first_norm, rank_down)))
    logits = low_back(matmul(rank_rows, rank_up) + decay_bias)
    decays = jax.nn.log_sigmoid(logits) / 16.0
    gate_rows = low_back(matmul(first_norm, gate_weight))

    def heads_of(values):
        return values.reshape(seq_count, seq_length, HEADS, DK)
    mixed_rows = lax.map(mix_sequence, (heads_of(query_rows) * DK ** (-0.5), heads_of(key_matrix), heads_of(value_matrix), heads_of(decays)))
    shaped = normed(mixed_rows) * head_gain.reshape(HEADS, DK)
    branch = low(shaped.reshape(row_count, feature_count) * jax.nn.silu(gate_rows))
    middle = flat_input + low_back(matmul(branch, out_weight))
    second = low(normed(middle) * mlp_norm)
    swish_rows = low_back(matmul(second, swish_weight))
    up_rows = low_back(matmul(second, up_weight))
    inner_rows = low(jax.nn.silu(swish_rows) * up_rows)
    result = middle + low_back(matmul(inner_rows, down_weight))
    return result.reshape(seq_count, seq_length, feature_count)

def reference(layer_input, attn_norm, query_weight, key_weight, value_weight, gate_weight, rank_down, rank_up, decay_bias, head_gain, out_weight, mlp_norm, swish_weight, up_weight, down_weight, cotangent):
    inputs = (layer_input, attn_norm, query_weight, key_weight, value_weight, gate_weight, rank_down, rank_up, decay_bias, head_gain, out_weight, mlp_norm, swish_weight, up_weight, down_weight)
    inputs = tuple((item.astype(jnp.float32) for item in inputs))
    result, pullback = jax.vjp(forward, *inputs)
    grads = pullback(cotangent.astype(jnp.float32))
    return (result.astype(jnp.bfloat16), grads[0].astype(jnp.bfloat16), grads[1], grads[2], grads[3], grads[4], grads[5], grads[6], grads[7], grads[8], grads[9], grads[10], grads[11], grads[12], grads[13], grads[14])
```

```python
import functools

import jax
import jax.numpy as jnp
from jax import lax
from jax.experimental import pallas as pl
from jax.experimental.pallas import tpu as pltpu
from jax.sharding import PartitionSpec as P

DK = 512
BLOCK = 64
VMEM = 48 * 1024 * 1024

bf16 = jnp.bfloat16
f32 = jnp.float32
highest_precision = lax.Precision.HIGHEST
epsilon = 1e-06


def contract(left, right, left_dim, right_dim, precision=None):
    return lax.dot_general(
        left,
        right,
        (((left_dim,), (right_dim,)), ((), ())),
        preferred_element_type=f32,
        precision=precision,
    )


def product(left, right):
    return contract(left, right, 1, 0)


def across(left, right):
    return contract(left, right, 0, 0)


def against(left, right):
    return contract(left, right, 1, 1)


def forget_logits(rank_ref, up_ref, bias_ref):
    return product(rank_ref[...], up_ref[...]) + bias_ref[...].astype(f32)


def positions(count):
    rows = lax.broadcasted_iota(jnp.int32, (count, count), 0)
    cols = lax.broadcasted_iota(jnp.int32, (count, count), 1)
    return rows, cols


def spread(pieces, size):
    width = pieces[0].shape[1]
    return jnp.concatenate([jnp.broadcast_to(piece, (size, width)) for piece in pieces], axis=0)


def scaled_pair(level, query_scaled, key_rows, run):
    count = run.shape[0]
    if level == 0:
        starts = range(0, count, BLOCK)
        center = spread([run[s + BLOCK // 2 : s + BLOCK // 2 + 1] for s in starts], BLOCK)
        query_factor = jnp.exp(run - center)
        key_factor = jnp.exp(center - run)
        return query_scaled * query_factor, key_rows * key_factor, query_factor, key_factor
    group = BLOCK << level
    half = group // 2
    center = spread([run[s + half - 1 : s + half] for s in range(0, count, group)], group)
    place = lax.broadcasted_iota(jnp.int32, run.shape, 0)
    right = (place % group) >= half
    gap = run - center
    query_factor = jnp.where(right, jnp.exp(jnp.where(right, gap, 0.0)), 0.0)
    key_factor = jnp.where(right, 0.0, jnp.exp(jnp.where(right, 0.0, -gap)))
    return query_scaled * query_factor, key_rows * key_factor, query_factor, key_factor


def level_mask(level, rows, cols):
    if level == 0:
        return (rows // BLOCK == cols // BLOCK) & (cols <= rows)
    group = BLOCK << level
    half = group // 2
    return (rows // group == cols // group) & (rows % group >= half) & (cols % group < half)


def level_count(count):
    levels = 1
    while (BLOCK << (levels - 1)) < count:
        levels += 1
    return levels


def state_kernel(rank_ref, up_ref, bias_ref, key_ref, value_ref, run_ref, state_ref):
    logits = forget_logits(rank_ref, up_ref, bias_ref)
    decays = (jnp.minimum(logits, 0.0) - jnp.log1p(jnp.exp(-jnp.abs(logits)))) * (1.0 / 16.0)
    rows, cols = positions(decays.shape[0])
    run = contract((cols <= rows).astype(f32), decays, 1, 0, highest_precision)
    run_ref[...] = run
    count = run.shape[0]
    left = (key_ref[...].astype(f32) * jnp.exp(run[count - 1 : count] - run)).astype(bf16)
    state_ref[0] = across(value_ref[...], left).astype(bf16)


def score_kernel(query_ref, key_ref, run_ref, score_ref):
    run = run_ref[...]
    query_scaled = query_ref[...].astype(f32) * DK ** (-0.5)
    key_rows = key_ref[...].astype(f32)
    rows, cols = positions(run.shape[0])
    scores = jnp.zeros(rows.shape, f32)
    for level in range(level_count(run.shape[0])):
        left, right, _, _ = scaled_pair(level, query_scaled, key_rows, run)
        scores = jnp.where(
            level_mask(level, rows, cols), against(left.astype(bf16), right.astype(bf16)), scores
        )
    score_ref[0] = scores.astype(bf16)


def whole_state(ref):
    return ref[...].reshape(DK, DK)


def mix_kernel(query_ref, value_ref, run_ref, score_ref, state_ref, gate_ref, gain_ref, mixed_ref, branch_ref):
    faded = (query_ref[...].astype(f32) * DK ** (-0.5) * jnp.exp(run_ref[...])).astype(bf16)
    mixed = product(score_ref[0], value_ref[...]) + against(faded, whole_state(state_ref))
    mixed_ref[...] = mixed
    scale = lax.rsqrt(jnp.mean(mixed * mixed, axis=-1, keepdims=True) + epsilon)
    gate = gate_ref[...]
    branch_ref[...] = (
        mixed * scale * gain_ref[...].astype(f32) * (gate * jax.nn.sigmoid(gate))
    ).astype(bf16)


def branch_back_kernel(
    rows_ref, weight_ref, mixed_ref, gate_ref, gain_ref, query_ref, run_ref,
    gate_back_ref, mixed_back_ref, gain_back_ref, state_back_ref,
):
    branch_grad = against(rows_ref[...], weight_ref[...])
    mixed = mixed_ref[...]
    scale = lax.rsqrt(jnp.mean(mixed * mixed, axis=-1, keepdims=True) + epsilon)
    unit = mixed * scale
    gate = gate_ref[...]
    gain = gain_ref[...].astype(f32)
    sig = jax.nn.sigmoid(gate)
    gate_back_ref[...] = (branch_grad * unit * gain * sig * (1.0 + gate * (1.0 - sig))).astype(bf16)
    shaped_grad = branch_grad * (gate * sig)
    gain_back_ref[0] = jnp.sum(shaped_grad * unit, axis=0, keepdims=True)
    unit_grad = shaped_grad * gain
    mixed_grad = scale * (unit_grad - unit * jnp.mean(unit_grad * unit, axis=-1, keepdims=True))
    mixed_back = mixed_grad.astype(bf16)
    mixed_back_ref[...] = mixed_back
    faded = (query_ref[...].astype(f32) * DK ** (-0.5) * jnp.exp(run_ref[...])).astype(bf16)
    state_back_ref[0] = across(mixed_back, faded).astype(bf16)


def ordered_sum(mask, values):
    high = values.astype(bf16)
    low = (values - high.astype(f32)).astype(bf16)
    ones = mask.astype(f32).astype(bf16)
    return product(ones, high) + product(ones, low)


def mix_back_kernel(
    query_ref, key_ref, value_ref, grad_ref, run_ref, score_ref, state_ref, state_back_ref,
    rank_ref, up_ref, bias_ref,
    query_back_ref, key_back_ref, value_back_ref, logit_back_ref, rank_back_ref, up_back_ref, bias_back_ref,
):
    run = run_ref[...]
    count = run.shape[0]
    query_scaled = query_ref[...].astype(f32) * DK ** (-0.5)
    key_rows = key_ref[...].astype(f32)
    values = value_ref[...]
    grads = grad_ref[...]
    state = whole_state(state_ref)
    state_back = whole_state(state_back_ref)
    rows, cols = positions(count)
    pairs = against(grads, values)

    closing = run[count - 1 : count]
    fade_in = jnp.exp(run)
    fade_out = jnp.exp(closing - run)
    kept = (key_rows * fade_out).astype(bf16)
    value_back_ref[...] = (across(score_ref[0], grads) + against(kept, state_back)).astype(bf16)

    from_state = product(grads, state)
    to_state = product(values, state_back)
    query_back = fade_in * from_state
    key_back = fade_out * to_state
    decay_back = jnp.exp(closing) * jnp.sum(
        state.astype(f32) * state_back.astype(f32), axis=0, keepdims=True
    )
    decay_back = decay_back + ordered_sum(cols >= rows, query_scaled * fade_in * from_state)
    decay_back = decay_back + ordered_sum(cols < rows, key_rows * fade_out * to_state)
    for level in range(level_count(count)):
        left, right, query_factor, key_factor = scaled_pair(level, query_scaled, key_rows, run)
        left, right = left.astype(bf16), right.astype(bf16)
        here = jnp.where(level_mask(level, rows, cols), pairs, 0.0).astype(bf16)
        to_query = product(here, right)
        to_key = across(here, left)
        query_back = query_back + query_factor * to_query
        key_back = key_back + key_factor * to_key
        left_part = left.astype(f32) * to_query
        right_part = right.astype(f32) * to_key
        if level == 0:
            mask = (rows // BLOCK == cols // BLOCK) & (cols >= rows)
            decay_back = decay_back + ordered_sum(mask, left_part - right_part)
        else:
            group = BLOCK << level
            half = group // 2
            same = rows // group == cols // group
            late = same & (rows % group >= half) & (cols >= rows)
            early = same & (rows % group < half) & (cols < rows)
            decay_back = decay_back + ordered_sum(late | early, left_part + right_part)
    query_back_ref[...] = (query_back * DK ** (-0.5)).astype(bf16)
    key_back_ref[...] = key_back.astype(bf16)
    logits = forget_logits(rank_ref, up_ref, bias_ref)
    logit_back = (decay_back * jax.nn.sigmoid(-logits) * (1.0 / 16.0)).astype(bf16)
    logit_back_ref[...] = logit_back
    rank_back_ref[0] = against(up_ref[...], logit_back)
    up_back_ref[0] = across(rank_ref[...], logit_back)
    bias_back_ref[0] = jnp.sum(logit_back.astype(f32), axis=0, keepdims=True)


def prefix_kernel(reverse, totals_ref, parts_ref, out_ref):
    count = parts_ref.shape[0]
    carry = jnp.zeros(parts_ref.shape[2:], f32)
    for step in range(count):
        at = count - 1 - step if reverse else step
        out_ref[at, 0] = carry.astype(bf16)
        carry = carry * jnp.exp(totals_ref[at, 0]) + parts_ref[at, 0].astype(f32)


def grid_call(kernel, grid, in_specs, out_specs, out_shape, flops, moved, *args):
    return pl.pallas_call(
        kernel,
        grid=grid,
        in_specs=in_specs,
        out_specs=out_specs,
        out_shape=out_shape,
        compiler_params=pltpu.CompilerParams(vmem_limit_bytes=VMEM),
        cost_estimate=pl.CostEstimate(flops=flops, bytes_accessed=moved, transcendentals=0),
    )(*args)


def struct(shape, dtype):
    return jax.ShapeDtypeStruct(shape, dtype)


def swap(values, axis, distance):
    count = lax.axis_size(axis)
    return lax.ppermute(values, axis, [(i, i ^ distance) for i in range(count)])


def bits_of(count):
    return [1 << k for k in range(count.bit_length() - 1)]


def spread_totals(values, axis):
    return lax.all_gather(values, axis)


def entering(local_state, totals, reverse):
    count = lax.axis_size("seq")
    seq_count = local_state.shape[0]
    rows = DK // count
    pieces = jnp.moveaxis(local_state.reshape(seq_count, count, rows, DK), 1, 0)
    pieces = lax.all_to_all(pieces, "seq", 0, 0)
    block = pl.BlockSpec((count, 1, rows, DK), lambda b: (0, b, 0, 0))
    carried = grid_call(
        functools.partial(prefix_kernel, reverse),
        (seq_count,),
        [pl.BlockSpec((count, 1, 1, DK), lambda b: (0, b, 0, 0)), block],
        block,
        struct(pieces.shape, bf16),
        2 * pieces.size,
        4 * pieces.size,
        totals,
        pieces,
    )
    return lax.all_to_all(carried, "seq", 0, 0)


def tensor_reduce(near, far):
    third = swap(far[1].astype(bf16), "tensor", 1)
    second = (far[0] + third.astype(f32)).astype(bf16)
    first = swap(near[1].astype(bf16), "tensor", 1)
    return near[0] + first.astype(f32) + swap(second, "tensor", 2).astype(f32)


def tensor_gather(own):
    first = swap(own, "tensor", 1)
    second = swap(own, "tensor", 2)
    third = swap(second, "tensor", 1)
    return jnp.stack([own, first]), jnp.stack([second, third])


def in_order(near, far):
    place = lax.axis_index("tensor")
    blocks = jnp.concatenate([near, far], axis=0)
    return jnp.concatenate(
        [lax.dynamic_index_in_dim(blocks, k ^ place, 0, keepdims=True) for k in range(4)], axis=0
    )


def scatter_grad(left, right, scatter_left, order):
    count = lax.axis_size("seq")
    me = lax.axis_index("seq")
    bits = bits_of(count)
    names = list(reversed(bits))
    rows = left.shape[0]
    cut = left if scatter_left else right
    share = cut.shape[1] // count
    cut = cut.reshape([rows] + [2] * len(bits) + [share])
    remaining = list(names)

    def choose(values, bit, first_axis, mine):
        at = remaining.index(bit) + first_axis
        here = (me // bit) % 2
        return lax.dynamic_index_in_dim(values, here if mine else 1 - here, at, keepdims=False)

    def grad(part):
        part = part.reshape(rows, -1)
        return across(part, right) if scatter_left else across(left, part)

    bit = order[0]
    away = grad(choose(cut, bit, 1, False)).astype(bf16)
    came = swap(away, "seq", bit)
    total = grad(choose(cut, bit, 1, True)) + came.astype(f32)
    remaining.remove(bit)
    for bit in order[1:]:
        total = total.astype(bf16)
        if scatter_left:
            view = total.reshape([2] * len(remaining) + [share, right.shape[1]])
            first_axis = 0
        else:
            view = total.reshape([left.shape[1]] + [2] * len(remaining) + [share])
            first_axis = 1
        came = swap(choose(view, bit, first_axis, False), "seq", bit)
        total = choose(view, bit, first_axis, True).astype(f32) + came.astype(f32)
        remaining.remove(bit)
    return total.reshape((share, right.shape[1]) if scatter_left else (left.shape[1], share))


def sum_over(values, axis):
    for bit in bits_of(lax.axis_size(axis)):
        values = values + swap(values, axis, bit)
    return values


def scatter_sum(values):
    count = lax.axis_size("seq")
    me = lax.axis_index("seq")
    share = values.shape[1] // count
    values = values.reshape(values.shape[0], count, share)
    for bit in reversed(bits_of(count)):
        view = values.reshape(values.shape[0], 2, -1, share)
        here = (me // bit) % 2
        came = swap(lax.dynamic_index_in_dim(view, 1 - here, 1, keepdims=False), "seq", bit)
        values = lax.dynamic_index_in_dim(view, here, 1, keepdims=False) + came
    return values.reshape(values.shape[0], share)


def local(
    layer_input,
    attn_norm,
    query_weight,
    key_weight,
    value_weight,
    gate_weight,
    rank_down,
    rank_up,
    decay_bias,
    head_gain,
    out_weight,
    mlp_norm,
    swish_weight,
    up_weight,
    down_weight,
    cotangent,
):
    seq_count, length, width = layer_input.shape
    place = lax.axis_index("tensor")
    devices = lax.axis_size("seq")
    bits = bits_of(devices)

    def arranged(values):
        return [lax.dynamic_index_in_dim(values, k ^ place, 0, keepdims=False) for k in range(4)]

    input_blocks = arranged(layer_input)
    grad_blocks = arranged(cotangent)
    grad_rows = jnp.concatenate(grad_blocks, axis=0)
    gain_one = attn_norm.astype(f32)
    gain_two = mlp_norm.astype(f32)
    bias = decay_bias.reshape(1, DK)
    gain = head_gain.reshape(1, DK)

    def normed(rows):
        scale = lax.rsqrt(jnp.mean(rows * rows, axis=-1, keepdims=True) + epsilon)
        return rows * scale, scale

    flat = jnp.concatenate(input_blocks, axis=0).astype(f32)
    first_norm = (normed(flat)[0] * gain_one).astype(bf16)
    own_input = input_blocks[0].astype(f32)

    key_rows = product(first_norm, key_weight).astype(bf16)
    value_rows = product(first_norm, value_weight).astype(bf16)
    rank_rows = product(first_norm, rank_down).astype(bf16)
    rank = rank_rows.shape[1]

    def row_spec(width, first=0):
        return pl.BlockSpec((length, width), lambda b: (b + first, 0))

    def fixed(shape):
        return pl.BlockSpec(shape, lambda b: (0,) * len(shape))

    def square(size, first=0):
        return pl.BlockSpec((1, size, size), lambda b: (b + first, 0, 0))

    def chunked(first=0):
        return pl.BlockSpec((devices, 1, DK // devices, DK), lambda b: (0, b + first, 0, 0))

    def line(rows, width, first=0):
        return pl.BlockSpec((1, rows, width), lambda b: (b + first, 0, 0))

    all_rows = seq_count * length
    run, local_state = grid_call(
        state_kernel,
        (seq_count,),
        [row_spec(rank), fixed((rank, DK)), fixed((1, DK)), row_spec(DK), row_spec(DK)],
        [row_spec(DK), square(DK)],
        [struct((all_rows, DK), f32), struct((seq_count, DK, DK), bf16)],
        2 * all_rows * DK * (DK + 6 * length),
        all_rows * DK * 8 + seq_count * DK * DK * 2,
        rank_rows, rank_up, bias, key_rows, value_rows,
    )
    totals = run.reshape(seq_count, length, DK)[:, length - 1 :]
    totals = spread_totals(totals, "seq")
    incoming = entering(local_state, totals, False)

    query_rows = product(first_norm, query_weight).astype(bf16)
    gate_rows = product(first_norm, gate_weight)
    scores = grid_call(
        score_kernel,
        (seq_count,),
        [row_spec(DK), row_spec(DK), row_spec(DK)],
        square(length),
        struct((seq_count, length, length), bf16),
        2 * all_rows * DK * length * 3,
        all_rows * DK * 8 + seq_count * length * length * 2,
        query_rows, key_rows, run,
    )

    half = 2
    half_rows = half * length

    def mix(first):
        return grid_call(
            mix_kernel,
            (half,),
            [
                row_spec(DK, first), row_spec(DK, first), row_spec(DK, first), square(length, first),
                chunked(first), row_spec(DK, first), fixed((1, DK)),
            ],
            [row_spec(DK), row_spec(DK)],
            [struct((half_rows, DK), f32), struct((half_rows, DK), bf16)],
            2 * half_rows * DK * (DK + length),
            half_rows * DK * 18 + half * DK * DK * 2,
            query_rows, value_rows, run, scores, incoming, gate_rows, gain,
        )

    def blocks(values):
        return values.reshape(half, length, values.shape[-1])

    mixed_far, branch_far = mix(half)
    out_far = product(branch_far, out_weight)
    mixed_near, branch_near = mix(0)
    out_near = product(branch_near, out_weight)
    middle = own_input + tensor_reduce(blocks(out_near), blocks(out_far))
    unit_two, scale_two = normed(middle)
    second_own = (unit_two * gain_two).astype(bf16)
    second_near, second_far = tensor_gather(second_own)

    def feed(second, grads):
        second = second.reshape(half_rows, width)
        swish_rows = product(second, swish_weight)
        up_rows = product(second, up_weight)
        sig = jax.nn.sigmoid(swish_rows)
        act = swish_rows * sig
        inner = (act * up_rows).astype(bf16)
        inner_grad = against(grads, down_weight)
        swish_back = (inner_grad * up_rows * sig * (1.0 + swish_rows * (1.0 - sig))).astype(bf16)
        up_back = (inner_grad * act).astype(bf16)
        down = product(inner, down_weight)
        second_grad = against(swish_back, swish_weight) + against(up_back, up_weight)
        return inner, swish_back, up_back, down, second_grad

    inner_near, swish_back_near, up_back_near, down_near, second_grad_near = feed(
        second_near, grad_rows[:half_rows]
    )
    inner_far, swish_back_far, up_back_far, down_far, second_grad_far = feed(
        second_far, grad_rows[half_rows:]
    )
    second_grad = tensor_reduce(blocks(second_grad_near), blocks(second_grad_far))

    join = lambda near, far: jnp.concatenate(
        [near.reshape(half_rows, near.shape[-1]), far.reshape(half_rows, far.shape[-1])], axis=0
    )
    second = join(second_near, second_far)
    down_share = scatter_grad(join(inner_near, inner_far), grad_rows, False, list(reversed(bits)))
    swish_share = scatter_grad(second, join(swish_back_near, swish_back_far), True, bits)
    up_share = scatter_grad(second, join(up_back_near, up_back_far), True, bits)

    mlp_norm_part = jnp.sum(second_grad * unit_two, axis=0, keepdims=True)
    scaled_two = second_grad * gain_two
    middle_grad = grad_blocks[0].astype(f32) + scale_two * (
        scaled_two - unit_two * jnp.mean(scaled_two * unit_two, axis=-1, keepdims=True)
    )
    rows_near, rows_far = tensor_gather(middle_grad.astype(bf16))

    def branch_back(branch_rows, mixed, first):
        return grid_call(
            branch_back_kernel,
            (half,),
            [
                row_spec(width), fixed((DK, width)), row_spec(DK), row_spec(DK, first), fixed((1, DK)),
                row_spec(DK, first), row_spec(DK, first),
            ],
            [row_spec(DK), row_spec(DK), line(1, DK), square(DK)],
            [
                struct((half_rows, DK), bf16), struct((half_rows, DK), bf16),
                struct((half, 1, DK), f32), struct((half, DK, DK), bf16),
            ],
            2 * half_rows * DK * (DK + width),
            half_rows * (width * 2 + DK * 18) + DK * width * 2 + half * DK * DK * 2,
            branch_rows.reshape(half_rows, width), out_weight, mixed, gate_rows, gain, query_rows, run,
        )

    gate_back_near, mixed_back_near, gain_back_near, state_back_near = branch_back(rows_near, mixed_near, 0)
    gate_back_far, mixed_back_far, gain_back_far, state_back_far = branch_back(rows_far, mixed_far, half)
    outgoing = entering(jnp.concatenate([state_back_near, state_back_far], axis=0), totals, True)

    branch = join(branch_near, branch_far)
    branch_rows = join(rows_near, rows_far)
    gate_back = join(gate_back_near, gate_back_far)
    mixed_back = join(mixed_back_near, mixed_back_far)
    out_share = scatter_grad(branch, branch_rows, False, bits)
    gate_share = scatter_grad(first_norm, gate_back, True, bits)

    query_back, key_back, value_back, logit_back, rank_part, up_part, bias_part = grid_call(
        mix_back_kernel,
        (seq_count,),
        [row_spec(DK)] * 5
        + [square(length), chunked(), chunked(), row_spec(rank), fixed((rank, DK)), fixed((1, DK))],
        [row_spec(DK)] * 4 + [line(rank, length), line(rank, DK), line(1, DK)],
        [struct((all_rows, DK), bf16)] * 4
        + [
            struct((seq_count, rank, length), f32),
            struct((seq_count, rank, DK), f32),
            struct((seq_count, 1, DK), f32),
        ],
        2 * all_rows * DK * (3 * DK + 20 * length),
        all_rows * DK * 20 + seq_count * DK * DK * 4,
        query_rows, key_rows, value_rows, mixed_back, run, scores, incoming, outgoing,
        rank_rows, rank_up, bias,
    )

    rank_part = rank_part + swap(rank_part, "tensor", 1)[jnp.array([1, 0, 3, 2])]
    rank_part = rank_part + swap(rank_part, "tensor", 2)[jnp.array([2, 3, 0, 1])]
    rank_back = rank_part.astype(bf16)

    def first_part(rows):
        return (
            against(query_back[rows], query_weight)
            + against(key_back[rows], key_weight)
            + against(value_back[rows], value_weight)
            + against(gate_back[rows], gate_weight)
        )

    first_far = first_part(slice(half_rows, all_rows))
    first_near = first_part(slice(0, half_rows))
    first_grad = tensor_reduce(blocks(first_near), blocks(first_far))
    first_grad = first_grad + contract(rank_back[0], rank_down, 0, 1)
    query_share = scatter_grad(first_norm, query_back, True, bits)
    key_share = scatter_grad(first_norm, key_back, True, bits)
    value_share = scatter_grad(first_norm, value_back, True, list(reversed(bits)))

    unit_one, scale_one = normed(own_input)
    attn_norm_part = jnp.sum(first_grad * unit_one, axis=0, keepdims=True)
    scaled_one = first_grad * gain_one
    input_rows = middle_grad + scale_one * (
        scaled_one - unit_one * jnp.mean(scaled_one * unit_one, axis=-1, keepdims=True)
    )
    input_grad = in_order(*tensor_gather(input_rows.astype(bf16)))

    down_sum = tensor_reduce(blocks(down_near), blocks(down_far))
    layer_output = in_order(*tensor_gather((middle + down_sum).astype(bf16)))

    rank_down_part = sum(
        contract(rank_back[k], first_norm[k * length : (k + 1) * length], 1, 0) for k in range(seq_count)
    )
    mlp_norm_part = sum_over(mlp_norm_part, "tensor")
    early = scatter_sum(jnp.concatenate([rank_down_part, mlp_norm_part], axis=0))
    attn_norm_share = scatter_sum(sum_over(attn_norm_part, "tensor")).reshape(-1)
    gain_back = sum(gain_back_near) + sum(gain_back_far)
    sums = jnp.concatenate([sum(up_part), sum(bias_part), gain_back], axis=0)
    sums = sum_over(sums, "seq")
    return (
        layer_output,
        input_grad,
        attn_norm_share,
        query_share,
        key_share,
        value_share,
        gate_share,
        early[:rank].T,
        sums[:rank],
        sums[rank],
        sums[rank + 1],
        out_share,
        early[rank],
        swish_share,
        up_share,
        down_share,
    )


def solution(mesh):
    return jax.shard_map(
        local,
        mesh=mesh,
        in_specs=(
            P(None, "seq", None),
            P(),
            P(None, "tensor"),
            P(None, "tensor"),
            P(None, "tensor"),
            P(None, "tensor"),
            P(),
            P(None, "tensor"),
            P("tensor"),
            P("tensor"),
            P("tensor", None),
            P(),
            P(None, "tensor"),
            P(None, "tensor"),
            P("tensor", None),
            P(None, "seq", None),
        ),
        out_specs=(
            P(None, "seq", None),
            P(None, "seq", None),
            P("seq"),
            P("seq", "tensor"),
            P("seq", "tensor"),
            P("seq", "tensor"),
            P("seq", "tensor"),
            P("seq", None),
            P(None, "tensor"),
            P("tensor"),
            P("tensor"),
            P("tensor", "seq"),
            P("seq"),
            P("seq", "tensor"),
            P("seq", "tensor"),
            P("tensor", "seq"),
        ),
        check_vma=False,
    )
```

```python
import functools

import jax
import jax.numpy as jnp
from jax import lax
from jax.experimental import pallas as pl
from jax.experimental.pallas import tpu as pltpu
from jax.sharding import PartitionSpec as P

DK = 512
BLOCK = 64
EXTRA = 16
ROWS = 256
COST = 1024
VMEM = 48 * 1024 * 1024

bf16 = jnp.bfloat16
f32 = jnp.float32
highest_precision = lax.Precision.HIGHEST
epsilon = 1e-06


def contract(left, right, left_dim, right_dim, precision=None):
    return lax.dot_general(
        left,
        right,
        (((left_dim,), (right_dim,)), ((), ())),
        preferred_element_type=f32,
        precision=precision,
    )


def product(left, right):
    return contract(left, right, 1, 0)


def across(left, right):
    return contract(left, right, 0, 0)


def against(left, right):
    return contract(left, right, 1, 1)


def forget_logits(rank_ref, up_ref, bias_ref):
    return product(rank_ref[...], up_ref[...]) + bias_ref[...].astype(f32)


def positions(count):
    rows = lax.broadcasted_iota(jnp.int32, (count, count), 0)
    cols = lax.broadcasted_iota(jnp.int32, (count, count), 1)
    return rows, cols


def spread(pieces, size):
    width = pieces[0].shape[1]
    return jnp.concatenate([jnp.broadcast_to(piece, (size, width)) for piece in pieces], axis=0)


def scaled_pair(level, query_scaled, key_rows, run):
    count = run.shape[0]
    if level == 0:
        starts = range(0, count, BLOCK)
        center = spread([run[s + BLOCK // 2 : s + BLOCK // 2 + 1] for s in starts], BLOCK)
        query_factor = jnp.exp(run - center)
        key_factor = jnp.exp(center - run)
        return query_scaled * query_factor, key_rows * key_factor, query_factor, key_factor
    group = BLOCK << level
    half = group // 2
    center = spread([run[s + half - 1 : s + half] for s in range(0, count, group)], group)
    place = lax.broadcasted_iota(jnp.int32, run.shape, 0)
    right = (place % group) >= half
    gap = run - center
    query_factor = jnp.where(right, jnp.exp(jnp.where(right, gap, 0.0)), 0.0)
    key_factor = jnp.where(right, 0.0, jnp.exp(jnp.where(right, 0.0, -gap)))
    return query_scaled * query_factor, key_rows * key_factor, query_factor, key_factor


def level_mask(level, rows, cols):
    if level == 0:
        return (rows // BLOCK == cols // BLOCK) & (cols <= rows)
    group = BLOCK << level
    half = group // 2
    return (rows // group == cols // group) & (rows % group >= half) & (cols % group < half)


def level_count(count):
    levels = 1
    while (BLOCK << (levels - 1)) < count:
        levels += 1
    return levels


def norm_kernel(order_ref, input_ref, grad_ref, gain_ref, norm_ref, rows_ref):
    values = input_ref[0].astype(f32)
    scale = lax.rsqrt(jnp.mean(values * values, axis=-1, keepdims=True) + epsilon)
    norm_ref[...] = (values * scale * gain_ref[...].astype(f32)).astype(bf16)
    rows_ref[...] = grad_ref[0]


def decay_kernel(rank_ref, up_ref, bias_ref, run_ref):
    logits = forget_logits(rank_ref, up_ref, bias_ref)
    decays = (jnp.minimum(logits, 0.0) - jnp.log1p(jnp.exp(-jnp.abs(logits)))) * (1.0 / 16.0)
    rows, cols = positions(decays.shape[0])
    run_ref[...] = contract((cols <= rows).astype(f32), decays, 1, 0, highest_precision)


def state_kernel(key_ref, value_ref, run_ref, state_ref):
    run = run_ref[...]
    count = run.shape[0]
    total = run[count - 1 : count]
    left = (key_ref[...].astype(f32) * jnp.exp(total - run)).astype(bf16)
    devices, _, rows, _ = state_ref.shape
    state = across(value_ref[...], left).astype(bf16).reshape(devices, rows - EXTRA, DK)
    high = total.astype(bf16)
    rest = total - high.astype(f32)
    middle = rest.astype(bf16)
    low = (rest - middle.astype(f32)).astype(bf16)
    place = lax.broadcasted_iota(jnp.int32, (EXTRA, DK), 0)
    lines = jnp.zeros((EXTRA, DK), f32)
    for at, line in enumerate((high, middle, low)):
        lines = jnp.where(place == at, line.astype(f32), lines)
    lines = lines.astype(bf16)
    for at in range(devices):
        state_ref[at, 0, : rows - EXTRA] = state[at]
        state_ref[at, 0, rows - EXTRA :] = lines


def score_kernel(query_ref, key_ref, run_ref, score_ref):
    run = run_ref[...]
    query_scaled = query_ref[...].astype(f32) * DK ** (-0.5)
    key_rows = key_ref[...].astype(f32)
    rows, cols = positions(run.shape[0])
    scores = jnp.zeros(rows.shape, f32)
    for level in range(level_count(run.shape[0])):
        left, right, _, _ = scaled_pair(level, query_scaled, key_rows, run)
        scores = jnp.where(
            level_mask(level, rows, cols), against(left.astype(bf16), right.astype(bf16)), scores
        )
    score_ref[0] = scores.astype(bf16)


def whole_state(ref):
    return ref[...].reshape(DK, DK)


def faded_queries(query_ref, run_ref):
    return (query_ref[...].astype(f32) * DK ** (-0.5) * jnp.exp(run_ref[...])).astype(bf16)


def mix_kernel(query_ref, value_ref, run_ref, score_ref, state_ref, gate_ref, gain_ref, mixed_ref, branch_ref):
    faded = faded_queries(query_ref, run_ref)
    mixed = product(score_ref[0], value_ref[...]) + against(faded, whole_state(state_ref))
    mixed_ref[...] = mixed
    scale = lax.rsqrt(jnp.mean(mixed * mixed, axis=-1, keepdims=True) + epsilon)
    gate = gate_ref[...]
    branch_ref[...] = (
        mixed * scale * gain_ref[...].astype(f32) * (gate * jax.nn.sigmoid(gate))
    ).astype(bf16)


def branch_back_kernel(
    first_ref, second_ref, weight_ref, mixed_ref, gate_ref, gain_ref, query_ref, run_ref,
    gate_back_ref, mixed_back_ref, gain_back_ref, state_back_ref,
):
    branch_grad = against(either(first_ref, second_ref), weight_ref[...])
    mixed = mixed_ref[...]
    scale = lax.rsqrt(jnp.mean(mixed * mixed, axis=-1, keepdims=True) + epsilon)
    unit = mixed * scale
    gate = gate_ref[...]
    gain = gain_ref[...].astype(f32)
    sig = jax.nn.sigmoid(gate)
    gate_back_ref[...] = (branch_grad * unit * gain * sig * (1.0 + gate * (1.0 - sig))).astype(bf16)
    shaped_grad = branch_grad * (gate * sig)
    gain_back_ref[0] = jnp.sum(shaped_grad * unit, axis=0, keepdims=True)
    unit_grad = shaped_grad * gain
    mixed_grad = scale * (unit_grad - unit * jnp.mean(unit_grad * unit, axis=-1, keepdims=True))
    mixed_back = mixed_grad.astype(bf16)
    mixed_back_ref[...] = mixed_back
    faded = faded_queries(query_ref, run_ref)
    state_back_ref[...] = across(mixed_back, faded).astype(bf16).reshape(state_back_ref.shape)


def ordered_sum(mask, values):
    high = values.astype(bf16)
    low = (values - high.astype(f32)).astype(bf16)
    ones = mask.astype(f32).astype(bf16)
    return product(ones, high) + product(ones, low)


def mix_back_kernel(
    query_ref, key_ref, value_ref, grad_ref, run_ref, score_ref, state_ref, state_back_ref,
    rank_ref, up_ref, bias_ref,
    query_back_ref, key_back_ref, value_back_ref, rank_back_ref, up_back_ref, bias_back_ref,
):
    run = run_ref[...]
    count = run.shape[0]
    query_scaled = query_ref[...].astype(f32) * DK ** (-0.5)
    key_rows = key_ref[...].astype(f32)
    values = value_ref[...]
    grads = grad_ref[...]
    state = whole_state(state_ref)
    state_back = whole_state(state_back_ref)
    rows, cols = positions(count)
    pairs = against(grads, values)

    closing = run[count - 1 : count]
    fade_in = jnp.exp(run)
    fade_out = jnp.exp(closing - run)
    kept = (key_rows * fade_out).astype(bf16)
    value_back_ref[...] = (across(score_ref[0], grads) + against(kept, state_back)).astype(bf16)

    from_state = product(grads, state)
    to_state = product(values, state_back)
    query_back = fade_in * from_state
    key_back = fade_out * to_state
    decay_back = jnp.exp(closing) * jnp.sum(
        state.astype(f32) * state_back.astype(f32), axis=0, keepdims=True
    )
    decay_back = decay_back + ordered_sum(cols >= rows, query_scaled * fade_in * from_state)
    decay_back = decay_back + ordered_sum(cols < rows, key_rows * fade_out * to_state)
    for level in range(level_count(count)):
        left, right, query_factor, key_factor = scaled_pair(level, query_scaled, key_rows, run)
        left, right = left.astype(bf16), right.astype(bf16)
        here = jnp.where(level_mask(level, rows, cols), pairs, 0.0).astype(bf16)
        to_query = product(here, right)
        to_key = across(here, left)
        query_back = query_back + query_factor * to_query
        key_back = key_back + key_factor * to_key
        left_part = left.astype(f32) * to_query
        right_part = right.astype(f32) * to_key
        if level == 0:
            mask = (rows // BLOCK == cols // BLOCK) & (cols >= rows)
            decay_back = decay_back + ordered_sum(mask, left_part - right_part)
        else:
            group = BLOCK << level
            half = group // 2
            same = rows // group == cols // group
            late = same & (rows % group >= half) & (cols >= rows)
            early = same & (rows % group < half) & (cols < rows)
            decay_back = decay_back + ordered_sum(late | early, left_part + right_part)
    query_back_ref[...] = (query_back * DK ** (-0.5)).astype(bf16)
    key_back_ref[...] = key_back.astype(bf16)
    logits = forget_logits(rank_ref, up_ref, bias_ref)
    logit_back = (decay_back * jax.nn.sigmoid(-logits) * (1.0 / 16.0)).astype(bf16)
    rank_back_ref[0] = against(up_ref[...], logit_back)
    up_back_ref[0] = across(rank_ref[...], logit_back)
    bias_back_ref[0] = jnp.sum(logit_back.astype(f32), axis=0, keepdims=True)


def prefix_kernel(reverse, lines_ref, parts_ref, out_ref):
    count = parts_ref.shape[0]
    rows = out_ref.shape[2]
    carry = jnp.zeros(out_ref.shape[2:], f32)
    for step in range(count):
        at = count - 1 - step if reverse else step
        out_ref[at, 0] = carry.astype(bf16)
        lines = lines_ref[at, 0].astype(f32)
        total = lines[0:1] + lines[1:2] + lines[2:3]
        carry = carry * jnp.exp(total) + parts_ref[at, 0, :rows].astype(f32)


def hold_kernel(values_ref, out_ref):
    out_ref[...] = values_ref[...]


def either(first_ref, second_ref):
    return jnp.where(pl.program_id(0) == 0, first_ref[...], second_ref[...])


def middle_kernel(place_ref, input_ref, own_ref, first_ref, last_ref, gain_ref, middle_ref, second_ref):
    middle = input_ref[0].astype(f32) + (
        own_ref[...].astype(f32) + first_ref[...].astype(f32) + last_ref[...].astype(f32)
    )
    middle_ref[...] = middle
    scale = lax.rsqrt(jnp.mean(middle * middle, axis=-1, keepdims=True) + epsilon)
    second_ref[...] = (middle * scale * gain_ref[...].astype(f32)).astype(bf16)


def norm_back(values, grad, gain):
    scale = lax.rsqrt(jnp.mean(values * values, axis=-1, keepdims=True) + epsilon)
    unit = values * scale
    scaled = grad * gain
    back = scale * (scaled - unit * jnp.mean(scaled * unit, axis=-1, keepdims=True))
    return back, jnp.sum(grad * unit, axis=0, keepdims=True)


def add_part(out_ref, part):
    @pl.when(pl.program_id(0) == 0)
    def _():
        out_ref[...] = part

    @pl.when(pl.program_id(0) != 0)
    def _():
        out_ref[...] += part


def middle_back_kernel(
    place_ref, grad_ref, own_ref, first_ref, last_ref, middle_ref, gain_ref, back_ref, rows_ref, part_ref
):
    grad = own_ref[...].astype(f32) + first_ref[...].astype(f32) + last_ref[...].astype(f32)
    back, part = norm_back(middle_ref[...], grad, gain_ref[...].astype(f32))
    back = grad_ref[0].astype(f32) + back
    back_ref[...] = back
    rows_ref[...] = back.astype(bf16)
    add_part(part_ref, part)


def input_back_kernel(
    place_ref, input_ref, own_ref, first_ref, last_ref, rank_ref, down_ref, middle_ref, gain_ref, rows_ref, part_ref
):
    grad = own_ref[...].astype(f32) + first_ref[...].astype(f32) + last_ref[...].astype(f32)
    grad = grad + contract(rank_ref[...], down_ref[...], 0, 1)
    back, part = norm_back(input_ref[0].astype(f32), grad, gain_ref[...].astype(f32))
    rows_ref[...] = (middle_ref[...] + back).astype(bf16)
    add_part(part_ref, part)


def feed_kernel(
    first_ref, second_ref, grads_ref, swish_ref, up_ref, down_ref,
    inner_ref, swish_back_ref, up_back_ref, second_back_ref, out_ref,
    swish_held, up_held, down_held, semaphores,
):
    copies = [
        pltpu.make_async_copy(swish_ref, swish_held, semaphores.at[0]),
        pltpu.make_async_copy(up_ref, up_held, semaphores.at[1]),
        pltpu.make_async_copy(down_ref, down_held, semaphores.at[2]),
    ]
    start = pl.program_id(0) == 0

    @pl.when(start)
    def _():
        for copy in copies:
            copy.start()

    rows = either(first_ref, second_ref)

    @pl.when(start)
    def _():
        copies[0].wait()

    swish = product(rows, swish_held[...])

    @pl.when(start)
    def _():
        copies[1].wait()

    up = product(rows, up_held[...])
    sig = jax.nn.sigmoid(swish)
    act = swish * sig
    inner = (act * up).astype(bf16)
    inner_ref[...] = inner

    @pl.when(start)
    def _():
        copies[2].wait()

    inner_grad = against(grads_ref[...], down_held[...])
    swish_back = (inner_grad * up * sig * (1.0 + swish * (1.0 - sig))).astype(bf16)
    up_back = (inner_grad * act).astype(bf16)
    swish_back_ref[...] = swish_back
    up_back_ref[...] = up_back
    second_back_ref[...] = (against(swish_back, swish_held[...]) + against(up_back, up_held[...])).astype(bf16)
    out_ref[...] = product(inner, down_held[...]).astype(bf16)


def place_kernel(order_ref, *refs):
    out_ref = refs[-1]
    step = pl.program_id(0)
    for k in range(4):

        @pl.when(step == k)
        def _():
            out_ref[0] = refs[k][...]


def sum_kernel(count, *refs):
    out_ref = refs[-1]
    total = against(refs[0][...], refs[count][...])
    for k in range(1, count):
        total = total + against(refs[k][...], refs[count + k][...])
    out_ref[...] = total.astype(out_ref.dtype)


def grad_kernel(parts, groups, turned, pick_ref, *refs):
    cuts, refs = refs[:parts], refs[parts:]
    others, refs = refs[: parts * groups], refs[parts * groups :]
    arrived, out_ref = refs[:-1], refs[-1]
    for group in range(groups):
        total = None
        members = others[group * parts : (group + 1) * parts]
        width = members[0].shape[1]
        columns = slice(group * width, (group + 1) * width)
        for cut, other in zip(cuts, members):
            part = across(cut[...], other[...])
            total = part if total is None else total + part
        for ref in arrived:
            total = total + ref[0, :, columns].astype(f32)
        if turned:
            out_ref[...] = total.T
        else:
            out_ref[0, :, columns] = total.astype(out_ref.dtype)


def struct(shape, dtype):
    return jax.ShapeDtypeStruct(shape, dtype)


def grid_call(kernel, grid, in_specs, out_specs, out_shape, args, prefetch=0, after=(), scratch=(), into=None):
    first, last = len(args), len(args) + len(after)
    aliases = {}
    if into is not None:
        aliases = {last: into[1]}
        after = (*after, into[0])
        last += 1

    def run(*refs):
        kernel(*refs[:first], *refs[last:])

    return pl.pallas_call(
        run,
        grid_spec=pltpu.PrefetchScalarGridSpec(
            num_scalar_prefetch=prefetch,
            grid=grid,
            in_specs=list(in_specs) + [pl.BlockSpec(memory_space=pl.ANY)] * len(after),
            out_specs=out_specs,
            scratch_shapes=list(scratch),
        ),
        out_shape=out_shape,
        input_output_aliases=aliases,
        compiler_params=pltpu.CompilerParams(vmem_limit_bytes=VMEM),
        cost_estimate=pl.CostEstimate(flops=COST, bytes_accessed=COST, transcendentals=0),
    )(*args, *after)


def swap(values, axis, distance):
    count = lax.axis_size(axis)
    return lax.ppermute(values, axis, [(i, i ^ distance) for i in range(count)])


def region(function, *args):
    shapes = jax.eval_shape(function, *args)

    def never(*_):
        return jax.tree.map(lambda a: jnp.zeros(a.shape, a.dtype), shapes)

    return lax.cond(lax.axis_index("seq") >= 0, function, never, *args)


def bits_of(count):
    return [1 << k for k in range(count.bit_length() - 1)]


def hold(values, after):
    spec = pl.BlockSpec(values.shape, lambda: (0,) * values.ndim)
    return grid_call(hold_kernel, (), [spec], spec, struct(values.shape, values.dtype), [values], after=after)


def chunk_spec(count, extra=0, first=0):
    return pl.BlockSpec((count, 1, DK // count + extra, DK), lambda b, *_: (0, b + first, 0, 0))


def carried(pieces, lines, reverse, after=()):
    count, seq_count, rows, _ = pieces.shape
    share = DK // count
    return grid_call(
        functools.partial(prefix_kernel, reverse),
        (seq_count,),
        [
            pl.BlockSpec((count, 1, EXTRA, DK), lambda b: (0, b, share // EXTRA, 0)),
            chunk_spec(count, rows - share),
        ],
        chunk_spec(count),
        struct((count, seq_count, share, DK), bf16),
        [lines, pieces],
        after=after,
    )


def deal(pieces):
    return lax.all_to_all(pieces, "seq", 0, 0)


def tensor_reduce(near, far):
    third = swap(far[1], "tensor", 1)
    second = (far[0].astype(f32) + third.astype(f32)).astype(bf16)
    first = swap(near[1], "tensor", 1)
    return (near[0], first, swap(second, "tensor", 2)), second


def tensor_gather(own):
    first = swap(own, "tensor", 1)
    second = swap(own, "tensor", 2)

    def third(after):
        return swap(hold(second, after) if after else second, "tensor", 1)

    return own, first, second, third


def in_order(blocks, order, after=()):
    length, width = blocks[0].shape
    whole = pl.BlockSpec((length, width), lambda k, order: (0, 0))
    return grid_call(
        place_kernel,
        (4,),
        [whole] * 4,
        pl.BlockSpec((1, length, width), lambda k, order: (order[k], 0, 0)),
        struct((4, length, width), blocks[0].dtype),
        [order, *blocks],
        prefetch=1,
        after=after,
    )


def grad_part(cuts, groups, picks, arrived, dtype, turned=False, after=()):
    rows = ROWS
    width = groups[0][0][0].shape[1]
    whole = width * len(groups)
    share = cuts[0][0].shape[1] // lax.axis_size("seq")
    chunks = len(picks)
    me = lax.axis_index("seq")
    index = jnp.stack([me ^ r for r in picks]).astype(jnp.int32)
    others = [block for group in groups for block in group]
    in_specs = [pl.BlockSpec((rows, share), lambda k, pick, at=at: (at, pick[k])) for _, at in cuts]
    in_specs += [pl.BlockSpec((rows, width), lambda k, pick, at=at: (at, 0)) for _, at in others]
    for _, first in arrived:
        in_specs.append(pl.BlockSpec((1, share, whole), lambda k, pick, first=first: (k + first, 0, 0)))
    if turned:
        out_spec = pl.BlockSpec((whole, share), lambda k, pick: (0, 0))
        shape = (whole, share)
    else:
        out_spec = pl.BlockSpec((1, share, whole), lambda k, pick: (k, 0, 0))
        shape = (chunks, share, whole)
    return grid_call(
        functools.partial(grad_kernel, len(cuts), len(groups), turned),
        (chunks,),
        in_specs,
        out_spec,
        struct(shape, dtype),
        [index, *[a for a, _ in cuts], *[a for a, _ in others], *[a for a, _ in arrived]],
        prefetch=1,
        after=after,
    )


class Scatter:
    def __init__(self, cuts, groups, order, turned=False):
        self.cuts, self.groups, self.order, self.turned = cuts, groups, order, turned
        self.split = lax.axis_size("seq") == 8

    def part(self, picks, arrived, dtype, turned=False, after=()):
        return grad_part(self.cuts, self.groups, picks, arrived, dtype, turned, after)

    def send(self, after=()):
        if not self.split:
            total = jnp.concatenate(
                [
                    sum(
                        across(a[i * ROWS : (i + 1) * ROWS], b[j * ROWS : (j + 1) * ROWS])
                        for (a, i), (b, j) in zip(self.cuts, group)
                    ).astype(bf16)
                    for group in self.groups
                ],
                axis=1,
            )
            self.total = lax.psum_scatter(total, "seq", scatter_dimension=0, tiled=True).astype(f32)
            return self.total
        a, b, c = self.order
        away = self.part([a ^ b, a ^ b ^ c, a ^ c, a], [], bf16, after=after)
        self.came = swap(away, "seq", a)
        return away

    def step_one(self, after=()):
        if not self.split:
            return self.total
        a, b, c = self.order
        first = self.part([b, b ^ c], [(self.came, 0)], bf16, after=after)
        self.came_first = swap(first, "seq", b)
        return first

    def step_two(self, after=()):
        if not self.split:
            return self.total
        a, b, c = self.order
        second = self.part([c], [(self.came, 2), (self.came_first, 1)], bf16, after=after)
        self.came_second = swap(second, "seq", c)
        return second

    def last(self, after=()):
        if not self.split:
            return self.total.T if self.turned else self.total
        total = self.part(
            [0],
            [(self.came, 3), (self.came_first, 0), (self.came_second, 0)],
            f32,
            self.turned,
            after=after,
        )
        return total if self.turned else total[0]


def product_sum(pairs, dtype, after=()):
    rows = pairs[0][0].shape[0]
    width = pairs[0][1].shape[0]
    tile = 512
    in_specs = [pl.BlockSpec((rows, p[0].shape[1]), lambda j: (0, 0)) for p in pairs]
    in_specs += [pl.BlockSpec((tile, p[1].shape[1]), lambda j: (j, 0)) for p in pairs]
    return grid_call(
        functools.partial(sum_kernel, len(pairs)),
        (width // tile,),
        in_specs,
        pl.BlockSpec((rows, tile), lambda j: (0, j)),
        struct((rows, width), dtype),
        [p[0] for p in pairs] + [p[1] for p in pairs],
        after=after,
    )


def sum_over(values, axis):
    for bit in bits_of(lax.axis_size(axis)):
        values = values + swap(values, axis, bit)
    return values


def spread_sum(values):
    return jnp.sum(lax.all_to_all(values, "seq", 0, 0), axis=0)


def local(
    layer_input,
    attn_norm,
    query_weight,
    key_weight,
    value_weight,
    gate_weight,
    rank_down,
    rank_up,
    decay_bias,
    head_gain,
    out_weight,
    mlp_norm,
    swish_weight,
    up_weight,
    down_weight,
    cotangent,
):
    seq_count, length, width = layer_input.shape
    place = lax.axis_index("tensor")
    devices = lax.axis_size("seq")
    half = seq_count // 2
    half_rows = half * length
    rank = rank_down.shape[1]
    bias = decay_bias.reshape(1, DK)
    gain = head_gain.reshape(1, DK)
    share = DK // devices

    def row_spec(size):
        return pl.BlockSpec((length, size), lambda b, *_: (b, 0))

    def fixed(shape):
        return pl.BlockSpec(shape, lambda b, *_: (0,) * len(shape))

    def square(size):
        return pl.BlockSpec((1, size, size), lambda b, *_: (b, 0, 0))

    def line(rows, size):
        return pl.BlockSpec((1, rows, size), lambda b, *_: (b, 0, 0))

    def rows_of(size, dtype):
        return struct((half_rows, size), dtype)

    chunks = struct((devices, seq_count, share, DK), bf16)
    whole_block = pl.BlockSpec((length, width), lambda b, *_: (0, 0))

    def blocks(near, far):
        return [(near, 0), (near, 1), (far, 0), (far, 1)]

    def halves(values):
        return values[:length], values[length:]

    def first_rows(order, after=()):
        spec = pl.BlockSpec((1, length, width), lambda b, order: (order[b], 0, 0))
        return grid_call(
            norm_kernel,
            (half,),
            [spec, spec, fixed((1, width))],
            [row_spec(width), row_spec(width)],
            [rows_of(width, bf16), rows_of(width, bf16)],
            [order, layer_input, cotangent, attn_norm.reshape(1, width)],
            prefetch=1,
            after=after,
        )

    def decays(norm):
        rank_rows = product(norm, rank_down).astype(bf16)
        run = grid_call(
            decay_kernel,
            (half,),
            [row_spec(rank), fixed((rank, DK)), fixed((1, DK))],
            row_spec(DK),
            rows_of(DK, f32),
            [rank_rows, rank_up, bias],
        )
        return rank_rows, run

    def states(norm, run, at, into=None):
        keys = product(norm, key_weight).astype(bf16)
        values = product(norm, value_weight).astype(bf16)
        state = grid_call(
            state_kernel,
            (half,),
            [row_spec(DK)] * 3,
            chunk_spec(devices, EXTRA, at),
            struct((devices, seq_count, share + EXTRA, DK), bf16),
            [keys, values, run],
            into=None if into is None else (into, 0),
        )
        return keys, values, state

    def scored(norm, keys, run, after=()):
        queries = product(norm, query_weight).astype(bf16)
        gates = product(norm, gate_weight)
        scores = grid_call(
            score_kernel,
            (half,),
            [row_spec(DK)] * 3,
            square(length),
            struct((half, length, length), bf16),
            [queries, keys, run],
            after=after,
        )
        return queries, gates, scores

    def mix(queries, values, run, scores, incoming, at, gates, after=()):
        return grid_call(
            mix_kernel,
            (half,),
            [row_spec(DK)] * 3
            + [square(length), chunk_spec(devices, 0, at), row_spec(DK), fixed((1, DK))],
            [row_spec(DK), row_spec(DK)],
            [rows_of(DK, f32), rows_of(DK, bf16)],
            [queries, values, run, scores, incoming, gates, gain],
            after=after,
        )

    order = jnp.arange(seq_count, dtype=jnp.int32) ^ place
    place_index = order[:1]
    norm_far, grads_far = first_rows(order[half:])
    rank_far, run_far = decays(norm_far)
    keys_far, values_far, state = states(norm_far, run_far, 0)
    norm_near, grads_near = first_rows(order[:half])
    rank_near, run_near = decays(norm_near)
    keys_near, values_near, state = states(norm_near, run_near, half, state)
    queries_far, gates_far, scores_far = scored(norm_far, keys_far, run_far, [state])
    queries_near, gates_near, scores_near = scored(norm_near, keys_near, run_near, [scores_far])
    lines = deal(state)
    incoming = deal(carried(lines, lines, False, [scores_far, gates_far, scores_near, gates_near]))

    mixed_far, branch_far = mix(queries_far, values_far, run_far, scores_far, incoming, 0, gates_far)
    out_far = product(branch_far, out_weight).astype(bf16)
    out_third = swap(out_far[length:], "tensor", 1)
    out_second = (out_far[:length].astype(f32) + out_third.astype(f32)).astype(bf16)
    out_last = swap(out_second, "tensor", 2)
    mixed_near, branch_near = mix(
        queries_near, values_near, run_near, scores_near, incoming, half, gates_near, [out_second]
    )
    out_near = product(branch_near, out_weight).astype(bf16)
    out_parts = (out_near[:length], swap(out_near[length:], "tensor", 1), out_last)

    tile = 128
    tiles = (length // tile,)
    tile_spec = pl.BlockSpec((tile, width), lambda b, *_: (b, 0))
    own_spec = pl.BlockSpec((1, tile, width), lambda b, place: (place[0], b, 0))
    gain_two = mlp_norm.reshape(1, width)
    middle, second_own = grid_call(
        middle_kernel,
        tiles,
        [own_spec] + [tile_spec] * 3 + [fixed((1, width))],
        [tile_spec] * 2,
        [struct((length, width), f32), struct((length, width), bf16)],
        [place_index, layer_input, *out_parts, gain_two],
        prefetch=1,
    )
    *seconds, second_third = tensor_gather(second_own)

    hidden = swish_weight.shape[1]
    anywhere = pl.BlockSpec(memory_space=pl.ANY)

    def feed(rows, grads, at, after=()):
        count = len(rows)
        return grid_call(
            feed_kernel,
            (count,),
            [whole_block] * 2
            + [pl.BlockSpec((length, width), lambda b: (b + at, 0))]
            + [anywhere] * 3,
            [row_spec(hidden)] * 3 + [row_spec(width)] * 2,
            [struct((count * length, hidden), bf16)] * 3 + [struct((count * length, width), bf16)] * 2,
            [rows[0], rows[-1], grads, swish_weight, up_weight, down_weight],
            scratch=[
                pltpu.VMEM((width, hidden), bf16),
                pltpu.VMEM((width, hidden), bf16),
                pltpu.VMEM((hidden, width), bf16),
                pltpu.SemaphoreType.DMA((3,)),
            ],
            after=after,
        )

    feed_near = feed(seconds[:2], grads_near, 0)
    seconds.append(second_third([feed_near[4]]))
    feed_two = feed(seconds[2:3], grads_far, 0, [feed_near[4]])
    feed_three = feed(seconds[3:4], grads_far, 1, [feed_two[4]])
    inner, swish_back, up_back = (
        [(feed_near[k], 0), (feed_near[k], 1), (feed_two[k], 0), (feed_three[k], 0)] for k in range(3)
    )
    second_parts, second_sent = tensor_reduce(halves(feed_near[3]), (feed_two[3], feed_three[3]))
    down_near, down_far = halves(feed_near[4]), (feed_two[4], feed_three[4])

    bits = bits_of(devices)
    late_bits = [bits[1], bits[0], *bits[2:]]
    second_blocks = [(values, 0) for values in seconds]
    swish_grad = Scatter(second_blocks, [swish_back], bits)
    up_grad = Scatter(second_blocks, [up_back], bits)
    down_grad = Scatter(blocks(grads_near, grads_far), [inner], late_bits, True)
    swish_away = swish_grad.send()
    down_away = down_grad.send([second_sent, swish_away])
    up_away = up_grad.send([down_away])

    middle_grad, own_rows, mlp_norm_part = grid_call(
        middle_back_kernel,
        tiles,
        [own_spec] + [tile_spec] * 4 + [fixed((1, width))],
        [tile_spec, tile_spec, fixed((1, width))],
        [struct((length, width), f32), struct((length, width), bf16), struct((1, width), f32)],
        [place_index, cotangent, *second_parts, middle, gain_two],
        prefetch=1,
        after=[up_away],
    )

    def branch_back(first, second, mixed, gates, queries, run, at, into=None):
        return grid_call(
            branch_back_kernel,
            (half,),
            [
                whole_block, whole_block, fixed((DK, width)), row_spec(DK), row_spec(DK), fixed((1, DK)),
                row_spec(DK), row_spec(DK),
            ],
            [row_spec(DK), row_spec(DK), line(1, DK), chunk_spec(devices, 0, at)],
            [rows_of(DK, bf16), rows_of(DK, bf16), struct((half, 1, DK), f32), chunks],
            [first, second, out_weight, mixed, gates, gain, queries, run],
            into=None if into is None else (into, 3),
        )

    def gather_back(own_rows):
        *rows, rows_third = tensor_gather(own_rows)
        *near, state_back = branch_back(
            rows[0], rows[1], mixed_near, gates_near, queries_near, run_near, half
        )
        rows.append(rows_third([near[0]]))
        *far, state_back = branch_back(
            rows[2], rows[3], mixed_far, gates_far, queries_far, run_far, 0, state_back
        )
        return rows[1:], near, far, state_back

    others, near, far, state_back = region(gather_back, own_rows)
    rows = [own_rows, *others]
    gate_back_near, mixed_back_near, gain_back_near = near
    gate_back_far, mixed_back_far, gain_back_far = far
    norms = blocks(norm_near, norm_far)
    out_grad = Scatter([(values, 0) for values in rows], [blocks(branch_near, branch_far)], bits, True)
    out_away = out_grad.send([state_back])

    def states_back(state_back):
        came = deal(state_back)
        down_parts, _ = tensor_reduce(down_near, down_far)
        return came, down_parts[1:]

    came, down_parts = region(states_back, state_back)
    swish_one = swish_grad.step_one([came])
    down_one = down_grad.step_one([swish_one])

    def states_out(came, down_parts):
        outgoing = deal(carried(came, lines, True, [swish_one, down_one]))
        own = sum((part.astype(f32) for part in (down_near[0], *down_parts)), middle).astype(bf16)
        *blocks, third = tensor_gather(own)
        return outgoing, [*blocks, third([])]

    outgoing, output_blocks = region(states_out, came, down_parts)

    def mix_back(queries, keys, values, mixed_back, run, scores, at, rank_rows, after):
        return grid_call(
            mix_back_kernel,
            (half,),
            [row_spec(DK)] * 5
            + [square(length)]
            + [chunk_spec(devices, 0, at)] * 2
            + [row_spec(rank), fixed((rank, DK)), fixed((1, DK))],
            [row_spec(DK)] * 3 + [line(rank, length), line(rank, DK), line(1, DK)],
            [rows_of(DK, bf16)] * 3
            + [
                struct((half, rank, length), f32),
                struct((half, rank, DK), f32),
                struct((half, 1, DK), f32),
            ],
            [
                queries, keys, values, mixed_back, run, scores, incoming, outgoing,
                rank_rows, rank_up, bias,
            ],
            after=after,
        )

    query_back_near, key_back_near, value_back_near, rank_part_near, up_part_near, bias_part_near = (
        mix_back(
            queries_near, keys_near, values_near, mixed_back_near, run_near, scores_near,
            half, rank_near, [],
        )
    )
    query_back_far, key_back_far, value_back_far, rank_part_far, up_part_far, bias_part_far = mix_back(
        queries_far, keys_far, values_far, mixed_back_far, run_far, scores_far,
        0, rank_far, [bias_part_near],
    )
    up_one = up_grad.step_one([bias_part_far])

    query_gate_grad = Scatter(
        norms, [blocks(query_back_near, query_back_far), blocks(gate_back_near, gate_back_far)], bits
    )
    key_value_grad = Scatter(
        norms, [blocks(key_back_near, key_back_far), blocks(value_back_near, value_back_far)], late_bits
    )
    query_gate_away = query_gate_grad.send([up_one])
    key_value_away = key_value_grad.send([query_gate_away])

    def first_part(query_back, key_back, value_back, gate_back, after):
        return product_sum(
            [
                (query_back, query_weight),
                (key_back, key_weight),
                (value_back, value_weight),
                (gate_back, gate_weight),
            ],
            bf16,
            after,
        )

    first_far = first_part(query_back_far, key_back_far, value_back_far, gate_back_far, [key_value_away])
    first_near = first_part(query_back_near, key_back_near, value_back_near, gate_back_near, [first_far])
    first_parts, first_sent = tensor_reduce(halves(first_near), halves(first_far))

    rank_part = jnp.concatenate([rank_part_near, rank_part_far], axis=0)
    rank_part = rank_part + swap(rank_part, "tensor", 1)[jnp.array([1, 0, 3, 2])]
    rank_part = rank_part + swap(rank_part, "tensor", 2)[jnp.array([2, 3, 0, 1])]
    rank_back = rank_part.astype(bf16)

    swish_two = swish_grad.step_two([first_near, first_sent])
    down_two = down_grad.step_two([swish_two])
    out_one = out_grad.step_one([down_two])
    up_two = up_grad.step_two([out_one])

    input_rows, attn_norm_part = grid_call(
        input_back_kernel,
        tiles,
        [own_spec] + [tile_spec] * 3
        + [
            pl.BlockSpec((rank, tile), lambda b, *_: (0, b)), fixed((width, rank)), tile_spec,
            fixed((1, width)),
        ],
        [tile_spec, fixed((1, width))],
        [struct((length, width), bf16), struct((1, width), f32)],
        [
            place_index, layer_input, *first_parts, rank_back[0], rank_down, middle_grad,
            attn_norm.reshape(1, width),
        ],
        prefetch=1,
        after=[up_two],
    )
    *input_blocks, input_third = tensor_gather(input_rows)
    input_blocks.append(input_third([]))
    query_gate_one = query_gate_grad.step_one([input_rows])
    key_value_one = key_value_grad.step_one([query_gate_one])
    out_two = out_grad.step_two([key_value_one])
    swish_share = swish_grad.last([out_two])
    down_share = down_grad.last([swish_share])
    up_share = up_grad.last([down_share])
    query_gate_two = query_gate_grad.step_two([up_share])
    key_value_two = key_value_grad.step_two([query_gate_two])
    layer_output = in_order(output_blocks, order, [key_value_two])
    out_share = out_grad.last([layer_output])
    input_grad = in_order(input_blocks, order, [out_share])
    query_gate_share = query_gate_grad.last([out_share])
    key_value_share = key_value_grad.last([query_gate_share])

    rank_down_part = sum(
        contract(rank_back[k], array[at * length : (at + 1) * length], 1, 0)
        for k, (array, at) in enumerate(norms)
    )
    own_part = jnp.concatenate([rank_down_part, mlp_norm_part, attn_norm_part], axis=0)
    shared = jnp.concatenate(
        [
            sum(up_part_near) + sum(up_part_far),
            sum(bias_part_near) + sum(bias_part_far),
            sum(gain_back_near) + sum(gain_back_far),
        ],
        axis=0,
    )
    column = width // devices
    own_part = jnp.moveaxis(own_part.reshape(rank + 2, devices, column), 1, 0)
    own_size = (rank + 2) * column
    mail = jnp.concatenate(
        [
            own_part.reshape(devices, own_size),
            jnp.broadcast_to(shared.reshape(1, -1), (devices, shared.size)),
        ],
        axis=1,
    )
    mail = spread_sum(mail.reshape(devices, 1, -1)).reshape(-1)
    own_part = mail[:own_size].reshape(rank + 2, column)
    shared = mail[own_size:].reshape(rank + 2, DK)
    norm_parts = sum_over(own_part[rank:], "tensor")
    return (
        layer_output,
        input_grad,
        norm_parts[1],
        query_gate_share[:, :DK],
        key_value_share[:, :DK],
        key_value_share[:, DK:],
        query_gate_share[:, DK:],
        own_part[:rank].T,
        shared[:rank],
        shared[rank],
        shared[rank + 1],
        out_share,
        norm_parts[0],
        swish_share,
        up_share,
        down_share,
    )


def solution(mesh):
    return jax.shard_map(
        local,
        mesh=mesh,
        in_specs=(
            P(None, "seq", None),
            P(),
            P(None, "tensor"),
            P(None, "tensor"),
            P(None, "tensor"),
            P(None, "tensor"),
            P(),
            P(None, "tensor"),
            P("tensor"),
            P("tensor"),
            P("tensor", None),
            P(),
            P(None, "tensor"),
            P(None, "tensor"),
            P("tensor", None),
            P(None, "seq", None),
        ),
        out_specs=(
            P(None, "seq", None),
            P(None, "seq", None),
            P("seq"),
            P("seq", "tensor"),
            P("seq", "tensor"),
            P("seq", "tensor"),
            P("seq", "tensor"),
            P("seq", None),
            P(None, "tensor"),
            P("tensor"),
            P("tensor"),
            P("tensor", "seq"),
            P("seq"),
            P("seq", "tensor"),
            P("seq", "tensor"),
            P("tensor", "seq"),
        ),
        check_vma=False,
    )
```

```python
import functools

import jax
import jax.numpy as jnp
from jax import lax
from jax.experimental import pallas as pl
from jax.experimental.pallas import tpu as pltpu
from jax.sharding import PartitionSpec as P

DK = 512
BLOCK = 64
EXTRA = 16
ROWS = 256
COST = 1024
VMEM = 48 * 1024 * 1024

bf16 = jnp.bfloat16
f32 = jnp.float32
highest_precision = lax.Precision.HIGHEST
epsilon = 1e-06


def contract(left, right, left_dim, right_dim, precision=None):
    return lax.dot_general(
        left,
        right,
        (((left_dim,), (right_dim,)), ((), ())),
        preferred_element_type=f32,
        precision=precision,
    )


def product(left, right):
    return contract(left, right, 1, 0)


def across(left, right):
    return contract(left, right, 0, 0)


def against(left, right):
    return contract(left, right, 1, 1)


def forget_logits(rank_ref, up_ref, bias_ref):
    return product(rank_ref[...], up_ref[...]) + bias_ref[...].astype(f32)


def positions(count):
    rows = lax.broadcasted_iota(jnp.int32, (count, count), 0)
    cols = lax.broadcasted_iota(jnp.int32, (count, count), 1)
    return rows, cols


def spread(pieces, size):
    width = pieces[0].shape[1]
    return jnp.concatenate([jnp.broadcast_to(piece, (size, width)) for piece in pieces], axis=0)


def scaled_pair(level, query_scaled, key_rows, run):
    count = run.shape[0]
    if level == 0:
        starts = range(0, count, BLOCK)
        center = spread([run[s + BLOCK // 2 : s + BLOCK // 2 + 1] for s in starts], BLOCK)
        query_factor = jnp.exp(run - center)
        key_factor = jnp.exp(center - run)
        return query_scaled * query_factor, key_rows * key_factor, query_factor, key_factor
    group = BLOCK << level
    half = group // 2
    center = spread([run[s + half - 1 : s + half] for s in range(0, count, group)], group)
    place = lax.broadcasted_iota(jnp.int32, run.shape, 0)
    right = (place % group) >= half
    gap = run - center
    query_factor = jnp.where(right, jnp.exp(jnp.where(right, gap, 0.0)), 0.0)
    key_factor = jnp.where(right, 0.0, jnp.exp(jnp.where(right, 0.0, -gap)))
    return query_scaled * query_factor, key_rows * key_factor, query_factor, key_factor


def level_mask(level, rows, cols):
    if level == 0:
        return (rows // BLOCK == cols // BLOCK) & (cols <= rows)
    group = BLOCK << level
    half = group // 2
    return (rows // group == cols // group) & (rows % group >= half) & (cols % group < half)


def level_count(count):
    levels = 1
    while (BLOCK << (levels - 1)) < count:
        levels += 1
    return levels


def norm_kernel(order_ref, input_ref, grad_ref, gain_ref, norm_ref, rows_ref):
    values = input_ref[0].astype(f32)
    scale = lax.rsqrt(jnp.mean(values * values, axis=-1, keepdims=True) + epsilon)
    norm_ref[...] = (values * scale * gain_ref[...].astype(f32)).astype(bf16)
    rows_ref[...] = grad_ref[0]


def decay_kernel(rank_ref, up_ref, bias_ref, run_ref):
    logits = forget_logits(rank_ref, up_ref, bias_ref)
    decays = (jnp.minimum(logits, 0.0) - jnp.log1p(jnp.exp(-jnp.abs(logits)))) * (1.0 / 16.0)
    rows, cols = positions(decays.shape[0])
    run_ref[...] = contract((cols <= rows).astype(f32), decays, 1, 0, highest_precision)


def total_lines(run):
    return as_lines(run[run.shape[0] - 1 :])


def as_lines(total):
    high = total.astype(bf16)
    rest = total - high.astype(f32)
    middle = rest.astype(bf16)
    low = (rest - middle.astype(f32)).astype(bf16)
    place = lax.broadcasted_iota(jnp.int32, (EXTRA, DK), 0)
    lines = jnp.zeros((EXTRA, DK), f32)
    for at, line in enumerate((high, middle, low)):
        lines = jnp.where(place == at, line.astype(f32), lines)
    return lines.astype(bf16)


def from_lines(lines):
    lines = lines.astype(f32)
    return lines[0:1] + lines[1:2] + lines[2:3]


def state_of(key_ref, value_ref, run):
    left = (key_ref[...].astype(f32) * jnp.exp(run[run.shape[0] - 1 :] - run)).astype(bf16)
    return across(value_ref[...], left).astype(bf16)


def state_kernel(key_ref, value_ref, run_ref, state_ref, lines_ref):
    run = run_ref[...]
    state_ref[0] = state_of(key_ref, value_ref, run)
    lines_ref[0] = total_lines(run)


def cut_state_kernel(me_ref, key_ref, value_ref, run_ref, keep_ref, send_ref, lines_ref, held):
    run = run_ref[...]
    held[...] = state_of(key_ref, value_ref, run).reshape(held.shape)
    lines = total_lines(run)
    y, z = me_ref[0] % 2, me_ref[0] // 2
    for at in range(4):
        keep_ref[0, at] = held[y * 4 + (z ^ at)]
        send_ref[0, at] = held[(1 - y) * 4 + (z ^ at)]
    lines_ref[0] = lines
    send_ref[0, 4, :EXTRA] = lines


def pair_kernel(me_ref, keep_ref, lines_ref, came_ref, first_ref, *part_refs):
    lead = me_ref[0] % 2 == 0
    own, other = from_lines(lines_ref[0]), from_lines(came_ref[0, 4, :EXTRA])
    later = jnp.exp(jnp.where(lead, other, own))
    lines = as_lines(own + other)
    for at, part_ref in enumerate(part_refs):
        mine, came = keep_ref[0, at].astype(f32), came_ref[0, at].astype(f32)
        first = jnp.where(lead, mine, came)
        first_ref[0, at] = first.astype(bf16)
        rows = first.shape[0]
        part_ref[0, :rows] = (first * later + jnp.where(lead, came, mine)).astype(bf16)
        part_ref[0, rows:] = lines


def chain_kernel(me_ref, *refs):
    part_refs, out_refs = refs[:4], refs[4:8]
    held, lines, entered = refs[8:]
    z = me_ref[0] // 2
    rows = held.shape[1]
    for at in range(4):
        held[z ^ at] = part_refs[at][0, :rows]
        lines[z ^ at] = part_refs[at][0, rows:]
    carry = jnp.zeros(held.shape[1:], f32)
    for at in range(4):
        entered[at] = carry.astype(bf16)
        carry = carry * jnp.exp(from_lines(lines[at])) + held[at].astype(f32)
    for at in range(4):
        out_refs[at][0] = entered[z ^ at]


def enter_kernel(me_ref, lines_ref, came_ref, first_ref, *refs):
    *part_refs, whole_ref, send_ref = refs
    y, z = me_ref[0] % 2, me_ref[0] // 2
    lead = y == 0
    earlier = jnp.exp(jnp.where(lead, from_lines(lines_ref[0]), from_lines(came_ref[0, 0, :EXTRA])))
    for at in range(4):
        pair = part_refs[at][0].astype(f32)
        inner = pair * earlier + first_ref[0, at].astype(f32)
        whole_ref[0, 0, z ^ at] = jnp.where(lead, pair, inner).astype(bf16)
        send_ref[0, z ^ at] = jnp.where(lead, inner, pair).astype(bf16)


def join_kernel(me_ref, came_ref, whole_ref):
    whole_ref[0, 0] = came_ref[0]


def score_kernel(query_ref, key_ref, run_ref, score_ref):
    run = run_ref[...]
    query_scaled = query_ref[...].astype(f32) * DK ** (-0.5)
    key_rows = key_ref[...].astype(f32)
    rows, cols = positions(run.shape[0])
    scores = jnp.zeros(rows.shape, f32)
    for level in range(level_count(run.shape[0])):
        left, right, _, _ = scaled_pair(level, query_scaled, key_rows, run)
        scores = jnp.where(
            level_mask(level, rows, cols), against(left.astype(bf16), right.astype(bf16)), scores
        )
    score_ref[0] = scores.astype(bf16)


def whole_state(ref):
    return ref[...].reshape(DK, DK)


def faded_queries(query_ref, run_ref):
    return (query_ref[...].astype(f32) * DK ** (-0.5) * jnp.exp(run_ref[...])).astype(bf16)


def mix_kernel(query_ref, value_ref, run_ref, score_ref, state_ref, gate_ref, gain_ref, mixed_ref, branch_ref):
    faded = faded_queries(query_ref, run_ref)
    mixed = product(score_ref[0], value_ref[...]) + against(faded, whole_state(state_ref))
    mixed_ref[...] = mixed
    scale = lax.rsqrt(jnp.mean(mixed * mixed, axis=-1, keepdims=True) + epsilon)
    gate = gate_ref[...]
    branch_ref[...] = (
        mixed * scale * gain_ref[...].astype(f32) * (gate * jax.nn.sigmoid(gate))
    ).astype(bf16)


def branch_back_kernel(
    first_ref, second_ref, weight_ref, mixed_ref, gate_ref, gain_ref, query_ref, run_ref,
    gate_back_ref, mixed_back_ref, gain_back_ref, state_back_ref,
):
    branch_grad = against(either(first_ref, second_ref), weight_ref[...])
    mixed = mixed_ref[...]
    scale = lax.rsqrt(jnp.mean(mixed * mixed, axis=-1, keepdims=True) + epsilon)
    unit = mixed * scale
    gate = gate_ref[...]
    gain = gain_ref[...].astype(f32)
    sig = jax.nn.sigmoid(gate)
    gate_back_ref[...] = (branch_grad * unit * gain * sig * (1.0 + gate * (1.0 - sig))).astype(bf16)
    shaped_grad = branch_grad * (gate * sig)
    gain_back_ref[0] = jnp.sum(shaped_grad * unit, axis=0, keepdims=True)
    unit_grad = shaped_grad * gain
    mixed_grad = scale * (unit_grad - unit * jnp.mean(unit_grad * unit, axis=-1, keepdims=True))
    mixed_back = mixed_grad.astype(bf16)
    mixed_back_ref[...] = mixed_back
    faded = faded_queries(query_ref, run_ref)
    state_back_ref[...] = across(mixed_back, faded).astype(bf16).reshape(state_back_ref.shape)


def ordered_sum(mask, values):
    high = values.astype(bf16)
    low = (values - high.astype(f32)).astype(bf16)
    ones = mask.astype(f32).astype(bf16)
    return product(ones, high) + product(ones, low)


def mix_back_kernel(
    query_ref, key_ref, value_ref, grad_ref, run_ref, score_ref, state_ref, state_back_ref,
    rank_ref, up_ref, bias_ref,
    query_back_ref, key_back_ref, value_back_ref, rank_back_ref, up_back_ref, bias_back_ref,
):
    run = run_ref[...]
    count = run.shape[0]
    query_scaled = query_ref[...].astype(f32) * DK ** (-0.5)
    key_rows = key_ref[...].astype(f32)
    values = value_ref[...]
    grads = grad_ref[...]
    state = whole_state(state_ref)
    state_back = whole_state(state_back_ref)
    rows, cols = positions(count)
    pairs = against(grads, values)

    closing = run[count - 1 : count]
    fade_in = jnp.exp(run)
    fade_out = jnp.exp(closing - run)
    kept = (key_rows * fade_out).astype(bf16)
    value_back_ref[...] = (across(score_ref[0], grads) + against(kept, state_back)).astype(bf16)

    from_state = product(grads, state)
    to_state = product(values, state_back)
    query_back = fade_in * from_state
    key_back = fade_out * to_state
    decay_back = jnp.exp(closing) * jnp.sum(
        state.astype(f32) * state_back.astype(f32), axis=0, keepdims=True
    )
    decay_back = decay_back + ordered_sum(cols >= rows, query_scaled * fade_in * from_state)
    decay_back = decay_back + ordered_sum(cols < rows, key_rows * fade_out * to_state)
    for level in range(level_count(count)):
        left, right, query_factor, key_factor = scaled_pair(level, query_scaled, key_rows, run)
        left, right = left.astype(bf16), right.astype(bf16)
        here = jnp.where(level_mask(level, rows, cols), pairs, 0.0).astype(bf16)
        to_query = product(here, right)
        to_key = across(here, left)
        query_back = query_back + query_factor * to_query
        key_back = key_back + key_factor * to_key
        left_part = left.astype(f32) * to_query
        right_part = right.astype(f32) * to_key
        if level == 0:
            mask = (rows // BLOCK == cols // BLOCK) & (cols >= rows)
            decay_back = decay_back + ordered_sum(mask, left_part - right_part)
        else:
            group = BLOCK << level
            half = group // 2
            same = rows // group == cols // group
            late = same & (rows % group >= half) & (cols >= rows)
            early = same & (rows % group < half) & (cols < rows)
            decay_back = decay_back + ordered_sum(late | early, left_part + right_part)
    query_back_ref[...] = (query_back * DK ** (-0.5)).astype(bf16)
    key_back_ref[...] = key_back.astype(bf16)
    logits = forget_logits(rank_ref, up_ref, bias_ref)
    logit_back = (decay_back * jax.nn.sigmoid(-logits) * (1.0 / 16.0)).astype(bf16)
    rank_back_ref[0] = against(up_ref[...], logit_back)
    up_back_ref[0] = across(rank_ref[...], logit_back)
    bias_back_ref[0] = jnp.sum(logit_back.astype(f32), axis=0, keepdims=True)


def prefix_kernel(reverse, lines_ref, parts_ref, out_ref):
    count = parts_ref.shape[0]
    rows = out_ref.shape[2]
    carry = jnp.zeros(out_ref.shape[2:], f32)
    for step in range(count):
        at = count - 1 - step if reverse else step
        out_ref[at, 0] = carry.astype(bf16)
        total = from_lines(lines_ref[at, 0])
        carry = carry * jnp.exp(total) + parts_ref[at, 0].astype(f32)


def hold_kernel(values_ref, out_ref):
    out_ref[...] = values_ref[...]


def either(first_ref, second_ref):
    return jnp.where(pl.program_id(0) == 0, first_ref[...], second_ref[...])


def middle_kernel(place_ref, input_ref, own_ref, first_ref, last_ref, gain_ref, middle_ref, second_ref):
    middle = input_ref[0].astype(f32) + (
        own_ref[...].astype(f32) + first_ref[...].astype(f32) + last_ref[...].astype(f32)
    )
    middle_ref[...] = middle
    scale = lax.rsqrt(jnp.mean(middle * middle, axis=-1, keepdims=True) + epsilon)
    second_ref[...] = (middle * scale * gain_ref[...].astype(f32)).astype(bf16)


def norm_back(values, grad, gain):
    scale = lax.rsqrt(jnp.mean(values * values, axis=-1, keepdims=True) + epsilon)
    unit = values * scale
    scaled = grad * gain
    back = scale * (scaled - unit * jnp.mean(scaled * unit, axis=-1, keepdims=True))
    return back, jnp.sum(grad * unit, axis=0, keepdims=True)


def add_part(out_ref, part):
    @pl.when(pl.program_id(0) == 0)
    def _():
        out_ref[...] = part

    @pl.when(pl.program_id(0) != 0)
    def _():
        out_ref[...] += part


def middle_back_kernel(
    place_ref, grad_ref, own_ref, first_ref, last_ref, middle_ref, gain_ref, back_ref, rows_ref, part_ref
):
    grad = own_ref[...].astype(f32) + first_ref[...].astype(f32) + last_ref[...].astype(f32)
    back, part = norm_back(middle_ref[...], grad, gain_ref[...].astype(f32))
    back = grad_ref[0].astype(f32) + back
    back_ref[...] = back
    rows_ref[...] = back.astype(bf16)
    add_part(part_ref, part)


def input_back_kernel(
    place_ref, input_ref, sum_ref, rank_ref, down_ref, middle_ref, gain_ref, rows_ref, part_ref
):
    grad = sum_ref[0].astype(f32) + contract(rank_ref[...], down_ref[...], 0, 1)
    back, part = norm_back(input_ref[0].astype(f32), grad, gain_ref[...].astype(f32))
    rows_ref[...] = (middle_ref[...] + back).astype(bf16)
    add_part(part_ref, part)


def feed_kernel(
    first_ref, second_ref, grads_ref, swish_ref, up_ref, down_ref,
    inner_ref, swish_back_ref, up_back_ref, second_back_ref, out_ref,
    swish_held, up_held, down_held, semaphores,
):
    copies = [
        pltpu.make_async_copy(swish_ref, swish_held, semaphores.at[0]),
        pltpu.make_async_copy(up_ref, up_held, semaphores.at[1]),
        pltpu.make_async_copy(down_ref, down_held, semaphores.at[2]),
    ]
    start = pl.program_id(0) == 0

    @pl.when(start)
    def _():
        for copy in copies:
            copy.start()

    rows = either(first_ref, second_ref)

    @pl.when(start)
    def _():
        copies[0].wait()

    swish = product(rows, swish_held[...])

    @pl.when(start)
    def _():
        copies[1].wait()

    up = product(rows, up_held[...])
    sig = jax.nn.sigmoid(swish)
    act = swish * sig
    inner = (act * up).astype(bf16)
    inner_ref[...] = inner

    @pl.when(start)
    def _():
        copies[2].wait()

    inner_grad = against(grads_ref[...], down_held[...])
    swish_back = (inner_grad * up * sig * (1.0 + swish * (1.0 - sig))).astype(bf16)
    up_back = (inner_grad * act).astype(bf16)
    swish_back_ref[...] = swish_back
    up_back_ref[...] = up_back
    second_back_ref[...] = (against(swish_back, swish_held[...]) + against(up_back, up_held[...])).astype(bf16)
    out_ref[...] = product(inner, down_held[...]).astype(bf16)


def place_kernel(order_ref, *refs):
    out_ref = refs[-1]
    step = pl.program_id(0)
    for k in range(4):

        @pl.when(step == k)
        def _():
            out_ref[0] = refs[k][...]


def output_kernel(order_ref, middle_ref, *refs):
    out_ref = refs[-1]
    step = pl.program_id(0)

    @pl.when(step == 0)
    def _():
        out_ref[0] = (refs[0][...].astype(f32) + middle_ref[...]).astype(bf16)

    for k in range(1, 4):

        @pl.when(step == k)
        def _():
            out_ref[0] = refs[k][...]


def sum_kernel(order_ref, *refs):
    *refs, out_ref, held = refs
    count = (len(refs)) // 2
    rows = out_ref.shape[1]

    @pl.when(pl.program_id(1) == 0)
    def _():
        total = against(refs[0][...], refs[count][...])
        for k in range(1, count):
            total = total + against(refs[k][...], refs[count + k][...])
        held[...] = total.astype(bf16)
        out_ref[0] = held[:rows]

    @pl.when(pl.program_id(1) == 1)
    def _():
        out_ref[0] = held[rows:]


def grad_kernel(parts, groups, cut_groups, turned, pick_ref, *refs):
    cuts, refs = refs[: parts * cut_groups], refs[parts * cut_groups :]
    others, refs = refs[: parts * groups], refs[parts * groups :]
    arrived, out_ref = refs[:-1], refs[-1]
    for group in range(groups):
        total = None
        members = others[group * parts : (group + 1) * parts]
        width = members[0].shape[1]
        columns = slice(group * width, (group + 1) * width)
        first = group * parts if cut_groups > 1 else 0
        for cut, other in zip(cuts[first : first + parts], members):
            part = across(cut[...], other[...])
            total = part if total is None else total + part
        for ref in arrived:
            total = total + ref[0, :, columns].astype(f32)
        if turned:
            out_ref[...] = total.T
        else:
            out_ref[0, :, columns] = total.astype(out_ref.dtype)


def struct(shape, dtype):
    return jax.ShapeDtypeStruct(shape, dtype)


def grid_call(kernel, grid, in_specs, out_specs, out_shape, args, prefetch=0, after=(), scratch=(), into=()):
    first, last = len(args), len(args) + len(after)
    aliases = {}
    for array, at in into:
        aliases[last] = at
        after = (*after, array)
        last += 1

    def run(*refs):
        kernel(*refs[:first], *refs[last:])

    return pl.pallas_call(
        run,
        grid_spec=pltpu.PrefetchScalarGridSpec(
            num_scalar_prefetch=prefetch,
            grid=grid,
            in_specs=list(in_specs) + [pl.BlockSpec(memory_space=pl.ANY)] * len(after),
            out_specs=out_specs,
            scratch_shapes=list(scratch),
        ),
        out_shape=out_shape,
        input_output_aliases=aliases,
        compiler_params=pltpu.CompilerParams(vmem_limit_bytes=VMEM),
        cost_estimate=pl.CostEstimate(flops=COST, bytes_accessed=COST, transcendentals=0),
    )(*args, *after)


def swap(values, axis, distance):
    count = lax.axis_size(axis)
    return lax.ppermute(values, axis, [(i, i ^ distance) for i in range(count)])


def region(function, *args):
    shapes = jax.eval_shape(function, *args)

    def never(*_):
        return jax.tree.map(lambda a: jnp.zeros(a.shape, a.dtype), shapes)

    return lax.cond(lax.axis_index("seq") >= 0, function, never, *args)


def bits_of(count):
    return [1 << k for k in range(count.bit_length() - 1)]


def hold(values, after):
    spec = pl.BlockSpec(values.shape, lambda: (0,) * values.ndim)
    return grid_call(hold_kernel, (), [spec], spec, struct(values.shape, values.dtype), [values], after=after)


def chunk_spec(count, first=0):
    return pl.BlockSpec((count, 1, DK // count, DK), lambda b, *_: (0, b + first, 0, 0))


def carried(pieces, lines, reverse, after=()):
    count, seq_count, share, _ = pieces.shape
    return grid_call(
        functools.partial(prefix_kernel, reverse),
        (seq_count,),
        [pl.BlockSpec((count, 1, EXTRA, DK), lambda b: (0, b, 0, 0)), chunk_spec(count)],
        chunk_spec(count),
        struct((count, seq_count, share, DK), bf16),
        [lines, pieces],
        after=after,
    )


def deal(pieces):
    return lax.all_to_all(pieces, "seq", 0, 0)


def tensor_reduce(near, far):
    third = swap(far[1], "tensor", 1)
    second = (far[0].astype(f32) + third.astype(f32)).astype(bf16)
    first = swap(near[1], "tensor", 1)
    return (near[0], first, swap(second, "tensor", 2)), second


def tensor_gather(own):
    first = swap(own, "tensor", 1)
    second = swap(own, "tensor", 2)

    def third(after):
        return swap(hold(second, after) if after else second, "tensor", 1)

    return own, first, second, third


def grad_part(cuts, groups, picks, arrived, dtype, turned=False, after=()):
    rows = ROWS
    width = groups[0][0][0].shape[1]
    whole = width * len(groups)
    parts = len(groups[0])
    cut_groups = len(cuts)
    cuts = [block for group in cuts for block in group]
    share = cuts[0][0].shape[1] // lax.axis_size("seq")
    chunks = len(picks)
    me = lax.axis_index("seq")
    index = jnp.stack([me ^ r for r in picks]).astype(jnp.int32)
    others = [block for group in groups for block in group]
    in_specs = [pl.BlockSpec((rows, share), lambda k, pick, at=at: (at, pick[k])) for _, at in cuts]
    in_specs += [pl.BlockSpec((rows, width), lambda k, pick, at=at: (at, 0)) for _, at in others]
    for _, first in arrived:
        in_specs.append(pl.BlockSpec((1, share, whole), lambda k, pick, first=first: (k + first, 0, 0)))
    if turned:
        out_spec = pl.BlockSpec((whole, share), lambda k, pick: (0, 0))
        shape = (whole, share)
    else:
        out_spec = pl.BlockSpec((1, share, whole), lambda k, pick: (k, 0, 0))
        shape = (chunks, share, whole)
    return grid_call(
        functools.partial(grad_kernel, parts, len(groups), cut_groups, turned),
        (chunks,),
        in_specs,
        out_spec,
        struct(shape, dtype),
        [index, *[a for a, _ in cuts], *[a for a, _ in others], *[a for a, _ in arrived]],
        prefetch=1,
        after=after,
    )


class Scatter:
    def __init__(self, cuts, groups, order, turned=False):
        cuts = cuts if isinstance(cuts[0], list) else [cuts]
        self.cuts, self.groups, self.order, self.turned = cuts, groups, order, turned
        self.split = lax.axis_size("seq") == 8
        self.came = [None] * 3

    def part(self, picks, arrived, dtype, turned=False, after=()):
        return grad_part(self.cuts, self.groups, picks, arrived, dtype, turned, after)

    def hop(self, at, part):
        if self.split:
            return swap(part, "seq", self.order[at])
        return part if at else lax.psum_scatter(part, "seq", scatter_dimension=0, tiled=True)

    def away(self, after=()):
        if not self.split:
            return jnp.concatenate(
                [
                    sum(
                        across(a[i * ROWS : (i + 1) * ROWS], b[j * ROWS : (j + 1) * ROWS])
                        for (a, i), (b, j) in zip(cuts, group)
                    ).astype(bf16)
                    for cuts, group in zip(
                        self.cuts if len(self.cuts) > 1 else self.cuts * len(self.groups), self.groups
                    )
                ],
                axis=1,
            )
        a, b, c = self.order
        return self.part([a ^ b, a ^ b ^ c, a ^ c, a], [], bf16, after=after)

    def one(self, after=()):
        if not self.split:
            return self.came[0]
        a, b, c = self.order
        return self.part([b, b ^ c], [(self.came[0], 0)], bf16, after=after)

    def two(self, after=()):
        if not self.split:
            return self.came[0]
        c = self.order[2]
        return self.part([c], [(self.came[0], 2), (self.came[1], 1)], bf16, after=after)

    def last(self, after=()):
        if not self.split:
            total = self.came[0].astype(f32)
            return total.T if self.turned else total
        arrived = [(self.came[0], 3), (self.came[1], 0), (self.came[2], 0)]
        total = self.part([0], arrived, f32, self.turned, after=after)
        return total if self.turned else total[0]


def sum_over(values, axis):
    for bit in bits_of(lax.axis_size(axis)):
        values = values + swap(values, axis, bit)
    return values


def local(
    layer_input,
    attn_norm,
    query_weight,
    key_weight,
    value_weight,
    gate_weight,
    rank_down,
    rank_up,
    decay_bias,
    head_gain,
    out_weight,
    mlp_norm,
    swish_weight,
    up_weight,
    down_weight,
    cotangent,
):
    seq_count, length, width = layer_input.shape
    place = lax.axis_index("tensor")
    devices = lax.axis_size("seq")
    half = seq_count // 2
    half_rows = half * length
    rank = rank_down.shape[1]
    bias = decay_bias.reshape(1, DK)
    gain = head_gain.reshape(1, DK)
    share = DK // devices

    def row_spec(size):
        return pl.BlockSpec((length, size), lambda b, *_: (b, 0))

    def fixed(shape):
        return pl.BlockSpec(shape, lambda b, *_: (0,) * len(shape))

    def square(size):
        return pl.BlockSpec((1, size, size), lambda b, *_: (b, 0, 0))

    def line(rows, size):
        return pl.BlockSpec((1, rows, size), lambda b, *_: (b, 0, 0))

    def rows_of(size, dtype):
        return struct((half_rows, size), dtype)

    chunks = struct((devices, seq_count, share, DK), bf16)
    whole_block = pl.BlockSpec((length, width), lambda b, *_: (0, 0))

    def blocks(near, far):
        return [(near, 0), (near, 1), (far, 0), (far, 1)]

    def halves(values):
        return values[:length], values[length:]

    def first_rows(order, after=()):
        spec = pl.BlockSpec((1, length, width), lambda b, order: (order[b], 0, 0))
        return grid_call(
            norm_kernel,
            (half,),
            [spec, spec, fixed((1, width))],
            [row_spec(width), row_spec(width)],
            [rows_of(width, bf16), rows_of(width, bf16)],
            [order, layer_input, cotangent, attn_norm.reshape(1, width)],
            prefetch=1,
            after=after,
        )

    def decays(norm):
        rank_rows = product(norm, rank_down).astype(bf16)
        run = grid_call(
            decay_kernel,
            (half,),
            [row_spec(rank), fixed((rank, DK)), fixed((1, DK))],
            row_spec(DK),
            rows_of(DK, f32),
            [rank_rows, rank_up, bias],
        )
        return rank_rows, run

    quarter = DK // 8
    me = lax.axis_index("seq").astype(jnp.int32).reshape(1)

    def quarters(count, size=quarter):
        return pl.BlockSpec((1, count, size, DK), lambda b, *_: (b, 0, 0, 0))

    def states(norm, run, after=()):
        keys = product(norm, key_weight).astype(bf16)
        values = product(norm, value_weight).astype(bf16)
        lines = struct((half, EXTRA, DK), bf16)
        if devices != 8:
            parts = grid_call(
                state_kernel,
                (half,),
                [row_spec(DK)] * 3,
                [square(DK), line(EXTRA, DK)],
                [struct((half, DK, DK), bf16), lines],
                [keys, values, run],
                after=after,
            )
        else:
            parts = grid_call(
                cut_state_kernel,
                (half,),
                [row_spec(DK)] * 3,
                [quarters(4), quarters(5), line(EXTRA, DK)],
                [struct((half, 4, quarter, DK), bf16), struct((half, 5, quarter, DK), bf16), lines],
                [me, keys, values, run],
                prefetch=1,
                after=after,
                scratch=[pltpu.VMEM((8, quarter, DK), bf16)],
            )
        return keys, values, parts

    def pairs(parts, came, after=()):
        keep, _, lines = parts
        return grid_call(
            pair_kernel,
            (half,),
            [quarters(4), line(EXTRA, DK), quarters(5)],
            [quarters(4)] + [line(quarter + EXTRA, DK)] * 4,
            [struct((half, 4, quarter, DK), bf16)] + [struct((half, quarter + EXTRA, DK), bf16)] * 4,
            [me, keep, lines, came],
            prefetch=1,
            after=after,
        )

    def chain(own, came, after=()):
        return grid_call(
            chain_kernel,
            (half,),
            [line(quarter + EXTRA, DK)] * 4,
            [line(quarter, DK)] * 4,
            [struct((half, quarter, DK), bf16)] * 4,
            [me, own, *came],
            prefetch=1,
            after=after,
            scratch=[
                pltpu.VMEM((4, quarter, DK), bf16),
                pltpu.VMEM((4, EXTRA, DK), bf16),
                pltpu.VMEM((4, quarter, DK), bf16),
            ],
        )

    def enter(parts, came, first, own, others, after=()):
        return grid_call(
            enter_kernel,
            (half,),
            [line(EXTRA, DK), pl.BlockSpec((1, 1, quarter, DK), lambda b, *_: (b, 4, 0, 0)), quarters(4)]
            + [line(quarter, DK)] * 4,
            [pl.BlockSpec((1, 1, 4, quarter, DK), lambda b, me: (me[0] % 2, b, 0, 0, 0)), quarters(4)],
            [struct((2, half, 4, quarter, DK), bf16), struct((half, 4, quarter, DK), bf16)],
            [me, parts[2], came, first, own, *others],
            prefetch=1,
            after=after,
        )

    def join(whole, came):
        return grid_call(
            join_kernel,
            (half,),
            [quarters(4)],
            pl.BlockSpec((1, 1, 4, quarter, DK), lambda b, me: (1 - me[0] % 2, b, 0, 0, 0)),
            struct(whole.shape, bf16),
            [me, came],
            prefetch=1,
            into=[(whole, 0)],
        )

    def along(parts):
        return [swap(part, "seq", 2 * at) for at, part in enumerate(parts, 1)]

    def scored(norm, keys, run, after=()):
        queries = product(norm, query_weight).astype(bf16)
        gates = product(norm, gate_weight)
        scores = grid_call(
            score_kernel,
            (half,),
            [row_spec(DK)] * 3,
            square(length),
            struct((half, length, length), bf16),
            [queries, keys, run],
            after=after,
        )
        return queries, gates, scores

    def mix(queries, values, run, scores, incoming, at, gates, after=()):
        return grid_call(
            mix_kernel,
            (half,),
            [row_spec(DK)] * 3
            + [square(length), state_specs[at], row_spec(DK), fixed((1, DK))],
            [row_spec(DK), row_spec(DK)],
            [rows_of(DK, f32), rows_of(DK, bf16)],
            [queries, values, run, scores, incoming, gates, gain],
            after=after,
        )

    order = jnp.arange(seq_count, dtype=jnp.int32) ^ place
    place_index = order[:1]
    norm_far, grads_far = first_rows(order[half:])
    rank_far, run_far = decays(norm_far)
    keys_far, values_far, parts_far = states(norm_far, run_far)
    norm_near, grads_near = first_rows(order[:half], [parts_far[1]])
    rank_near, run_near = decays(norm_near)
    keys_near, values_near, parts_near = states(norm_near, run_near)
    queries_far, gates_far, scores_far = scored(norm_far, keys_far, run_far, [parts_near[1]])
    if devices != 8:
        queries_near, gates_near, scores_near = scored(norm_near, keys_near, run_near, [scores_far])
        state = jnp.concatenate([parts_far[0], parts_near[0]], axis=0)
        state = jnp.moveaxis(state.reshape(seq_count, devices, share, DK), 1, 0)
        every_line = jnp.concatenate([parts_far[1], parts_near[1]], axis=0)
        lines = deal(jnp.broadcast_to(every_line[None], (devices, *every_line.shape)))
        incoming = deal(carried(deal(state), lines, False))
        incoming_far = incoming_near = incoming
        state_specs = [chunk_spec(devices, at) for at in (0, half)]
    else:
        came_far = swap(parts_far[1], "seq", 1)
        came_near = swap(parts_near[1], "seq", 1)
        first_far, *pair_far = pairs(parts_far, came_far, [parts_near[1]])
        others_far = along(pair_far[1:])
        first_near, *pair_near = pairs(parts_near, came_near, [pair_far[0], scores_far])
        others_near = along(pair_near[1:])
        chain_far = chain(pair_far[0], others_far, [pair_near[0]])
        back_far = along(chain_far[1:])
        queries_near, gates_near, scores_near = scored(norm_near, keys_near, run_near, [chain_far[0]])
        chain_near = chain(pair_near[0], others_near, [chain_far[0]])
        back_near = along(chain_near[1:])
        whole_far, send_far = enter(parts_far, came_far, first_far, chain_far[0], back_far, [chain_near[0]])
        half_far = swap(send_far, "seq", 1)
        whole_near, send_near = enter(
            parts_near, came_near, first_near, chain_near[0], back_near, [send_far, scores_near]
        )
        half_near = swap(send_near, "seq", 1)
        incoming_far = join(whole_far, half_far)
        incoming_near = join(whole_near, half_near)
        every_line = jnp.concatenate([parts_far[2], parts_near[2]], axis=0)
        lines = deal(jnp.broadcast_to(every_line[None], (devices, *every_line.shape)))
        state_specs = [
            pl.BlockSpec((2, 1, 4, quarter, DK), lambda b, *_: (0, b, 0, 0, 0)) for at in range(2)
        ]

    mixed_far, branch_far = mix(queries_far, values_far, run_far, scores_far, incoming_far, 0, gates_far)
    out_far = product(branch_far, out_weight).astype(bf16)
    out_third = swap(out_far[length:], "tensor", 1)
    out_second = (out_far[:length].astype(f32) + out_third.astype(f32)).astype(bf16)
    out_last = swap(out_second, "tensor", 2)
    mixed_near, branch_near = mix(
        queries_near, values_near, run_near, scores_near, incoming_near, 1, gates_near, [out_second]
    )
    out_near = product(branch_near, out_weight).astype(bf16)
    out_parts = (out_near[:length], swap(out_near[length:], "tensor", 1), out_last)

    tile = 128
    tiles = (length // tile,)
    tile_spec = pl.BlockSpec((tile, width), lambda b, *_: (b, 0))
    own_spec = pl.BlockSpec((1, tile, width), lambda b, place: (place[0], b, 0))
    gain_two = mlp_norm.reshape(1, width)
    middle, second_own = grid_call(
        middle_kernel,
        tiles,
        [own_spec] + [tile_spec] * 3 + [fixed((1, width))],
        [tile_spec] * 2,
        [struct((length, width), f32), struct((length, width), bf16)],
        [place_index, layer_input, *out_parts, gain_two],
        prefetch=1,
    )
    *seconds, second_third = tensor_gather(second_own)

    hidden = swish_weight.shape[1]
    anywhere = pl.BlockSpec(memory_space=pl.ANY)

    def feed(rows, grads, at, after=()):
        count = len(rows)
        return grid_call(
            feed_kernel,
            (count,),
            [whole_block] * 2
            + [pl.BlockSpec((length, width), lambda b: (b + at, 0))]
            + [anywhere] * 3,
            [row_spec(hidden)] * 3 + [row_spec(width)] * 2,
            [struct((count * length, hidden), bf16)] * 3 + [struct((count * length, width), bf16)] * 2,
            [rows[0], rows[-1], grads, swish_weight, up_weight, down_weight],
            scratch=[
                pltpu.VMEM((width, hidden), bf16),
                pltpu.VMEM((width, hidden), bf16),
                pltpu.VMEM((hidden, width), bf16),
                pltpu.SemaphoreType.DMA((3,)),
            ],
            after=after,
        )

    feed_near = feed(seconds[:2], grads_near, 0)
    seconds.append(second_third([feed_near[4]]))
    feed_two = feed(seconds[2:3], grads_far, 0, [feed_near[4]])
    feed_three = feed(seconds[3:4], grads_far, 1, [feed_two[4]])
    inner, swish_back, up_back = (
        [(feed_near[k], 0), (feed_near[k], 1), (feed_two[k], 0), (feed_three[k], 0)] for k in range(3)
    )

    bits = bits_of(devices)
    late_bits = [bits[1], bits[0], *bits[2:]]
    second_blocks = [(values, 0) for values in seconds]
    swish_grad = Scatter(second_blocks, [swish_back], bits)
    up_grad = Scatter(second_blocks, [up_back], bits)
    down_grad = Scatter(blocks(grads_near, grads_far), [inner], late_bits, True)
    swish_away = swish_grad.away([lines])
    swish_grad.came[0] = swish_grad.hop(0, swish_away)

    def second_sum(near, far):
        parts, _ = tensor_reduce(near, far)
        down_away = down_grad.away([swish_away])
        return parts[1:], down_away, up_grad.away([down_away])

    second_parts, down_away, up_away = region(
        second_sum, halves(feed_near[3]), (feed_two[3], feed_three[3])
    )
    second_parts = (feed_near[3], *second_parts)
    down_grad.came[0] = down_grad.hop(0, down_away)
    up_grad.came[0] = up_grad.hop(0, up_away)

    middle_grad, own_rows, mlp_norm_part = grid_call(
        middle_back_kernel,
        tiles,
        [own_spec] + [tile_spec] * 4 + [fixed((1, width))],
        [tile_spec, tile_spec, fixed((1, width))],
        [struct((length, width), f32), struct((length, width), bf16), struct((1, width), f32)],
        [place_index, cotangent, *second_parts, middle, gain_two],
        prefetch=1,
    )

    def branch_back(first, second, mixed, gates, queries, run, at, into=None):
        return grid_call(
            branch_back_kernel,
            (half,),
            [
                whole_block, whole_block, fixed((DK, width)), row_spec(DK), row_spec(DK), fixed((1, DK)),
                row_spec(DK), row_spec(DK),
            ],
            [row_spec(DK), row_spec(DK), line(1, DK), chunk_spec(devices, at)],
            [rows_of(DK, bf16), rows_of(DK, bf16), struct((half, 1, DK), f32), chunks],
            [first, second, out_weight, mixed, gates, gain, queries, run],
            into=() if into is None else [(into, 3)],
        )

    first_row = swap(own_rows, "tensor", 1)

    def gather_back(own_rows, first_row):
        second_row = swap(own_rows, "tensor", 2)
        *near, state_back = branch_back(
            own_rows, first_row, mixed_near, gates_near, queries_near, run_near, half
        )
        third_row = swap(second_row, "tensor", 1)
        *far, state_back = branch_back(
            second_row, third_row, mixed_far, gates_far, queries_far, run_far, 0, state_back
        )
        return second_row, third_row, near, far, state_back

    second_row, third_row, near, far, state_back = region(gather_back, own_rows, first_row)
    rows = [(values, 0) for values in (own_rows, first_row, second_row, third_row)]
    gate_back_near, mixed_back_near, gain_back_near = near
    gate_back_far, mixed_back_far, gain_back_far = far
    norms = blocks(norm_near, norm_far)

    def ordered_output():
        return grid_call(
            output_kernel,
            (4,),
            [whole_block]
            + [pl.BlockSpec((length, width), lambda k, order, at=at: (at, 0)) for at in (0, 1, 0, 0)],
            pl.BlockSpec((1, length, width), lambda k, order: (order[k], 0, 0)),
            struct((seq_count, length, width), bf16),
            [order, middle, feed_near[4], feed_near[4], feed_two[4], feed_three[4]],
            prefetch=1,
        )

    out_grad = Scatter(rows, [blocks(branch_near, branch_far)], bits, True)
    gate_grad = Scatter(norms, [blocks(gate_back_near, gate_back_far)], bits)

    def states_back(state_back):
        swish_one = swish_grad.one([state_back])
        gate_away = gate_grad.away([swish_one])
        return deal(state_back), swish_one, gate_away, out_grad.away([gate_away]), ordered_output()

    came, swish_one, gate_away, out_away, output = region(states_back, state_back)
    layer_output = lax.psum(output, "tensor")

    def states_out(came, swish_one, out_away):
        up_one = up_grad.one([came])
        return (
            deal(carried(came, lines, True)), swish_grad.hop(1, swish_one), out_grad.hop(0, out_away),
            up_one, down_grad.one([up_one]),
        )

    outgoing, swish_grad.came[1], out_grad.came[0], up_one, down_one = region(
        states_out, came, swish_one, out_away
    )
    swish_two = swish_grad.two([outgoing])

    def mix_back(queries, keys, values, mixed_back, run, scores, incoming, at, rank_rows, after):
        return grid_call(
            mix_back_kernel,
            (half,),
            [row_spec(DK)] * 5
            + [square(length)]
            + [state_specs[1 if at else 0], chunk_spec(devices, at)]
            + [row_spec(rank), fixed((rank, DK)), fixed((1, DK))],
            [row_spec(DK)] * 3 + [line(rank, length), line(rank, DK), line(1, DK)],
            [rows_of(DK, bf16)] * 3
            + [
                struct((half, rank, length), f32),
                struct((half, rank, DK), f32),
                struct((half, 1, DK), f32),
            ],
            [
                queries, keys, values, mixed_back, run, scores, incoming, outgoing,
                rank_rows, rank_up, bias,
            ],
            after=after,
        )

    def first_part(query_back, key_back, value_back, gate_back, first, into=()):
        tile = 512
        pairs = [
            (query_back, query_weight),
            (key_back, key_weight),
            (value_back, value_weight),
            (gate_back, gate_weight),
        ]
        return grid_call(
            sum_kernel,
            (width // tile, half),
            [pl.BlockSpec((half_rows, DK), lambda j, r, order: (0, 0))] * 4
            + [pl.BlockSpec((tile, DK), lambda j, r, order: (j, 0))] * 4,
            pl.BlockSpec((1, length, tile), lambda j, r, order: (order[first + r], 0, j)),
            struct((seq_count, length, width), bf16),
            [order, *[p[0] for p in pairs], *[p[1] for p in pairs]],
            prefetch=1,
            into=into,
            scratch=[pltpu.VMEM((half_rows, tile), bf16)],
        )

    def mixed_pair(near, far):
        query_key = Scatter(norms, [blocks(near[0], far[0]), blocks(near[1], far[1])], bits)
        return query_key, Scatter(norms, [blocks(near[2], far[2])], late_bits)

    def mixes_back(up_one, swish_two, down_one, gate_away):
        near = mix_back(
            queries_near, keys_near, values_near, mixed_back_near, run_near, scores_near,
            incoming_near, half, rank_near, [swish_two],
        )
        far = mix_back(
            queries_far, keys_far, values_far, mixed_back_far, run_far, scores_far,
            incoming_far, 0, rank_far, [near[5]],
        )
        query_key, value = mixed_pair(near, far)
        query_key_away = query_key.away([far[5]])
        value_away = value.away([query_key_away])
        first_sum = first_part(*far[:3], gate_back_far, half)
        first_sum = first_part(*near[:3], gate_back_near, 0, [(first_sum, 0)])
        return (
            up_grad.hop(1, up_one), swish_grad.hop(2, swish_two), down_grad.hop(1, down_one),
            gate_grad.hop(0, gate_away), near, far, query_key_away, value_away, first_sum, out_grad.one([first_sum]),
        )

    (
        up_grad.came[1], swish_grad.came[2], down_grad.came[1], gate_grad.came[0], near, far, query_key_away,
        value_away, first_sum, out_one,
    ) = region(mixes_back, up_one, swish_two, down_one, gate_away)
    gate_one = gate_grad.one([first_sum])
    down_two = down_grad.two([gate_one])
    rank_part_near, up_part_near, bias_part_near = near[3:]
    rank_part_far, up_part_far, bias_part_far = far[3:]
    query_key_grad, value_grad = mixed_pair(near, far)
    first_grad = lax.psum_scatter(first_sum, "tensor", scatter_dimension=0, tiled=True)

    def third_window(query_key_away, value_away, gate_one, down_two):
        rank_part = jnp.concatenate([rank_part_near, rank_part_far], axis=0)
        rank_part = lax.all_to_all(jnp.take(rank_part, order, axis=0), "tensor", 0, 0)
        return (
            query_key_grad.hop(0, query_key_away), value_grad.hop(0, value_away),
            gate_grad.hop(1, gate_one), down_grad.hop(2, down_two), up_grad.two(),
            swish_grad.last(), jnp.sum(rank_part, axis=0).astype(bf16),
        )

    (
        query_key_grad.came[0], value_grad.came[0], gate_grad.came[1], down_grad.came[2], up_two,
        swish_share, rank_back,
    ) = region(third_window, query_key_away, value_away, gate_one, down_two)
    query_key_one = query_key_grad.one()
    value_one = value_grad.one([query_key_one])

    def fourth_window(query_key_one, value_one, up_two, out_one, layer_output):
        return (
            query_key_grad.hop(1, query_key_one), value_grad.hop(1, value_one), up_grad.hop(2, up_two),
            out_grad.hop(1, out_one), gate_grad.two(), down_grad.last(), layer_output,
        )

    (
        query_key_grad.came[1], value_grad.came[1], up_grad.came[2], out_grad.came[1], gate_two, down_share,
        layer_output,
    ) = region(fourth_window, query_key_one, value_one, up_two, out_one, layer_output)

    input_rows, attn_norm_part = grid_call(
        input_back_kernel,
        tiles,
        [own_spec, pl.BlockSpec((1, tile, width), lambda b, *_: (0, b, 0))]
        + [
            pl.BlockSpec((rank, tile), lambda b, *_: (0, b)), fixed((width, rank)), tile_spec,
            fixed((1, width)),
        ],
        [tile_spec, fixed((1, width))],
        [struct((length, width), bf16), struct((1, width), f32)],
        [
            place_index, layer_input, first_grad, rank_back, rank_down, middle_grad,
            attn_norm.reshape(1, width),
        ],
        prefetch=1,
        after=[gate_two],
    )
    out_two = out_grad.two([input_rows])
    query_key_two = query_key_grad.two([out_two])
    value_two = value_grad.two([query_key_two])

    rank_down_part = contract(rank_back, norm_near[:length], 1, 0)
    own_part = jnp.concatenate([rank_down_part, mlp_norm_part, attn_norm_part], axis=0)
    shared = jnp.concatenate(
        [
            sum(up_part_near) + sum(up_part_far),
            sum(bias_part_near) + sum(bias_part_far),
            sum(gain_back_near) + sum(gain_back_far),
        ],
        axis=0,
    )
    column = width // devices
    own_part = jnp.moveaxis(own_part.reshape(rank + 2, devices, column), 1, 0)
    own_size = (rank + 2) * column
    mail = jnp.concatenate(
        [
            own_part.reshape(devices, own_size),
            jnp.broadcast_to(shared.reshape(1, -1), (devices, shared.size)),
        ],
        axis=1,
    )

    def fifth_window(input_rows, query_key_two, value_two, gate_two, out_two, mail):
        mail = lax.all_to_all(mail, "seq", 0, 0)
        return (
            swap(input_rows, "tensor", 2), query_key_grad.hop(2, query_key_two),
            value_grad.hop(2, value_two), gate_grad.hop(2, gate_two),
            jnp.sum(mail.astype(f32), axis=0), up_grad.last(), out_grad.hop(2, out_two),
        )

    (
        second_rows, query_key_grad.came[2], value_grad.came[2], gate_grad.came[2], mail, up_share,
        out_grad.came[2],
    ) = region(
        fifth_window, input_rows, query_key_two, value_two, gate_two, out_two,
        mail.reshape(devices, 1, -1).astype(bf16),
    )

    def sixth_window(input_rows, second_rows):
        pair = swap(jnp.stack([input_rows, second_rows]), "tensor", 1)
        whole = pl.BlockSpec((length, width), lambda k, order: (0, 0))
        input_grad = grid_call(
            place_kernel,
            (4,),
            [whole] * 4,
            pl.BlockSpec((1, length, width), lambda k, order: (order[k], 0, 0)),
            struct((seq_count, length, width), bf16),
            [order, input_rows, pair[0], second_rows, pair[1]],
            prefetch=1,
        )
        return input_grad, query_key_grad.last(), value_grad.last(), gate_grad.last(), out_grad.last()

    input_grad, query_key_share, value_share, gate_share, out_share = region(
        sixth_window, input_rows, second_rows
    )
    mail = mail.reshape(-1)
    own_part = mail[:own_size].reshape(rank + 2, column)
    shared = mail[own_size:].reshape(rank + 2, DK)
    own_part = sum_over(own_part, "tensor")
    return (
        layer_output,
        input_grad,
        own_part[rank + 1],
        query_key_share[:, :DK],
        query_key_share[:, DK:],
        value_share,
        gate_share,
        own_part[:rank].T,
        shared[:rank],
        shared[rank],
        shared[rank + 1],
        out_share,
        own_part[rank],
        swish_share,
        up_share,
        down_share,
    )


def solution(mesh):
    return jax.shard_map(
        local,
        mesh=mesh,
        in_specs=(
            P(None, "seq", None),
            P(),
            P(None, "tensor"),
            P(None, "tensor"),
            P(None, "tensor"),
            P(None, "tensor"),
            P(),
            P(None, "tensor"),
            P("tensor"),
            P("tensor"),
            P("tensor", None),
            P(),
            P(None, "tensor"),
            P(None, "tensor"),
            P("tensor", None),
            P(None, "seq", None),
        ),
        out_specs=(
            P(None, "seq", None),
            P(None, "seq", None),
            P("seq"),
            P("seq", "tensor"),
            P("seq", "tensor"),
            P("seq", "tensor"),
            P("seq", "tensor"),
            P("seq", None),
            P(None, "tensor"),
            P("tensor"),
            P("tensor"),
            P("tensor", "seq"),
            P("seq"),
            P("seq", "tensor"),
            P("seq", "tensor"),
            P("tensor", "seq"),
        ),
        check_vma=False,
    )
```

```python
import functools

import jax
import jax.numpy as jnp
from jax import lax
from jax.experimental import pallas as pl
from jax.experimental.pallas import tpu as pltpu
from jax.sharding import PartitionSpec as P

DK = 512
BLOCK = 64
EXTRA = 16
ROWS = 256
COST = 1024
VMEM = 48 * 1024 * 1024

bf16 = jnp.bfloat16
f32 = jnp.float32
highest_precision = lax.Precision.HIGHEST
epsilon = 1e-06


def contract(left, right, left_dim, right_dim, precision=None):
    return lax.dot_general(
        left,
        right,
        (((left_dim,), (right_dim,)), ((), ())),
        preferred_element_type=f32,
        precision=precision,
    )


def product(left, right):
    return contract(left, right, 1, 0)


def across(left, right):
    return contract(left, right, 0, 0)


def against(left, right):
    return contract(left, right, 1, 1)


def forget_logits(rank_ref, up_ref, bias_ref):
    return product(rank_ref[...], up_ref[...]) + bias_ref[...].astype(f32)


def positions(count):
    rows = lax.broadcasted_iota(jnp.int32, (count, count), 0)
    cols = lax.broadcasted_iota(jnp.int32, (count, count), 1)
    return rows, cols


def spread(pieces, size):
    width = pieces[0].shape[1]
    return jnp.concatenate([jnp.broadcast_to(piece, (size, width)) for piece in pieces], axis=0)


def scaled_pair(level, query_scaled, key_rows, run):
    count = run.shape[0]
    if level == 0:
        starts = range(0, count, BLOCK)
        center = spread([run[s + BLOCK // 2 : s + BLOCK // 2 + 1] for s in starts], BLOCK)
        query_factor = jnp.exp(run - center)
        key_factor = jnp.exp(center - run)
        return query_scaled * query_factor, key_rows * key_factor, query_factor, key_factor
    group = BLOCK << level
    half = group // 2
    center = spread([run[s + half - 1 : s + half] for s in range(0, count, group)], group)
    place = lax.broadcasted_iota(jnp.int32, run.shape, 0)
    right = (place % group) >= half
    gap = run - center
    query_factor = jnp.where(right, jnp.exp(jnp.where(right, gap, 0.0)), 0.0)
    key_factor = jnp.where(right, 0.0, jnp.exp(jnp.where(right, 0.0, -gap)))
    return query_scaled * query_factor, key_rows * key_factor, query_factor, key_factor


def level_mask(level, rows, cols):
    if level == 0:
        return (rows // BLOCK == cols // BLOCK) & (cols <= rows)
    group = BLOCK << level
    half = group // 2
    return (rows // group == cols // group) & (rows % group >= half) & (cols % group < half)


def level_count(count):
    levels = 1
    while (BLOCK << (levels - 1)) < count:
        levels += 1
    return levels


def norm_kernel(order_ref, input_ref, grad_ref, gain_ref, norm_ref, rows_ref):
    values = input_ref[0].astype(f32)
    scale = lax.rsqrt(jnp.mean(values * values, axis=-1, keepdims=True) + epsilon)
    norm_ref[...] = (values * scale * gain_ref[...].astype(f32)).astype(bf16)
    rows_ref[...] = grad_ref[0]


def decay_kernel(rank_ref, up_ref, bias_ref, run_ref):
    logits = forget_logits(rank_ref, up_ref, bias_ref)
    decays = (jnp.minimum(logits, 0.0) - jnp.log1p(jnp.exp(-jnp.abs(logits)))) * (1.0 / 16.0)
    rows, cols = positions(decays.shape[0])
    run_ref[...] = contract((cols <= rows).astype(f32), decays, 1, 0, highest_precision)


def total_lines(run):
    return as_lines(run[run.shape[0] - 1 :])


def as_lines(*totals):
    place = lax.broadcasted_iota(jnp.int32, (EXTRA, DK), 0)
    lines = jnp.zeros((EXTRA, DK), f32)
    for first, total in enumerate(totals):
        high = total.astype(bf16)
        rest = total - high.astype(f32)
        middle = rest.astype(bf16)
        low = (rest - middle.astype(f32)).astype(bf16)
        for at, line in enumerate((high, middle, low)):
            lines = jnp.where(place == 3 * first + at, line.astype(f32), lines)
    return lines.astype(bf16)


def from_lines(lines, first=0):
    lines = lines.astype(f32)[3 * first : 3 * first + 3]
    return lines[0:1] + lines[1:2] + lines[2:3]


def state_of(key_ref, value_ref, run):
    left = (key_ref[...].astype(f32) * jnp.exp(run[run.shape[0] - 1 :] - run)).astype(bf16)
    return across(value_ref[...], left).astype(bf16)


def state_kernel(key_ref, value_ref, run_ref, state_ref, lines_ref):
    run = run_ref[...]
    state_ref[0] = state_of(key_ref, value_ref, run)
    lines_ref[0] = total_lines(run)


def cut_state_kernel(me_ref, key_ref, value_ref, run_ref, keep_ref, send_ref, lines_ref, held):
    run = run_ref[...]
    held[...] = state_of(key_ref, value_ref, run).reshape(held.shape)
    lines = total_lines(run)
    y, z = me_ref[0] % 2, me_ref[0] // 2
    for at in range(4):
        keep_ref[0, at] = held[y * 4 + (z ^ at)]
        send_ref[0, at] = held[(1 - y) * 4 + (z ^ at)]
    lines_ref[0] = lines
    send_ref[0, 4, :EXTRA] = lines


def pair_kernel(me_ref, keep_ref, lines_ref, came_ref, first_ref, *part_refs):
    lead = me_ref[0] % 2 == 0
    own, other = from_lines(lines_ref[0]), from_lines(came_ref[0, 4, :EXTRA])
    later = jnp.exp(jnp.where(lead, other, own))
    lines = as_lines(jnp.where(lead, own, other), jnp.where(lead, other, own))
    for at, part_ref in enumerate(part_refs):
        mine, came = keep_ref[0, at].astype(f32), came_ref[0, at].astype(f32)
        first = jnp.where(lead, mine, came)
        first_ref[0, at] = first.astype(bf16)
        rows = first.shape[0]
        part_ref[0, :rows] = (first * later + jnp.where(lead, came, mine)).astype(bf16)
        part_ref[0, rows:] = lines


def chain_kernel(me_ref, *refs):
    part_refs, out_refs, every_ref = refs[:4], refs[4:8], refs[8]
    held, lines, entered = refs[9:]
    z = me_ref[0] // 2
    rows = held.shape[1]
    for at in range(4):
        held[z ^ at] = part_refs[at][0, :rows]
        lines[z ^ at] = part_refs[at][0, rows:]
    carry = jnp.zeros(held.shape[1:], f32)
    for at in range(4):
        entered[at] = carry.astype(bf16)
        totals = from_lines(lines[at]), from_lines(lines[at], 1)
        for y in range(2):
            every_ref[2 * at + y, 0] = as_lines(totals[y])
        carry = carry * jnp.exp(totals[0] + totals[1]) + held[at].astype(f32)
    for at in range(4):
        out_refs[at][0] = entered[z ^ at]


def enter_kernel(me_ref, lines_ref, came_ref, first_ref, *refs):
    *part_refs, whole_ref, send_ref = refs
    y, z = me_ref[0] % 2, me_ref[0] // 2
    lead = y == 0
    earlier = jnp.exp(jnp.where(lead, from_lines(lines_ref[0]), from_lines(came_ref[0, 0, :EXTRA])))
    for at in range(4):
        pair = part_refs[at][0].astype(f32)
        inner = pair * earlier + first_ref[0, at].astype(f32)
        whole_ref[0, 0, z ^ at] = jnp.where(lead, pair, inner).astype(bf16)
        send_ref[0, z ^ at] = jnp.where(lead, inner, pair).astype(bf16)


def join_kernel(me_ref, came_ref, whole_ref):
    whole_ref[0, 0] = came_ref[0]


def score_kernel(query_ref, key_ref, run_ref, score_ref):
    run = run_ref[...]
    query_scaled = query_ref[...].astype(f32) * DK ** (-0.5)
    key_rows = key_ref[...].astype(f32)
    rows, cols = positions(run.shape[0])
    scores = jnp.zeros(rows.shape, f32)
    for level in range(level_count(run.shape[0])):
        left, right, _, _ = scaled_pair(level, query_scaled, key_rows, run)
        scores = jnp.where(
            level_mask(level, rows, cols), against(left.astype(bf16), right.astype(bf16)), scores
        )
    score_ref[0] = scores.astype(bf16)


def whole_state(ref):
    return ref[...].reshape(DK, DK)


def faded_queries(query_ref, run_ref):
    return (query_ref[...].astype(f32) * DK ** (-0.5) * jnp.exp(run_ref[...])).astype(bf16)


def mix_kernel(query_ref, value_ref, run_ref, score_ref, state_ref, gate_ref, gain_ref, mixed_ref, branch_ref):
    faded = faded_queries(query_ref, run_ref)
    mixed = product(score_ref[0], value_ref[...]) + against(faded, whole_state(state_ref))
    mixed_ref[...] = mixed
    scale = lax.rsqrt(jnp.mean(mixed * mixed, axis=-1, keepdims=True) + epsilon)
    gate = gate_ref[...]
    branch_ref[...] = (
        mixed * scale * gain_ref[...].astype(f32) * (gate * jax.nn.sigmoid(gate))
    ).astype(bf16)


def branch_back_kernel(
    first_ref, second_ref, weight_ref, mixed_ref, gate_ref, gain_ref, query_ref, run_ref,
    gate_back_ref, mixed_back_ref, gain_back_ref, state_back_ref,
):
    branch_grad = against(either(first_ref, second_ref), weight_ref[...])
    mixed = mixed_ref[...]
    scale = lax.rsqrt(jnp.mean(mixed * mixed, axis=-1, keepdims=True) + epsilon)
    unit = mixed * scale
    gate = gate_ref[...]
    gain = gain_ref[...].astype(f32)
    sig = jax.nn.sigmoid(gate)
    gate_back_ref[...] = (branch_grad * unit * gain * sig * (1.0 + gate * (1.0 - sig))).astype(bf16)
    shaped_grad = branch_grad * (gate * sig)
    gain_back_ref[0] = jnp.sum(shaped_grad * unit, axis=0, keepdims=True)
    unit_grad = shaped_grad * gain
    mixed_grad = scale * (unit_grad - unit * jnp.mean(unit_grad * unit, axis=-1, keepdims=True))
    mixed_back = mixed_grad.astype(bf16)
    mixed_back_ref[...] = mixed_back
    faded = faded_queries(query_ref, run_ref)
    state_back_ref[...] = across(mixed_back, faded).astype(bf16).reshape(state_back_ref.shape)


def ordered_sum(mask, values):
    high = values.astype(bf16)
    low = (values - high.astype(f32)).astype(bf16)
    ones = mask.astype(f32).astype(bf16)
    return product(ones, high) + product(ones, low)


def mix_back_kernel(
    query_ref, key_ref, value_ref, grad_ref, run_ref, score_ref, state_ref, state_back_ref,
    rank_ref, up_ref, bias_ref,
    query_back_ref, key_back_ref, value_back_ref, rank_back_ref, up_back_ref, bias_back_ref,
):
    run = run_ref[...]
    count = run.shape[0]
    query_scaled = query_ref[...].astype(f32) * DK ** (-0.5)
    key_rows = key_ref[...].astype(f32)
    values = value_ref[...]
    grads = grad_ref[...]
    state = whole_state(state_ref)
    state_back = whole_state(state_back_ref)
    rows, cols = positions(count)
    pairs = against(grads, values)

    closing = run[count - 1 : count]
    fade_in = jnp.exp(run)
    fade_out = jnp.exp(closing - run)
    kept = (key_rows * fade_out).astype(bf16)
    value_back_ref[...] = (across(score_ref[0], grads) + against(kept, state_back)).astype(bf16)

    from_state = product(grads, state)
    to_state = product(values, state_back)
    query_back = fade_in * from_state
    key_back = fade_out * to_state
    decay_back = jnp.exp(closing) * jnp.sum(
        state.astype(f32) * state_back.astype(f32), axis=0, keepdims=True
    )
    decay_back = decay_back + ordered_sum(cols >= rows, query_scaled * fade_in * from_state)
    decay_back = decay_back + ordered_sum(cols < rows, key_rows * fade_out * to_state)
    for level in range(level_count(count)):
        left, right, query_factor, key_factor = scaled_pair(level, query_scaled, key_rows, run)
        left, right = left.astype(bf16), right.astype(bf16)
        here = jnp.where(level_mask(level, rows, cols), pairs, 0.0).astype(bf16)
        to_query = product(here, right)
        to_key = across(here, left)
        query_back = query_back + query_factor * to_query
        key_back = key_back + key_factor * to_key
        left_part = left.astype(f32) * to_query
        right_part = right.astype(f32) * to_key
        if level == 0:
            mask = (rows // BLOCK == cols // BLOCK) & (cols >= rows)
            decay_back = decay_back + ordered_sum(mask, left_part - right_part)
        else:
            group = BLOCK << level
            half = group // 2
            same = rows // group == cols // group
            late = same & (rows % group >= half) & (cols >= rows)
            early = same & (rows % group < half) & (cols < rows)
            decay_back = decay_back + ordered_sum(late | early, left_part + right_part)
    query_back_ref[...] = (query_back * DK ** (-0.5)).astype(bf16)
    key_back_ref[...] = key_back.astype(bf16)
    logits = forget_logits(rank_ref, up_ref, bias_ref)
    logit_back = (decay_back * jax.nn.sigmoid(-logits) * (1.0 / 16.0)).astype(bf16)
    rank_back_ref[0] = against(up_ref[...], logit_back)
    up_back_ref[0] = across(rank_ref[...], logit_back)
    bias_back_ref[0] = jnp.sum(logit_back.astype(f32), axis=0, keepdims=True)


def prefix_kernel(reverse, lines_ref, parts_ref, out_ref):
    count = parts_ref.shape[0]
    rows = out_ref.shape[2]
    carry = jnp.zeros(out_ref.shape[2:], f32)
    for step in range(count):
        at = count - 1 - step if reverse else step
        out_ref[at, 0] = carry.astype(bf16)
        total = from_lines(lines_ref[at, 0])
        carry = carry * jnp.exp(total) + parts_ref[at, 0].astype(f32)


def hold_kernel(values_ref, out_ref):
    out_ref[...] = values_ref[...]


def either(first_ref, second_ref):
    return jnp.where(pl.program_id(0) == 0, first_ref[...], second_ref[...])


def middle_kernel(place_ref, input_ref, own_ref, first_ref, last_ref, gain_ref, middle_ref, second_ref):
    middle = input_ref[0].astype(f32) + (
        own_ref[...].astype(f32) + first_ref[...].astype(f32) + last_ref[...].astype(f32)
    )
    middle_ref[...] = middle
    scale = lax.rsqrt(jnp.mean(middle * middle, axis=-1, keepdims=True) + epsilon)
    second_ref[...] = (middle * scale * gain_ref[...].astype(f32)).astype(bf16)


def norm_back(values, grad, gain):
    scale = lax.rsqrt(jnp.mean(values * values, axis=-1, keepdims=True) + epsilon)
    unit = values * scale
    scaled = grad * gain
    back = scale * (scaled - unit * jnp.mean(scaled * unit, axis=-1, keepdims=True))
    return back, jnp.sum(grad * unit, axis=0, keepdims=True)


def add_part(out_ref, part):
    @pl.when(pl.program_id(0) == 0)
    def _():
        out_ref[...] = part

    @pl.when(pl.program_id(0) != 0)
    def _():
        out_ref[...] += part


def middle_back_kernel(
    place_ref, grad_ref, own_ref, first_ref, last_ref, middle_ref, gain_ref, back_ref, rows_ref, part_ref
):
    grad = own_ref[...].astype(f32) + first_ref[...].astype(f32) + last_ref[...].astype(f32)
    back, part = norm_back(middle_ref[...], grad, gain_ref[...].astype(f32))
    back = grad_ref[0].astype(f32) + back
    back_ref[...] = back
    rows_ref[...] = back.astype(bf16)
    add_part(part_ref, part)


def input_back_kernel(
    place_ref, input_ref, own_ref, first_ref, last_ref, rank_ref, down_ref, middle_ref, gain_ref, rows_ref, part_ref
):
    grad = own_ref[0].astype(f32) + first_ref[0].astype(f32) + last_ref[...].astype(f32)
    grad = grad + contract(rank_ref[...], down_ref[...], 0, 1)
    back, part = norm_back(input_ref[0].astype(f32), grad, gain_ref[...].astype(f32))
    rows_ref[...] = (middle_ref[...] + back).astype(bf16)
    add_part(part_ref, part)


def feed_kernel(
    first_ref, second_ref, grads_ref, swish_ref, up_ref, down_ref,
    inner_ref, swish_back_ref, up_back_ref, second_back_ref, out_ref,
    swish_held, up_held, down_held, semaphores,
):
    copies = [
        pltpu.make_async_copy(swish_ref, swish_held, semaphores.at[0]),
        pltpu.make_async_copy(up_ref, up_held, semaphores.at[1]),
        pltpu.make_async_copy(down_ref, down_held, semaphores.at[2]),
    ]
    start = pl.program_id(0) == 0

    @pl.when(start)
    def _():
        for copy in copies:
            copy.start()

    rows = either(first_ref, second_ref)

    @pl.when(start)
    def _():
        copies[0].wait()

    swish = product(rows, swish_held[...])

    @pl.when(start)
    def _():
        copies[1].wait()

    up = product(rows, up_held[...])
    sig = jax.nn.sigmoid(swish)
    act = swish * sig
    inner = (act * up).astype(bf16)
    inner_ref[...] = inner

    @pl.when(start)
    def _():
        copies[2].wait()

    inner_grad = against(grads_ref[...], down_held[...])
    swish_back = (inner_grad * up * sig * (1.0 + swish * (1.0 - sig))).astype(bf16)
    up_back = (inner_grad * act).astype(bf16)
    swish_back_ref[...] = swish_back
    up_back_ref[...] = up_back
    second_back_ref[...] = (against(swish_back, swish_held[...]) + against(up_back, up_held[...])).astype(bf16)
    out_ref[...] = product(inner, down_held[...]).astype(bf16)


def place_kernel(order_ref, *refs):
    out_ref = refs[-1]
    step = pl.program_id(0)
    for k in range(4):

        @pl.when(step == k)
        def _():
            out_ref[0] = refs[k][...]


def sum_kernel(*refs):
    *refs, keep_ref, send_ref = refs
    count = len(refs) // 2
    rows = keep_ref.shape[1]
    total = against(refs[0][...], refs[count][...])
    for k in range(1, count):
        total = total + against(refs[k][...], refs[count + k][...])
    total = total.astype(bf16)
    keep_ref[0] = total[:rows]
    send_ref[0] = total[rows:]


def grad_kernel(parts, groups, cut_groups, turned, pick_ref, *refs):
    cuts, refs = refs[: parts * cut_groups], refs[parts * cut_groups :]
    others, refs = refs[: parts * groups], refs[parts * groups :]
    arrived, out_ref = refs[:-1], refs[-1]
    for group in range(groups):
        total = None
        members = others[group * parts : (group + 1) * parts]
        width = members[0].shape[1]
        columns = slice(group * width, (group + 1) * width)
        first = group * parts if cut_groups > 1 else 0
        for cut, other in zip(cuts[first : first + parts], members):
            part = across(cut[...], other[...])
            total = part if total is None else total + part
        for ref in arrived:
            total = total + ref[0, :, columns].astype(f32)
        if turned:
            out_ref[...] = total.T
        else:
            out_ref[0, :, columns] = total.astype(out_ref.dtype)


def struct(shape, dtype):
    return jax.ShapeDtypeStruct(shape, dtype)


def grid_call(kernel, grid, in_specs, out_specs, out_shape, args, prefetch=0, after=(), scratch=(), into=()):
    first, last = len(args), len(args) + len(after)
    aliases = {}
    for array, at in into:
        aliases[last] = at
        after = (*after, array)
        last += 1

    def run(*refs):
        kernel(*refs[:first], *refs[last:])

    return pl.pallas_call(
        run,
        grid_spec=pltpu.PrefetchScalarGridSpec(
            num_scalar_prefetch=prefetch,
            grid=grid,
            in_specs=list(in_specs) + [pl.BlockSpec(memory_space=pl.ANY)] * len(after),
            out_specs=out_specs,
            scratch_shapes=list(scratch),
        ),
        out_shape=out_shape,
        input_output_aliases=aliases,
        compiler_params=pltpu.CompilerParams(vmem_limit_bytes=VMEM),
        cost_estimate=pl.CostEstimate(flops=COST, bytes_accessed=COST, transcendentals=0),
    )(*args, *after)


def swap(values, axis, distance):
    count = lax.axis_size(axis)
    return lax.ppermute(values, axis, [(i, i ^ distance) for i in range(count)])


def region(function, *args):
    shapes = jax.eval_shape(function, *args)

    def never(*_):
        return jax.tree.map(lambda a: jnp.zeros(a.shape, a.dtype), shapes)

    return lax.cond(lax.axis_index("seq") >= 0, function, never, *args)


def bits_of(count):
    return [1 << k for k in range(count.bit_length() - 1)]


def hold(values, after):
    spec = pl.BlockSpec(values.shape, lambda: (0,) * values.ndim)
    return grid_call(hold_kernel, (), [spec], spec, struct(values.shape, values.dtype), [values], after=after)


def chunk_spec(count, first=0):
    return pl.BlockSpec((count, 1, DK // count, DK), lambda b, *_: (0, b + first, 0, 0))


def carried(pieces, lines, reverse, after=()):
    count, seq_count, share, _ = pieces.shape
    return grid_call(
        functools.partial(prefix_kernel, reverse),
        (seq_count,),
        [pl.BlockSpec((count, 1, EXTRA, DK), lambda b: (0, b, 0, 0)), chunk_spec(count)],
        chunk_spec(count),
        struct((count, seq_count, share, DK), bf16),
        [lines, pieces],
        after=after,
    )


def deal(pieces):
    return lax.all_to_all(pieces, "seq", 0, 0)


def tensor_reduce(near, far):
    third = swap(far[1], "tensor", 1)
    second = (far[0].astype(f32) + third.astype(f32)).astype(bf16)
    first = swap(near[1], "tensor", 1)
    return (near[0], first, swap(second, "tensor", 2)), second


def tensor_gather(own):
    first = swap(own, "tensor", 1)
    second = swap(own, "tensor", 2)

    def third(after):
        return swap(hold(second, after) if after else second, "tensor", 1)

    return own, first, second, third


def grad_part(cuts, groups, picks, arrived, dtype, turned=False, after=()):
    rows = ROWS
    width = groups[0][0][0].shape[1]
    whole = width * len(groups)
    parts = len(groups[0])
    cut_groups = len(cuts)
    cuts = [block for group in cuts for block in group]
    share = cuts[0][0].shape[1] // lax.axis_size("seq")
    chunks = len(picks)
    me = lax.axis_index("seq")
    index = jnp.stack([me ^ r for r in picks]).astype(jnp.int32)
    others = [block for group in groups for block in group]
    in_specs = [pl.BlockSpec((rows, share), lambda k, pick, at=at: (at, pick[k])) for _, at in cuts]
    in_specs += [pl.BlockSpec((rows, width), lambda k, pick, at=at: (at, 0)) for _, at in others]
    for _, first in arrived:
        in_specs.append(pl.BlockSpec((1, share, whole), lambda k, pick, first=first: (k + first, 0, 0)))
    if turned:
        out_spec = pl.BlockSpec((whole, share), lambda k, pick: (0, 0))
        shape = (whole, share)
    else:
        out_spec = pl.BlockSpec((1, share, whole), lambda k, pick: (k, 0, 0))
        shape = (chunks, share, whole)
    return grid_call(
        functools.partial(grad_kernel, parts, len(groups), cut_groups, turned),
        (chunks,),
        in_specs,
        out_spec,
        struct(shape, dtype),
        [index, *[a for a, _ in cuts], *[a for a, _ in others], *[a for a, _ in arrived]],
        prefetch=1,
        after=after,
    )


class Scatter:
    def __init__(self, cuts, groups, order, turned=False):
        cuts = cuts if isinstance(cuts[0], list) else [cuts]
        self.cuts, self.groups, self.order, self.turned = cuts, groups, order, turned
        self.split = lax.axis_size("seq") == 8
        self.came = [None] * 3

    def part(self, picks, arrived, dtype, turned=False, after=()):
        return grad_part(self.cuts, self.groups, picks, arrived, dtype, turned, after)

    def hop(self, at, part):
        if self.split:
            return swap(part, "seq", self.order[at])
        return part if at else lax.psum_scatter(part, "seq", scatter_dimension=0, tiled=True)

    def away(self, after=()):
        if not self.split:
            return jnp.concatenate(
                [
                    sum(
                        across(a[i * ROWS : (i + 1) * ROWS], b[j * ROWS : (j + 1) * ROWS])
                        for (a, i), (b, j) in zip(cuts, group)
                    ).astype(bf16)
                    for cuts, group in zip(
                        self.cuts if len(self.cuts) > 1 else self.cuts * len(self.groups), self.groups
                    )
                ],
                axis=1,
            )
        a, b, c = self.order
        return self.part([a ^ b, a ^ b ^ c, a ^ c, a], [], bf16, after=after)

    def one(self, after=()):
        if not self.split:
            return self.came[0]
        a, b, c = self.order
        return self.part([b, b ^ c], [(self.came[0], 0)], bf16, after=after)

    def two(self, after=()):
        if not self.split:
            return self.came[0]
        c = self.order[2]
        return self.part([c], [(self.came[0], 2), (self.came[1], 1)], bf16, after=after)

    def last(self, after=()):
        if not self.split:
            total = self.came[0].astype(f32)
            return total.T if self.turned else total
        arrived = [(self.came[0], 3), (self.came[1], 0), (self.came[2], 0)]
        total = self.part([0], arrived, f32, self.turned, after=after)
        return total if self.turned else total[0]


def sum_over(values, axis):
    for bit in bits_of(lax.axis_size(axis)):
        values = values + swap(values, axis, bit)
    return values


def local(
    layer_input,
    attn_norm,
    query_weight,
    key_weight,
    value_weight,
    gate_weight,
    rank_down,
    rank_up,
    decay_bias,
    head_gain,
    out_weight,
    mlp_norm,
    swish_weight,
    up_weight,
    down_weight,
    cotangent,
):
    seq_count, length, width = layer_input.shape
    place = lax.axis_index("tensor")
    devices = lax.axis_size("seq")
    half = seq_count // 2
    half_rows = half * length
    rank = rank_down.shape[1]
    bias = decay_bias.reshape(1, DK)
    gain = head_gain.reshape(1, DK)
    share = DK // devices

    def row_spec(size):
        return pl.BlockSpec((length, size), lambda b, *_: (b, 0))

    def fixed(shape):
        return pl.BlockSpec(shape, lambda b, *_: (0,) * len(shape))

    def square(size):
        return pl.BlockSpec((1, size, size), lambda b, *_: (b, 0, 0))

    def line(rows, size):
        return pl.BlockSpec((1, rows, size), lambda b, *_: (b, 0, 0))

    def rows_of(size, dtype):
        return struct((half_rows, size), dtype)

    chunks = struct((devices, seq_count, share, DK), bf16)
    whole_block = pl.BlockSpec((length, width), lambda b, *_: (0, 0))

    def blocks(near, far):
        return [(near, 0), (near, 1), (far, 0), (far, 1)]

    def halves(values):
        return values[:length], values[length:]

    def first_rows(order, after=()):
        spec = pl.BlockSpec((1, length, width), lambda b, order: (order[b], 0, 0))
        return grid_call(
            norm_kernel,
            (half,),
            [spec, spec, fixed((1, width))],
            [row_spec(width), row_spec(width)],
            [rows_of(width, bf16), rows_of(width, bf16)],
            [order, layer_input, cotangent, attn_norm.reshape(1, width)],
            prefetch=1,
            after=after,
        )

    def decays(norm):
        rank_rows = product(norm, rank_down).astype(bf16)
        run = grid_call(
            decay_kernel,
            (half,),
            [row_spec(rank), fixed((rank, DK)), fixed((1, DK))],
            row_spec(DK),
            rows_of(DK, f32),
            [rank_rows, rank_up, bias],
        )
        return rank_rows, run

    quarter = DK // 8
    me = lax.axis_index("seq").astype(jnp.int32).reshape(1)

    def quarters(count, size=quarter):
        return pl.BlockSpec((1, count, size, DK), lambda b, *_: (b, 0, 0, 0))

    def states(norm, run, after=()):
        keys = product(norm, key_weight).astype(bf16)
        values = product(norm, value_weight).astype(bf16)
        lines = struct((half, EXTRA, DK), bf16)
        if devices != 8:
            parts = grid_call(
                state_kernel,
                (half,),
                [row_spec(DK)] * 3,
                [square(DK), line(EXTRA, DK)],
                [struct((half, DK, DK), bf16), lines],
                [keys, values, run],
                after=after,
            )
        else:
            parts = grid_call(
                cut_state_kernel,
                (half,),
                [row_spec(DK)] * 3,
                [quarters(4), quarters(5), line(EXTRA, DK)],
                [struct((half, 4, quarter, DK), bf16), struct((half, 5, quarter, DK), bf16), lines],
                [me, keys, values, run],
                prefetch=1,
                after=after,
                scratch=[pltpu.VMEM((8, quarter, DK), bf16)],
            )
        return keys, values, parts

    def pairs(parts, came, after=()):
        keep, _, lines = parts
        return grid_call(
            pair_kernel,
            (half,),
            [quarters(4), line(EXTRA, DK), quarters(5)],
            [quarters(4)] + [line(quarter + EXTRA, DK)] * 4,
            [struct((half, 4, quarter, DK), bf16)] + [struct((half, quarter + EXTRA, DK), bf16)] * 4,
            [me, keep, lines, came],
            prefetch=1,
            after=after,
        )

    def chain(own, came, first, after=(), into=()):
        return grid_call(
            chain_kernel,
            (half,),
            [line(quarter + EXTRA, DK)] * 4,
            [line(quarter, DK)] * 4
            + [pl.BlockSpec((8, 1, EXTRA, DK), lambda b, *_: (0, b + first, 0, 0))],
            [struct((half, quarter, DK), bf16)] * 4 + [struct((8, seq_count, EXTRA, DK), bf16)],
            [me, own, *came],
            prefetch=1,
            after=after,
            into=into,
            scratch=[
                pltpu.VMEM((4, quarter, DK), bf16),
                pltpu.VMEM((4, EXTRA, DK), bf16),
                pltpu.VMEM((4, quarter, DK), bf16),
            ],
        )

    def enter(parts, came, first, own, others, after=()):
        return grid_call(
            enter_kernel,
            (half,),
            [line(EXTRA, DK), pl.BlockSpec((1, 1, quarter, DK), lambda b, *_: (b, 4, 0, 0)), quarters(4)]
            + [line(quarter, DK)] * 4,
            [pl.BlockSpec((1, 1, 4, quarter, DK), lambda b, me: (me[0] % 2, b, 0, 0, 0)), quarters(4)],
            [struct((2, half, 4, quarter, DK), bf16), struct((half, 4, quarter, DK), bf16)],
            [me, parts[2], came, first, own, *others],
            prefetch=1,
            after=after,
        )

    def join(whole, came):
        return grid_call(
            join_kernel,
            (half,),
            [quarters(4)],
            pl.BlockSpec((1, 1, 4, quarter, DK), lambda b, me: (1 - me[0] % 2, b, 0, 0, 0)),
            struct(whole.shape, bf16),
            [me, came],
            prefetch=1,
            into=[(whole, 0)],
        )

    def along(parts):
        return [swap(part, "seq", 2 * at) for at, part in enumerate(parts, 1)]

    def scored(norm, keys, run, after=()):
        queries = product(norm, query_weight).astype(bf16)
        gates = product(norm, gate_weight)
        scores = grid_call(
            score_kernel,
            (half,),
            [row_spec(DK)] * 3,
            square(length),
            struct((half, length, length), bf16),
            [queries, keys, run],
            after=after,
        )
        return queries, gates, scores

    def mix(queries, values, run, scores, incoming, at, gates, after=()):
        return grid_call(
            mix_kernel,
            (half,),
            [row_spec(DK)] * 3
            + [square(length), state_specs[at], row_spec(DK), fixed((1, DK))],
            [row_spec(DK), row_spec(DK)],
            [rows_of(DK, f32), rows_of(DK, bf16)],
            [queries, values, run, scores, incoming, gates, gain],
            after=after,
        )

    order = jnp.arange(seq_count, dtype=jnp.int32) ^ place
    place_index = order[:1]
    norm_far, grads_far = first_rows(order[half:])
    rank_far, run_far = decays(norm_far)
    keys_far, values_far, parts_far = states(norm_far, run_far)
    norm_near, grads_near = first_rows(order[:half], [parts_far[1]])
    rank_near, run_near = decays(norm_near)
    keys_near, values_near, parts_near = states(norm_near, run_near)
    queries_far, gates_far, scores_far = scored(norm_far, keys_far, run_far, [parts_near[1]])
    if devices != 8:
        queries_near, gates_near, scores_near = scored(norm_near, keys_near, run_near, [scores_far])
        state = jnp.concatenate([parts_far[0], parts_near[0]], axis=0)
        state = jnp.moveaxis(state.reshape(seq_count, devices, share, DK), 1, 0)
        every_line = jnp.concatenate([parts_far[1], parts_near[1]], axis=0)
        lines = deal(jnp.broadcast_to(every_line[None], (devices, *every_line.shape)))
        incoming = deal(carried(deal(state), lines, False))
        incoming_far = incoming_near = incoming
        state_specs = [chunk_spec(devices, at) for at in (0, half)]
    else:
        came_far = swap(parts_far[1], "seq", 1)
        came_near = swap(parts_near[1], "seq", 1)
        first_far, *pair_far = pairs(parts_far, came_far, [parts_near[1]])
        others_far = along(pair_far[1:])
        first_near, *pair_near = pairs(parts_near, came_near, [pair_far[0], scores_far])
        others_near = along(pair_near[1:])
        *chain_far, lines = chain(pair_far[0], others_far, 0, [pair_near[0]])
        back_far = along(chain_far[1:])
        queries_near, gates_near, scores_near = scored(norm_near, keys_near, run_near, [chain_far[0]])
        *chain_near, lines = chain(pair_near[0], others_near, half, [chain_far[0]], [(lines, 4)])
        back_near = along(chain_near[1:])
        whole_far, send_far = enter(parts_far, came_far, first_far, chain_far[0], back_far, [chain_near[0]])
        half_far = swap(send_far, "seq", 1)
        whole_near, send_near = enter(
            parts_near, came_near, first_near, chain_near[0], back_near, [send_far, scores_near]
        )
        half_near = swap(send_near, "seq", 1)
        incoming_far = join(whole_far, half_far)
        incoming_near = join(whole_near, half_near)
        state_specs = [
            pl.BlockSpec((2, 1, 4, quarter, DK), lambda b, *_: (0, b, 0, 0, 0)) for at in range(2)
        ]

    mixed_far, branch_far = mix(queries_far, values_far, run_far, scores_far, incoming_far, 0, gates_far)
    out_far = product(branch_far, out_weight).astype(bf16)
    out_third = swap(out_far[length:], "tensor", 1)
    out_second = (out_far[:length].astype(f32) + out_third.astype(f32)).astype(bf16)
    out_last = swap(out_second, "tensor", 2)
    mixed_near, branch_near = mix(
        queries_near, values_near, run_near, scores_near, incoming_near, 1, gates_near, [out_second]
    )
    out_near = product(branch_near, out_weight).astype(bf16)
    out_first = region(lambda values: swap(values[length:], "tensor", 1), out_near)
    out_parts = (out_near[:length], out_first, out_last)

    tile = 128
    tiles = (length // tile,)
    tile_spec = pl.BlockSpec((tile, width), lambda b, *_: (b, 0))
    own_spec = pl.BlockSpec((1, tile, width), lambda b, place: (place[0], b, 0))
    gain_two = mlp_norm.reshape(1, width)
    middle, second_own = grid_call(
        middle_kernel,
        tiles,
        [own_spec] + [tile_spec] * 3 + [fixed((1, width))],
        [tile_spec] * 2,
        [struct((length, width), f32), struct((length, width), bf16)],
        [place_index, layer_input, *out_parts, gain_two],
        prefetch=1,
    )
    *seconds, second_third = tensor_gather(second_own)

    hidden = swish_weight.shape[1]
    anywhere = pl.BlockSpec(memory_space=pl.ANY)

    def feed(rows, grads, at, after=()):
        count = len(rows)
        return grid_call(
            feed_kernel,
            (count,),
            [whole_block] * 2
            + [pl.BlockSpec((length, width), lambda b: (b + at, 0))]
            + [anywhere] * 3,
            [row_spec(hidden)] * 3 + [row_spec(width)] * 2,
            [struct((count * length, hidden), bf16)] * 3 + [struct((count * length, width), bf16)] * 2,
            [rows[0], rows[-1], grads, swish_weight, up_weight, down_weight],
            scratch=[
                pltpu.VMEM((width, hidden), bf16),
                pltpu.VMEM((width, hidden), bf16),
                pltpu.VMEM((hidden, width), bf16),
                pltpu.SemaphoreType.DMA((3,)),
            ],
            after=after,
        )

    feed_near = feed(seconds[:2], grads_near, 0)
    seconds.append(second_third([feed_near[4]]))
    feed_two = feed(seconds[2:3], grads_far, 0, [feed_near[4]])
    feed_three = feed(seconds[3:4], grads_far, 1, [feed_two[4]])
    inner, swish_back, up_back = (
        [(feed_near[k], 0), (feed_near[k], 1), (feed_two[k], 0), (feed_three[k], 0)] for k in range(3)
    )

    bits = bits_of(devices)
    late_bits = [bits[1], bits[0], *bits[2:]]
    second_blocks = [(values, 0) for values in seconds]
    swish_grad = Scatter(second_blocks, [swish_back], bits)
    up_grad = Scatter(second_blocks, [up_back], bits)
    down_grad = Scatter(blocks(grads_near, grads_far), [inner], late_bits, True)
    swish_away = swish_grad.away()
    swish_grad.came[0] = swish_grad.hop(0, swish_away)

    def second_sum(near, far):
        parts, _ = tensor_reduce(near, far)
        down_away = down_grad.away([swish_away])
        return parts[1:], down_away, up_grad.away([down_away])

    second_parts, down_away, up_away = region(
        second_sum, halves(feed_near[3]), (feed_two[3], feed_three[3])
    )
    second_parts = (feed_near[3], *second_parts)
    down_grad.came[0] = down_grad.hop(0, down_away)
    up_grad.came[0] = up_grad.hop(0, up_away)

    middle_grad, own_rows, mlp_norm_part = grid_call(
        middle_back_kernel,
        tiles,
        [own_spec] + [tile_spec] * 4 + [fixed((1, width))],
        [tile_spec, tile_spec, fixed((1, width))],
        [struct((length, width), f32), struct((length, width), bf16), struct((1, width), f32)],
        [place_index, cotangent, *second_parts, middle, gain_two],
        prefetch=1,
    )

    def branch_back(first, second, mixed, gates, queries, run, at, into=None):
        return grid_call(
            branch_back_kernel,
            (half,),
            [
                whole_block, whole_block, fixed((DK, width)), row_spec(DK), row_spec(DK), fixed((1, DK)),
                row_spec(DK), row_spec(DK),
            ],
            [row_spec(DK), row_spec(DK), line(1, DK), chunk_spec(devices, at)],
            [rows_of(DK, bf16), rows_of(DK, bf16), struct((half, 1, DK), f32), chunks],
            [first, second, out_weight, mixed, gates, gain, queries, run],
            into=() if into is None else [(into, 3)],
        )

    first_row = swap(own_rows, "tensor", 1)

    def gather_back(own_rows, first_row):
        second_row = swap(own_rows, "tensor", 2)
        *near, state_back = branch_back(
            own_rows, first_row, mixed_near, gates_near, queries_near, run_near, half
        )
        third_row = swap(hold(second_row, [near[0]]), "tensor", 1)
        *far, state_back = branch_back(
            second_row, third_row, mixed_far, gates_far, queries_far, run_far, 0, state_back
        )
        return second_row, third_row, near, far, state_back

    second_row, third_row, near, far, state_back = region(gather_back, own_rows, first_row)
    rows = [(values, 0) for values in (own_rows, first_row, second_row, third_row)]
    gate_back_near, mixed_back_near, gain_back_near = near
    gate_back_far, mixed_back_far, gain_back_far = far
    norms = blocks(norm_near, norm_far)

    out_grad = Scatter(rows, [blocks(branch_near, branch_far)], bits, True)
    gate_grad = Scatter(norms, [blocks(gate_back_near, gate_back_far)], bits)

    def states_back(state_back):
        swish_one = swish_grad.one([state_back])
        gate_away = gate_grad.away([swish_one])
        return (
            deal(state_back), swish_one, gate_away, out_grad.away([gate_away]),
            tensor_reduce(halves(feed_near[4]), (feed_two[4], feed_three[4]))[0],
        )

    came, swish_one, gate_away, out_away, output_parts = region(states_back, state_back)

    def states_out(came, swish_one, out_away, gate_away, output_parts):
        up_one = up_grad.one([came])
        own = sum((part.astype(f32) for part in output_parts), middle).astype(bf16)
        return (
            deal(carried(came, lines, True)), swish_grad.hop(1, swish_one), out_grad.hop(0, out_away),
            up_one, down_grad.one([up_one]), own, swap(own, "tensor", 2), gate_grad.hop(0, gate_away),
        )

    (
        outgoing, swish_grad.came[1], out_grad.came[0], up_one, down_one, output_own, output_second,
        gate_grad.came[0],
    ) = region(states_out, came, swish_one, out_away, gate_away, output_parts)
    swish_two = swish_grad.two([outgoing])

    def mix_back(queries, keys, values, mixed_back, run, scores, incoming, at, rank_rows, after):
        return grid_call(
            mix_back_kernel,
            (half,),
            [row_spec(DK)] * 5
            + [square(length)]
            + [state_specs[1 if at else 0], chunk_spec(devices, at)]
            + [row_spec(rank), fixed((rank, DK)), fixed((1, DK))],
            [row_spec(DK)] * 3 + [line(rank, length), line(rank, DK), line(1, DK)],
            [rows_of(DK, bf16)] * 3
            + [
                struct((half, rank, length), f32),
                struct((half, rank, DK), f32),
                struct((half, 1, DK), f32),
            ],
            [
                queries, keys, values, mixed_back, run, scores, incoming, outgoing,
                rank_rows, rank_up, bias,
            ],
            after=after,
        )

    def first_part(query_back, key_back, value_back, gate_back, at, into=()):
        tile = 512
        pairs = [
            (query_back, query_weight),
            (key_back, key_weight),
            (value_back, value_weight),
            (gate_back, gate_weight),
        ]
        return grid_call(
            sum_kernel,
            (width // tile,),
            [pl.BlockSpec((half_rows, DK), lambda j: (0, 0))] * 4
            + [pl.BlockSpec((tile, DK), lambda j: (j, 0))] * 4,
            [pl.BlockSpec((1, length, tile), lambda j: (at, 0, j))] * 2,
            [struct((half, length, width), bf16)] * 2,
            [*[p[0] for p in pairs], *[p[1] for p in pairs]],
            into=into,
        )

    def in_order(blocks, after=()):
        whole = pl.BlockSpec((length, width), lambda k, order: (0, 0))
        return grid_call(
            place_kernel,
            (4,),
            [whole] * 4,
            pl.BlockSpec((1, length, width), lambda k, order: (order[k], 0, 0)),
            struct((seq_count, length, width), bf16),
            [order, *blocks],
            prefetch=1,
            after=after,
        )

    def mixed_pair(near, far):
        query_key = Scatter(norms, [blocks(near[0], far[0]), blocks(near[1], far[1])], bits)
        return query_key, Scatter(norms, [blocks(near[2], far[2])], late_bits)

    def mixes_back(up_one, swish_two, down_one, output_own, output_second):
        gate_one = gate_grad.one([swish_two])
        output_pair = swap(jnp.stack([output_own, output_second]), "tensor", 1)
        near = mix_back(
            queries_near, keys_near, values_near, mixed_back_near, run_near, scores_near,
            incoming_near, half, rank_near, [swish_two],
        )
        far = mix_back(
            queries_far, keys_far, values_far, mixed_back_far, run_far, scores_far,
            incoming_far, 0, rank_far, [near[5]],
        )
        query_key, value = mixed_pair(near, far)
        keep, send = first_part(*far[:3], gate_back_far, 1)
        keep, send = first_part(*near[:3], gate_back_near, 0, [(keep, 0), (send, 1)])
        query_key_away = query_key.away([send])
        value_away = value.away([query_key_away])
        return (
            up_grad.hop(1, up_one), swish_grad.hop(2, swish_two), down_grad.hop(1, down_one),
            gate_grad.hop(1, gate_one), near, far, query_key_away, value_away,
            keep, send, out_grad.one([value_away]), output_pair,
        )

    (
        up_grad.came[1], swish_grad.came[2], down_grad.came[1], gate_grad.came[1], near, far, query_key_away,
        value_away, first_keep, first_send, out_one, output_pair,
    ) = region(mixes_back, up_one, swish_two, down_one, output_own, output_second)

    def first_sum(keep, send):
        came = swap(send, "tensor", 1)
        gate_two = gate_grad.two([send])
        down_two = down_grad.two([gate_two])
        return came, (keep[1].astype(f32) + came[1].astype(f32)).astype(bf16), gate_two, down_two

    first_came, first_second, gate_two, down_two = region(first_sum, first_keep, first_send)
    rank_part_near, up_part_near, bias_part_near = near[3:]
    rank_part_far, up_part_far, bias_part_far = far[3:]
    query_key_grad, value_grad = mixed_pair(near, far)

    def third_window(query_key_away, value_away, gate_two, down_two, first_second):
        rank_part = jnp.concatenate([rank_part_near, rank_part_far], axis=0)
        rank_part = lax.all_to_all(jnp.take(rank_part, order, axis=0), "tensor", 0, 0)
        return (
            query_key_grad.hop(0, query_key_away), value_grad.hop(0, value_away),
            gate_grad.hop(2, gate_two), down_grad.hop(2, down_two), up_grad.two(),
            swish_grad.last(), jnp.sum(rank_part, axis=0).astype(bf16), swap(first_second, "tensor", 2),
            in_order([output_own, output_pair[0], output_second, output_pair[1]], [down_two]),
        )

    (
        query_key_grad.came[0], value_grad.came[0], gate_grad.came[2], down_grad.came[2], up_two,
        swish_share, rank_back, first_last, layer_output,
    ) = region(third_window, query_key_away, value_away, gate_two, down_two, first_second)
    query_key_one = query_key_grad.one()
    value_one = value_grad.one([query_key_one])

    rank_down_part = contract(rank_back, norm_near[:length], 1, 0)
    own_part = jnp.concatenate([rank_down_part, mlp_norm_part], axis=0)
    shared = jnp.concatenate(
        [
            sum(up_part_near) + sum(up_part_far),
            sum(bias_part_near) + sum(bias_part_far),
            sum(gain_back_near) + sum(gain_back_far),
        ],
        axis=0,
    )
    column = width // devices
    own_part = jnp.moveaxis(own_part.reshape(rank + 1, devices, column), 1, 0)
    own_size = (rank + 1) * column
    mail = jnp.concatenate(
        [
            own_part.reshape(devices, own_size),
            jnp.broadcast_to(shared.reshape(1, -1), (devices, shared.size)),
        ],
        axis=1,
    )

    def summed(mail):
        mail = mail.reshape(devices, 1, -1).astype(bf16)
        return jnp.sum(lax.all_to_all(mail, "seq", 0, 0).astype(f32), axis=0)

    def fourth_window(query_key_one, value_one, up_two, out_one, mail):
        return (
            query_key_grad.hop(1, query_key_one), value_grad.hop(1, value_one), up_grad.hop(2, up_two),
            out_grad.hop(1, out_one), gate_grad.last(), down_grad.last(), summed(mail),
        )

    (
        query_key_grad.came[1], value_grad.came[1], up_grad.came[2], out_grad.came[1], gate_share, down_share,
        mail,
    ) = region(fourth_window, query_key_one, value_one, up_two, out_one, mail)

    input_rows, attn_norm_part = grid_call(
        input_back_kernel,
        tiles,
        [own_spec]
        + [pl.BlockSpec((1, tile, width), lambda b, *_: (0, b, 0))] * 2
        + [
            tile_spec,
            pl.BlockSpec((rank, tile), lambda b, *_: (0, b)), fixed((width, rank)), tile_spec,
            fixed((1, width)),
        ],
        [tile_spec, fixed((1, width))],
        [struct((length, width), bf16), struct((1, width), f32)],
        [
            place_index, layer_input, first_keep, first_came, first_last, rank_back, rank_down, middle_grad,
            attn_norm.reshape(1, width),
        ],
        prefetch=1,
        after=[gate_share],
    )
    out_two = out_grad.two([input_rows])
    query_key_two = query_key_grad.two([out_two])
    value_two = value_grad.two([query_key_two])

    def fifth_window(input_rows, query_key_two, value_two, out_two, attn_norm_part):
        return (
            swap(input_rows, "tensor", 2), query_key_grad.hop(2, query_key_two),
            value_grad.hop(2, value_two), out_grad.hop(2, out_two),
            summed(attn_norm_part), up_grad.last(),
        )

    (
        second_rows, query_key_grad.came[2], value_grad.came[2], out_grad.came[2],
        attn_norm_part, up_share,
    ) = region(fifth_window, input_rows, query_key_two, value_two, out_two, attn_norm_part)

    def sixth_window(input_rows, second_rows, mail, attn_norm_part):
        first_rows = swap(input_rows, "tensor", 1)
        third_rows = swap(second_rows, "tensor", 1)
        parts = jnp.concatenate([mail.reshape(-1)[:own_size], attn_norm_part.reshape(-1)])
        return (
            in_order([input_rows, first_rows, second_rows, third_rows]), query_key_grad.last(),
            value_grad.last(), out_grad.last(),
            sum_over(parts.reshape(rank + 2, column), "tensor"),
        )

    input_grad, query_key_share, value_share, out_share, own_part = region(
        sixth_window, input_rows, second_rows, mail, attn_norm_part
    )
    shared = mail.reshape(-1)[own_size:].reshape(rank + 2, DK)
    return (
        layer_output,
        input_grad,
        own_part[rank + 1],
        query_key_share[:, :DK],
        query_key_share[:, DK:],
        value_share,
        gate_share,
        own_part[:rank].T,
        shared[:rank],
        shared[rank],
        shared[rank + 1],
        out_share,
        own_part[rank],
        swish_share,
        up_share,
        down_share,
    )


def solution(mesh):
    return jax.shard_map(
        local,
        mesh=mesh,
        in_specs=(
            P(None, "seq", None),
            P(),
            P(None, "tensor"),
            P(None, "tensor"),
            P(None, "tensor"),
            P(None, "tensor"),
            P(),
            P(None, "tensor"),
            P("tensor"),
            P("tensor"),
            P("tensor", None),
            P(),
            P(None, "tensor"),
            P(None, "tensor"),
            P("tensor", None),
            P(None, "seq", None),
        ),
        out_specs=(
            P(None, "seq", None),
            P(None, "seq", None),
            P("seq"),
            P("seq", "tensor"),
            P("seq", "tensor"),
            P("seq", "tensor"),
            P("seq", "tensor"),
            P("seq", None),
            P(None, "tensor"),
            P("tensor"),
            P("tensor"),
            P("tensor", "seq"),
            P("seq"),
            P("seq", "tensor"),
            P("seq", "tensor"),
            P("tensor", "seq"),
        ),
        check_vma=False,
    )
```

```python
import functools

import jax
import jax.numpy as jnp
from jax import lax
from jax.experimental import pallas as pl
from jax.experimental.pallas import tpu as pltpu
from jax.sharding import PartitionSpec as P

DK = 512
BLOCK = 64
EXTRA = 16
ROWS = 256
COST = 1024
VMEM = 48 * 1024 * 1024

bf16 = jnp.bfloat16
f32 = jnp.float32
highest_precision = lax.Precision.HIGHEST
epsilon = 1e-06


def contract(left, right, left_dim, right_dim, precision=None):
    return lax.dot_general(
        left,
        right,
        (((left_dim,), (right_dim,)), ((), ())),
        preferred_element_type=f32,
        precision=precision,
    )


def product(left, right):
    return contract(left, right, 1, 0)


def across(left, right):
    return contract(left, right, 0, 0)


def against(left, right):
    return contract(left, right, 1, 1)


def forget_logits(rank_ref, up_ref, bias_ref):
    return product(rank_ref[...], up_ref[...]) + bias_ref[...].astype(f32)


def positions(count):
    rows = lax.broadcasted_iota(jnp.int32, (count, count), 0)
    cols = lax.broadcasted_iota(jnp.int32, (count, count), 1)
    return rows, cols


def spread(pieces, size):
    width = pieces[0].shape[1]
    return jnp.concatenate([jnp.broadcast_to(piece, (size, width)) for piece in pieces], axis=0)


def scaled_pair(level, query_scaled, key_rows, run):
    count = run.shape[0]
    if level == 0:
        starts = range(0, count, BLOCK)
        center = spread([run[s + BLOCK // 2 : s + BLOCK // 2 + 1] for s in starts], BLOCK)
        query_factor = jnp.exp(run - center)
        key_factor = jnp.exp(center - run)
        return query_scaled * query_factor, key_rows * key_factor, query_factor, key_factor
    group = BLOCK << level
    half = group // 2
    center = spread([run[s + half - 1 : s + half] for s in range(0, count, group)], group)
    place = lax.broadcasted_iota(jnp.int32, run.shape, 0)
    right = (place % group) >= half
    gap = run - center
    query_factor = jnp.where(right, jnp.exp(jnp.where(right, gap, 0.0)), 0.0)
    key_factor = jnp.where(right, 0.0, jnp.exp(jnp.where(right, 0.0, -gap)))
    return query_scaled * query_factor, key_rows * key_factor, query_factor, key_factor


def level_mask(level, rows, cols):
    if level == 0:
        return (rows // BLOCK == cols // BLOCK) & (cols <= rows)
    group = BLOCK << level
    half = group // 2
    return (rows // group == cols // group) & (rows % group >= half) & (cols % group < half)


def level_count(count):
    levels = 1
    while (BLOCK << (levels - 1)) < count:
        levels += 1
    return levels


def norm_kernel(order_ref, input_ref, grad_ref, gain_ref, norm_ref, rows_ref):
    values = input_ref[0].astype(f32)
    scale = lax.rsqrt(jnp.mean(values * values, axis=-1, keepdims=True) + epsilon)
    norm_ref[...] = (values * scale * gain_ref[...].astype(f32)).astype(bf16)
    rows_ref[...] = grad_ref[0]


def decay_kernel(rank_ref, up_ref, bias_ref, run_ref):
    logits = forget_logits(rank_ref, up_ref, bias_ref)
    decays = (jnp.minimum(logits, 0.0) - jnp.log1p(jnp.exp(-jnp.abs(logits)))) * (1.0 / 16.0)
    rows, cols = positions(decays.shape[0])
    run_ref[...] = contract((cols <= rows).astype(f32), decays, 1, 0, highest_precision)


def total_lines(run):
    return as_lines(run[run.shape[0] - 1 :])


def as_lines(*totals):
    place = lax.broadcasted_iota(jnp.int32, (EXTRA, DK), 0)
    lines = jnp.zeros((EXTRA, DK), f32)
    for first, total in enumerate(totals):
        high = total.astype(bf16)
        rest = total - high.astype(f32)
        middle = rest.astype(bf16)
        low = (rest - middle.astype(f32)).astype(bf16)
        for at, line in enumerate((high, middle, low)):
            lines = jnp.where(place == 3 * first + at, line.astype(f32), lines)
    return lines.astype(bf16)


def from_lines(lines, first=0):
    lines = lines.astype(f32)[3 * first : 3 * first + 3]
    return lines[0:1] + lines[1:2] + lines[2:3]


def state_of(key_ref, value_ref, run):
    left = (key_ref[...].astype(f32) * jnp.exp(run[run.shape[0] - 1 :] - run)).astype(bf16)
    return across(value_ref[...], left).astype(bf16)


def state_kernel(key_ref, value_ref, run_ref, state_ref, lines_ref):
    run = run_ref[...]
    state_ref[0] = state_of(key_ref, value_ref, run)
    lines_ref[0] = total_lines(run)


def cut_state_kernel(me_ref, key_ref, value_ref, run_ref, keep_ref, send_ref, lines_ref, held):
    run = run_ref[...]
    held[...] = state_of(key_ref, value_ref, run).reshape(held.shape)
    lines = total_lines(run)
    y, z = me_ref[0] % 2, me_ref[0] // 2
    for at in range(4):
        keep_ref[0, at] = held[y * 4 + (z ^ at)]
        send_ref[0, at] = held[(1 - y) * 4 + (z ^ at)]
    lines_ref[0] = lines
    send_ref[0, 4, :EXTRA] = lines


def pair_kernel(me_ref, keep_ref, lines_ref, came_ref, first_ref, *part_refs):
    lead = me_ref[0] % 2 == 0
    own, other = from_lines(lines_ref[0]), from_lines(came_ref[0, 4, :EXTRA])
    later = jnp.exp(jnp.where(lead, other, own))
    lines = as_lines(jnp.where(lead, own, other), jnp.where(lead, other, own))
    for at, part_ref in enumerate(part_refs):
        mine, came = keep_ref[0, at].astype(f32), came_ref[0, at].astype(f32)
        first = jnp.where(lead, mine, came)
        first_ref[0, at] = first.astype(bf16)
        rows = first.shape[0]
        part_ref[0, :rows] = (first * later + jnp.where(lead, came, mine)).astype(bf16)
        part_ref[0, rows:] = lines


def chain_kernel(me_ref, *refs):
    part_refs, out_refs, every_ref = refs[:4], refs[4:8], refs[8]
    held, lines, entered = refs[9:]
    z = me_ref[0] // 2
    rows = held.shape[1]
    for at in range(4):
        held[z ^ at] = part_refs[at][0, :rows]
        lines[z ^ at] = part_refs[at][0, rows:]
    carry = jnp.zeros(held.shape[1:], f32)
    for at in range(4):
        entered[at] = carry.astype(bf16)
        totals = from_lines(lines[at]), from_lines(lines[at], 1)
        for y in range(2):
            every_ref[2 * at + y, 0] = as_lines(totals[y])
        carry = carry * jnp.exp(totals[0] + totals[1]) + held[at].astype(f32)
    for at in range(4):
        out_refs[at][0] = entered[z ^ at]


def enter_kernel(me_ref, lines_ref, came_ref, first_ref, *refs):
    *part_refs, whole_ref, send_ref = refs
    y, z = me_ref[0] % 2, me_ref[0] // 2
    lead = y == 0
    earlier = jnp.exp(jnp.where(lead, from_lines(lines_ref[0]), from_lines(came_ref[0, 0, :EXTRA])))
    for at in range(4):
        pair = part_refs[at][0].astype(f32)
        inner = pair * earlier + first_ref[0, at].astype(f32)
        whole_ref[0, 0, z ^ at] = jnp.where(lead, pair, inner).astype(bf16)
        send_ref[0, z ^ at] = jnp.where(lead, inner, pair).astype(bf16)


def join_kernel(me_ref, came_ref, whole_ref):
    whole_ref[0, 0] = came_ref[0]


def score_kernel(query_ref, key_ref, run_ref, score_ref):
    run = run_ref[...]
    query_scaled = query_ref[...].astype(f32) * DK ** (-0.5)
    key_rows = key_ref[...].astype(f32)
    rows, cols = positions(run.shape[0])
    scores = jnp.zeros(rows.shape, f32)
    for level in range(level_count(run.shape[0])):
        left, right, _, _ = scaled_pair(level, query_scaled, key_rows, run)
        scores = jnp.where(
            level_mask(level, rows, cols), against(left.astype(bf16), right.astype(bf16)), scores
        )
    score_ref[0] = scores.astype(bf16)


def whole_state(ref):
    return ref[...].reshape(DK, DK)


def faded_queries(query_ref, run_ref):
    return (query_ref[...].astype(f32) * DK ** (-0.5) * jnp.exp(run_ref[...])).astype(bf16)


def mix_kernel(query_ref, value_ref, run_ref, score_ref, state_ref, gate_ref, gain_ref, mixed_ref, branch_ref):
    faded = faded_queries(query_ref, run_ref)
    mixed = product(score_ref[0], value_ref[...]) + against(faded, whole_state(state_ref))
    mixed_ref[...] = mixed
    scale = lax.rsqrt(jnp.mean(mixed * mixed, axis=-1, keepdims=True) + epsilon)
    gate = gate_ref[...]
    branch_ref[...] = (
        mixed * scale * gain_ref[...].astype(f32) * (gate * jax.nn.sigmoid(gate))
    ).astype(bf16)


def branch_back_kernel(
    first_ref, second_ref, weight_ref, mixed_ref, gate_ref, gain_ref, query_ref, run_ref,
    gate_back_ref, mixed_back_ref, gain_back_ref, state_back_ref,
):
    branch_grad = against(either(first_ref, second_ref), weight_ref[...])
    mixed = mixed_ref[...]
    scale = lax.rsqrt(jnp.mean(mixed * mixed, axis=-1, keepdims=True) + epsilon)
    unit = mixed * scale
    gate = gate_ref[...]
    gain = gain_ref[...].astype(f32)
    sig = jax.nn.sigmoid(gate)
    gate_back_ref[...] = (branch_grad * unit * gain * sig * (1.0 + gate * (1.0 - sig))).astype(bf16)
    shaped_grad = branch_grad * (gate * sig)
    gain_back_ref[0] = jnp.sum(shaped_grad * unit, axis=0, keepdims=True)
    unit_grad = shaped_grad * gain
    mixed_grad = scale * (unit_grad - unit * jnp.mean(unit_grad * unit, axis=-1, keepdims=True))
    mixed_back = mixed_grad.astype(bf16)
    mixed_back_ref[...] = mixed_back
    faded = faded_queries(query_ref, run_ref)
    state_back_ref[...] = across(mixed_back, faded).astype(bf16).reshape(state_back_ref.shape)


def ordered_sum(mask, values):
    high = values.astype(bf16)
    low = (values - high.astype(f32)).astype(bf16)
    ones = mask.astype(f32).astype(bf16)
    return product(ones, high) + product(ones, low)


def mix_back_kernel(
    query_ref, key_ref, value_ref, grad_ref, run_ref, score_ref, state_ref, state_back_ref,
    rank_ref, up_ref, bias_ref,
    query_back_ref, key_back_ref, value_back_ref, rank_back_ref, up_back_ref, bias_back_ref,
):
    run = run_ref[...]
    count = run.shape[0]
    query_scaled = query_ref[...].astype(f32) * DK ** (-0.5)
    key_rows = key_ref[...].astype(f32)
    values = value_ref[...]
    grads = grad_ref[...]
    state = whole_state(state_ref)
    state_back = whole_state(state_back_ref)
    rows, cols = positions(count)
    pairs = against(grads, values)

    closing = run[count - 1 : count]
    fade_in = jnp.exp(run)
    fade_out = jnp.exp(closing - run)
    kept = (key_rows * fade_out).astype(bf16)
    value_back_ref[...] = (across(score_ref[0], grads) + against(kept, state_back)).astype(bf16)

    from_state = product(grads, state)
    to_state = product(values, state_back)
    query_back = fade_in * from_state
    key_back = fade_out * to_state
    decay_back = jnp.exp(closing) * jnp.sum(
        state.astype(f32) * state_back.astype(f32), axis=0, keepdims=True
    )
    decay_back = decay_back + ordered_sum(cols >= rows, query_scaled * fade_in * from_state)
    decay_back = decay_back + ordered_sum(cols < rows, key_rows * fade_out * to_state)
    for level in range(level_count(count)):
        left, right, query_factor, key_factor = scaled_pair(level, query_scaled, key_rows, run)
        left, right = left.astype(bf16), right.astype(bf16)
        here = jnp.where(level_mask(level, rows, cols), pairs, 0.0).astype(bf16)
        to_query = product(here, right)
        to_key = across(here, left)
        query_back = query_back + query_factor * to_query
        key_back = key_back + key_factor * to_key
        left_part = left.astype(f32) * to_query
        right_part = right.astype(f32) * to_key
        if level == 0:
            mask = (rows // BLOCK == cols // BLOCK) & (cols >= rows)
            decay_back = decay_back + ordered_sum(mask, left_part - right_part)
        else:
            group = BLOCK << level
            half = group // 2
            same = rows // group == cols // group
            late = same & (rows % group >= half) & (cols >= rows)
            early = same & (rows % group < half) & (cols < rows)
            decay_back = decay_back + ordered_sum(late | early, left_part + right_part)
    query_back_ref[...] = (query_back * DK ** (-0.5)).astype(bf16)
    key_back_ref[...] = key_back.astype(bf16)
    logits = forget_logits(rank_ref, up_ref, bias_ref)
    logit_back = (decay_back * jax.nn.sigmoid(-logits) * (1.0 / 16.0)).astype(bf16)
    rank_back_ref[0] = against(up_ref[...], logit_back)
    up_back_ref[0] = across(rank_ref[...], logit_back)
    bias_back_ref[0] = jnp.sum(logit_back.astype(f32), axis=0, keepdims=True)


def prefix_kernel(reverse, lines_ref, parts_ref, out_ref):
    count = parts_ref.shape[0]
    rows = out_ref.shape[2]
    carry = jnp.zeros(out_ref.shape[2:], f32)
    for step in range(count):
        at = count - 1 - step if reverse else step
        out_ref[at, 0] = carry.astype(bf16)
        total = from_lines(lines_ref[at, 0])
        carry = carry * jnp.exp(total) + parts_ref[at, 0].astype(f32)


def hold_kernel(values_ref, out_ref):
    out_ref[...] = values_ref[...]


def either(first_ref, second_ref):
    return jnp.where(pl.program_id(0) == 0, first_ref[...], second_ref[...])


def middle_kernel(place_ref, input_ref, own_ref, first_ref, last_ref, gain_ref, middle_ref, second_ref):
    middle = input_ref[0].astype(f32) + (
        own_ref[...].astype(f32) + first_ref[...].astype(f32) + last_ref[...].astype(f32)
    )
    middle_ref[...] = middle
    scale = lax.rsqrt(jnp.mean(middle * middle, axis=-1, keepdims=True) + epsilon)
    second_ref[...] = (middle * scale * gain_ref[...].astype(f32)).astype(bf16)


def norm_back(values, grad, gain):
    scale = lax.rsqrt(jnp.mean(values * values, axis=-1, keepdims=True) + epsilon)
    unit = values * scale
    scaled = grad * gain
    back = scale * (scaled - unit * jnp.mean(scaled * unit, axis=-1, keepdims=True))
    return back, jnp.sum(grad * unit, axis=0, keepdims=True)


def add_part(out_ref, part):
    @pl.when(pl.program_id(0) == 0)
    def _():
        out_ref[...] = part

    @pl.when(pl.program_id(0) != 0)
    def _():
        out_ref[...] += part


def middle_back_kernel(
    place_ref, grad_ref, own_ref, first_ref, last_ref, middle_ref, gain_ref, back_ref, rows_ref, part_ref
):
    grad = own_ref[...].astype(f32) + first_ref[...].astype(f32) + last_ref[...].astype(f32)
    back, part = norm_back(middle_ref[...], grad, gain_ref[...].astype(f32))
    back = grad_ref[0].astype(f32) + back
    back_ref[...] = back
    rows_ref[...] = back.astype(bf16)
    add_part(part_ref, part)


def input_back_kernel(
    place_ref, input_ref, own_ref, first_ref, last_ref, rank_ref, down_ref, middle_ref, gain_ref, rows_ref, part_ref
):
    grad = own_ref[0].astype(f32) + first_ref[0].astype(f32) + last_ref[...].astype(f32)
    grad = grad + contract(rank_ref[...], down_ref[...], 0, 1)
    back, part = norm_back(input_ref[0].astype(f32), grad, gain_ref[...].astype(f32))
    rows_ref[...] = (middle_ref[...] + back).astype(bf16)
    add_part(part_ref, part)


def feed_kernel(
    first_ref, second_ref, grads_ref, swish_ref, up_ref, down_ref,
    inner_ref, swish_back_ref, up_back_ref, second_back_ref, out_ref,
    swish_held, up_held, down_held, semaphores,
):
    copies = [
        pltpu.make_async_copy(swish_ref, swish_held, semaphores.at[0]),
        pltpu.make_async_copy(up_ref, up_held, semaphores.at[1]),
        pltpu.make_async_copy(down_ref, down_held, semaphores.at[2]),
    ]
    start = pl.program_id(0) == 0

    @pl.when(start)
    def _():
        for copy in copies:
            copy.start()

    rows = either(first_ref, second_ref)

    @pl.when(start)
    def _():
        copies[0].wait()

    swish = product(rows, swish_held[...])

    @pl.when(start)
    def _():
        copies[1].wait()

    up = product(rows, up_held[...])
    sig = jax.nn.sigmoid(swish)
    act = swish * sig
    inner = (act * up).astype(bf16)
    inner_ref[...] = inner

    @pl.when(start)
    def _():
        copies[2].wait()

    inner_grad = against(grads_ref[...], down_held[...])
    swish_back = (inner_grad * up * sig * (1.0 + swish * (1.0 - sig))).astype(bf16)
    up_back = (inner_grad * act).astype(bf16)
    swish_back_ref[...] = swish_back
    up_back_ref[...] = up_back
    second_back_ref[...] = (against(swish_back, swish_held[...]) + against(up_back, up_held[...])).astype(bf16)
    out_ref[...] = product(inner, down_held[...]).astype(bf16)


def place_kernel(order_ref, *refs):
    out_ref = refs[-1]
    step = pl.program_id(0)
    for k in range(4):

        @pl.when(step == k)
        def _():
            out_ref[0] = refs[k][...]


def sum_kernel(*refs):
    *refs, keep_ref, send_ref = refs
    count = len(refs) // 2
    rows = keep_ref.shape[1]
    total = against(refs[0][...], refs[count][...])
    for k in range(1, count):
        total = total + against(refs[k][...], refs[count + k][...])
    total = total.astype(bf16)
    keep_ref[0] = total[:rows]
    send_ref[0] = total[rows:]


def grad_kernel(parts, groups, cut_groups, turned, pick_ref, *refs):
    cuts, refs = refs[: parts * cut_groups], refs[parts * cut_groups :]
    others, refs = refs[: parts * groups], refs[parts * groups :]
    arrived, out_ref = refs[:-1], refs[-1]
    for group in range(groups):
        total = None
        members = others[group * parts : (group + 1) * parts]
        width = members[0].shape[1]
        columns = slice(group * width, (group + 1) * width)
        first = group * parts if cut_groups > 1 else 0
        for cut, other in zip(cuts[first : first + parts], members):
            part = across(cut[...], other[...])
            total = part if total is None else total + part
        for ref in arrived:
            total = total + ref[0, :, columns].astype(f32)
        if turned:
            out_ref[...] = total.T
        else:
            out_ref[0, :, columns] = total.astype(out_ref.dtype)


def struct(shape, dtype):
    return jax.ShapeDtypeStruct(shape, dtype)


def grid_call(kernel, grid, in_specs, out_specs, out_shape, args, prefetch=0, after=(), scratch=(), into=()):
    first, last = len(args), len(args) + len(after)
    aliases = {}
    for array, at in into:
        aliases[last] = at
        after = (*after, array)
        last += 1

    def run(*refs):
        kernel(*refs[:first], *refs[last:])

    return pl.pallas_call(
        run,
        grid_spec=pltpu.PrefetchScalarGridSpec(
            num_scalar_prefetch=prefetch,
            grid=grid,
            in_specs=list(in_specs) + [pl.BlockSpec(memory_space=pl.ANY)] * len(after),
            out_specs=out_specs,
            scratch_shapes=list(scratch),
        ),
        out_shape=out_shape,
        input_output_aliases=aliases,
        compiler_params=pltpu.CompilerParams(vmem_limit_bytes=VMEM),
        cost_estimate=pl.CostEstimate(flops=COST, bytes_accessed=COST, transcendentals=0),
    )(*args, *after)


def swap(values, axis, distance):
    count = lax.axis_size(axis)
    return lax.ppermute(values, axis, [(i, i ^ distance) for i in range(count)])


def region(function, *args):
    shapes = jax.eval_shape(function, *args)

    def never(*_):
        return jax.tree.map(lambda a: jnp.zeros(a.shape, a.dtype), shapes)

    return lax.cond(lax.axis_index("seq") >= 0, function, never, *args)


def bits_of(count):
    return [1 << k for k in range(count.bit_length() - 1)]


def hold(values, after):
    spec = pl.BlockSpec(values.shape, lambda: (0,) * values.ndim)
    return grid_call(hold_kernel, (), [spec], spec, struct(values.shape, values.dtype), [values], after=after)


def chunk_spec(count, first=0):
    return pl.BlockSpec((count, 1, DK // count, DK), lambda b, *_: (0, b + first, 0, 0))


def carried(pieces, lines, reverse, after=()):
    count, seq_count, share, _ = pieces.shape
    return grid_call(
        functools.partial(prefix_kernel, reverse),
        (seq_count,),
        [pl.BlockSpec((count, 1, EXTRA, DK), lambda b: (0, b, 0, 0)), chunk_spec(count)],
        chunk_spec(count),
        struct((count, seq_count, share, DK), bf16),
        [lines, pieces],
        after=after,
    )


def deal(pieces):
    return lax.all_to_all(pieces, "seq", 0, 0)


def tensor_reduce(near, far):
    third = swap(far[1], "tensor", 1)
    second = (far[0].astype(f32) + third.astype(f32)).astype(bf16)
    first = swap(near[1], "tensor", 1)
    return (near[0], first, swap(second, "tensor", 2)), second


def tensor_gather(own):
    first = swap(own, "tensor", 1)
    second = swap(own, "tensor", 2)

    def third(after):
        return swap(hold(second, after) if after else second, "tensor", 1)

    return own, first, second, third


def grad_part(cuts, groups, picks, arrived, dtype, turned=False, after=()):
    rows = ROWS
    width = groups[0][0][0].shape[1]
    whole = width * len(groups)
    parts = len(groups[0])
    cut_groups = len(cuts)
    cuts = [block for group in cuts for block in group]
    share = cuts[0][0].shape[1] // lax.axis_size("seq")
    chunks = len(picks)
    me = lax.axis_index("seq")
    index = jnp.stack([me ^ r for r in picks]).astype(jnp.int32)
    others = [block for group in groups for block in group]
    in_specs = [pl.BlockSpec((rows, share), lambda k, pick, at=at: (at, pick[k])) for _, at in cuts]
    in_specs += [pl.BlockSpec((rows, width), lambda k, pick, at=at: (at, 0)) for _, at in others]
    for _, first in arrived:
        in_specs.append(pl.BlockSpec((1, share, whole), lambda k, pick, first=first: (k + first, 0, 0)))
    if turned:
        out_spec = pl.BlockSpec((whole, share), lambda k, pick: (0, 0))
        shape = (whole, share)
    else:
        out_spec = pl.BlockSpec((1, share, whole), lambda k, pick: (k, 0, 0))
        shape = (chunks, share, whole)
    return grid_call(
        functools.partial(grad_kernel, parts, len(groups), cut_groups, turned),
        (chunks,),
        in_specs,
        out_spec,
        struct(shape, dtype),
        [index, *[a for a, _ in cuts], *[a for a, _ in others], *[a for a, _ in arrived]],
        prefetch=1,
        after=after,
    )


class Scatter:
    def __init__(self, cuts, groups, order, turned=False):
        cuts = cuts if isinstance(cuts[0], list) else [cuts]
        self.cuts, self.groups, self.order, self.turned = cuts, groups, order, turned
        self.split = lax.axis_size("seq") == 8
        self.came = [None] * 3

    def part(self, picks, arrived, dtype, turned=False, after=()):
        return grad_part(self.cuts, self.groups, picks, arrived, dtype, turned, after)

    def hop(self, at, part):
        if self.split:
            return swap(part, "seq", self.order[at])
        return part if at else lax.psum_scatter(part, "seq", scatter_dimension=0, tiled=True)

    def whole(self):
        return jnp.concatenate(
            [
                sum(
                    across(a[i * ROWS : (i + 1) * ROWS], b[j * ROWS : (j + 1) * ROWS])
                    for (a, i), (b, j) in zip(cuts, group)
                ).astype(bf16)
                for cuts, group in zip(
                    self.cuts if len(self.cuts) > 1 else self.cuts * len(self.groups), self.groups
                )
            ],
            axis=1,
        )

    def away(self, after=()):
        if not self.split:
            return self.whole()
        a, b, c = self.order
        return self.part([a ^ b, a ^ b ^ c, a ^ c, a], [], bf16, after=after)

    def away_halves(self, after=()):
        if not self.split:
            return self.whole(), jnp.zeros((8, 128), bf16)
        a, b, c = self.order
        front = self.part([a ^ b, a ^ b ^ c], [], bf16, after=after)
        return front, self.part([a ^ c, a], [], bf16, after=[front])

    def hop_rest(self, part):
        return swap(part, "seq", self.order[0]) if self.split else part

    def arrived(self, at):
        came = self.came[0]
        if not isinstance(came, tuple):
            return came, at
        return (came[0], at) if at < 2 else (came[1], at - 2)

    def one(self, after=()):
        if not self.split:
            return self.arrived(0)[0]
        a, b, c = self.order
        return self.part([b, b ^ c], [self.arrived(0)], bf16, after=after)

    def two(self, after=()):
        if not self.split:
            return self.arrived(0)[0]
        c = self.order[2]
        return self.part([c], [self.arrived(2), (self.came[1], 1)], bf16, after=after)

    def last(self, after=()):
        if not self.split:
            total = self.arrived(0)[0].astype(f32)
            return total.T if self.turned else total
        arrived = [self.arrived(3), (self.came[1], 0), (self.came[2], 0)]
        total = self.part([0], arrived, f32, self.turned, after=after)
        return total if self.turned else total[0]


def sum_over(values, axis):
    for bit in bits_of(lax.axis_size(axis)):
        values = values + swap(values, axis, bit)
    return values


def local(
    layer_input,
    attn_norm,
    query_weight,
    key_weight,
    value_weight,
    gate_weight,
    rank_down,
    rank_up,
    decay_bias,
    head_gain,
    out_weight,
    mlp_norm,
    swish_weight,
    up_weight,
    down_weight,
    cotangent,
):
    seq_count, length, width = layer_input.shape
    place = lax.axis_index("tensor")
    devices = lax.axis_size("seq")
    half = seq_count // 2
    half_rows = half * length
    rank = rank_down.shape[1]
    bias = decay_bias.reshape(1, DK)
    gain = head_gain.reshape(1, DK)
    share = DK // devices

    def row_spec(size):
        return pl.BlockSpec((length, size), lambda b, *_: (b, 0))

    def fixed(shape):
        return pl.BlockSpec(shape, lambda b, *_: (0,) * len(shape))

    def square(size):
        return pl.BlockSpec((1, size, size), lambda b, *_: (b, 0, 0))

    def line(rows, size):
        return pl.BlockSpec((1, rows, size), lambda b, *_: (b, 0, 0))

    def rows_of(size, dtype):
        return struct((half_rows, size), dtype)

    chunks = struct((devices, seq_count, share, DK), bf16)
    whole_block = pl.BlockSpec((length, width), lambda b, *_: (0, 0))

    def blocks(near, far):
        return [(near, 0), (near, 1), (far, 0), (far, 1)]

    def halves(values):
        return values[:length], values[length:]

    def first_rows(order, after=()):
        spec = pl.BlockSpec((1, length, width), lambda b, order: (order[b], 0, 0))
        return grid_call(
            norm_kernel,
            (half,),
            [spec, spec, fixed((1, width))],
            [row_spec(width), row_spec(width)],
            [rows_of(width, bf16), rows_of(width, bf16)],
            [order, layer_input, cotangent, attn_norm.reshape(1, width)],
            prefetch=1,
            after=after,
        )

    def decays(norm):
        rank_rows = product(norm, rank_down).astype(bf16)
        run = grid_call(
            decay_kernel,
            (half,),
            [row_spec(rank), fixed((rank, DK)), fixed((1, DK))],
            row_spec(DK),
            rows_of(DK, f32),
            [rank_rows, rank_up, bias],
        )
        return rank_rows, run

    quarter = DK // 8
    me = lax.axis_index("seq").astype(jnp.int32).reshape(1)

    def quarters(count, size=quarter):
        return pl.BlockSpec((1, count, size, DK), lambda b, *_: (b, 0, 0, 0))

    def states(norm, run, after=()):
        keys = product(norm, key_weight).astype(bf16)
        values = product(norm, value_weight).astype(bf16)
        lines = struct((half, EXTRA, DK), bf16)
        if devices != 8:
            parts = grid_call(
                state_kernel,
                (half,),
                [row_spec(DK)] * 3,
                [square(DK), line(EXTRA, DK)],
                [struct((half, DK, DK), bf16), lines],
                [keys, values, run],
                after=after,
            )
        else:
            parts = grid_call(
                cut_state_kernel,
                (half,),
                [row_spec(DK)] * 3,
                [quarters(4), quarters(5), line(EXTRA, DK)],
                [struct((half, 4, quarter, DK), bf16), struct((half, 5, quarter, DK), bf16), lines],
                [me, keys, values, run],
                prefetch=1,
                after=after,
                scratch=[pltpu.VMEM((8, quarter, DK), bf16)],
            )
        return keys, values, parts

    def pairs(parts, came, after=()):
        keep, _, lines = parts
        return grid_call(
            pair_kernel,
            (half,),
            [quarters(4), line(EXTRA, DK), quarters(5)],
            [quarters(4)] + [line(quarter + EXTRA, DK)] * 4,
            [struct((half, 4, quarter, DK), bf16)] + [struct((half, quarter + EXTRA, DK), bf16)] * 4,
            [me, keep, lines, came],
            prefetch=1,
            after=after,
        )

    def chain(own, came, first, after=(), into=()):
        return grid_call(
            chain_kernel,
            (half,),
            [line(quarter + EXTRA, DK)] * 4,
            [line(quarter, DK)] * 4
            + [pl.BlockSpec((8, 1, EXTRA, DK), lambda b, *_: (0, b + first, 0, 0))],
            [struct((half, quarter, DK), bf16)] * 4 + [struct((8, seq_count, EXTRA, DK), bf16)],
            [me, own, *came],
            prefetch=1,
            after=after,
            into=into,
            scratch=[
                pltpu.VMEM((4, quarter, DK), bf16),
                pltpu.VMEM((4, EXTRA, DK), bf16),
                pltpu.VMEM((4, quarter, DK), bf16),
            ],
        )

    def enter(parts, came, first, own, others, after=()):
        return grid_call(
            enter_kernel,
            (half,),
            [line(EXTRA, DK), pl.BlockSpec((1, 1, quarter, DK), lambda b, *_: (b, 4, 0, 0)), quarters(4)]
            + [line(quarter, DK)] * 4,
            [pl.BlockSpec((1, 1, 4, quarter, DK), lambda b, me: (me[0] % 2, b, 0, 0, 0)), quarters(4)],
            [struct((2, half, 4, quarter, DK), bf16), struct((half, 4, quarter, DK), bf16)],
            [me, parts[2], came, first, own, *others],
            prefetch=1,
            after=after,
        )

    def join(whole, came):
        return grid_call(
            join_kernel,
            (half,),
            [quarters(4)],
            pl.BlockSpec((1, 1, 4, quarter, DK), lambda b, me: (1 - me[0] % 2, b, 0, 0, 0)),
            struct(whole.shape, bf16),
            [me, came],
            prefetch=1,
            into=[(whole, 0)],
        )

    def along(parts):
        return [swap(part, "seq", 2 * at) for at, part in enumerate(parts, 1)]

    def scored(norm, keys, run, after=()):
        queries = product(norm, query_weight).astype(bf16)
        gates = product(norm, gate_weight)
        scores = grid_call(
            score_kernel,
            (half,),
            [row_spec(DK)] * 3,
            square(length),
            struct((half, length, length), bf16),
            [queries, keys, run],
            after=after,
        )
        return queries, gates, scores

    def mix(queries, values, run, scores, incoming, at, gates, after=()):
        return grid_call(
            mix_kernel,
            (half,),
            [row_spec(DK)] * 3
            + [square(length), state_specs[at], row_spec(DK), fixed((1, DK))],
            [row_spec(DK), row_spec(DK)],
            [rows_of(DK, f32), rows_of(DK, bf16)],
            [queries, values, run, scores, incoming, gates, gain],
            after=after,
        )

    order = jnp.arange(seq_count, dtype=jnp.int32) ^ place
    place_index = order[:1]
    norm_far, grads_far = first_rows(order[half:])
    rank_far, run_far = decays(norm_far)
    keys_far, values_far, parts_far = states(norm_far, run_far)
    norm_near, grads_near = first_rows(order[:half], [parts_far[1]])
    rank_near, run_near = decays(norm_near)
    keys_near, values_near, parts_near = states(norm_near, run_near)
    queries_far, gates_far, scores_far = scored(norm_far, keys_far, run_far, [parts_near[1]])
    if devices != 8:
        queries_near, gates_near, scores_near = scored(norm_near, keys_near, run_near, [scores_far])
        state = jnp.concatenate([parts_far[0], parts_near[0]], axis=0)
        state = jnp.moveaxis(state.reshape(seq_count, devices, share, DK), 1, 0)
        every_line = jnp.concatenate([parts_far[1], parts_near[1]], axis=0)
        lines = deal(jnp.broadcast_to(every_line[None], (devices, *every_line.shape)))
        incoming = deal(carried(deal(state), lines, False))
        incoming_far = incoming_near = incoming
        state_specs = [chunk_spec(devices, at) for at in (0, half)]
    else:
        came_far = swap(parts_far[1], "seq", 1)
        came_near = swap(parts_near[1], "seq", 1)
        first_far, *pair_far = pairs(parts_far, came_far, [parts_near[1]])
        others_far = along(pair_far[1:])
        first_near, *pair_near = pairs(parts_near, came_near, [pair_far[0], scores_far])
        others_near = along(pair_near[1:])
        *chain_far, lines = chain(pair_far[0], others_far, 0, [pair_near[0]])
        back_far = along(chain_far[1:])
        queries_near, gates_near, scores_near = scored(norm_near, keys_near, run_near, [chain_far[0]])
        *chain_near, lines = chain(pair_near[0], others_near, half, [chain_far[0]], [(lines, 4)])
        back_near = along(chain_near[1:])
        whole_far, send_far = enter(parts_far, came_far, first_far, chain_far[0], back_far, [chain_near[0]])
        half_far = swap(send_far, "seq", 1)
        whole_near, send_near = enter(
            parts_near, came_near, first_near, chain_near[0], back_near, [send_far, scores_near]
        )
        half_near = swap(send_near, "seq", 1)
        incoming_far = join(whole_far, half_far)
        incoming_near = join(whole_near, half_near)
        state_specs = [
            pl.BlockSpec((2, 1, 4, quarter, DK), lambda b, *_: (0, b, 0, 0, 0)) for at in range(2)
        ]

    mixed_far, branch_far = mix(queries_far, values_far, run_far, scores_far, incoming_far, 0, gates_far)
    out_far = product(branch_far, out_weight).astype(bf16)
    out_third = swap(out_far[length:], "tensor", 1)
    out_second = (out_far[:length].astype(f32) + out_third.astype(f32)).astype(bf16)
    out_last = swap(out_second, "tensor", 2)
    mixed_near, branch_near = mix(
        queries_near, values_near, run_near, scores_near, incoming_near, 1, gates_near, [out_second]
    )
    out_near = product(branch_near, out_weight).astype(bf16)
    out_first = region(lambda values: swap(values[length:], "tensor", 1), out_near)
    out_parts = (out_near[:length], out_first, out_last)

    tile = 128
    tiles = (length // tile,)
    tile_spec = pl.BlockSpec((tile, width), lambda b, *_: (b, 0))
    own_spec = pl.BlockSpec((1, tile, width), lambda b, place: (place[0], b, 0))
    gain_two = mlp_norm.reshape(1, width)
    middle, second_own = grid_call(
        middle_kernel,
        tiles,
        [own_spec] + [tile_spec] * 3 + [fixed((1, width))],
        [tile_spec] * 2,
        [struct((length, width), f32), struct((length, width), bf16)],
        [place_index, layer_input, *out_parts, gain_two],
        prefetch=1,
    )
    *seconds, second_third = tensor_gather(second_own)

    hidden = swish_weight.shape[1]
    anywhere = pl.BlockSpec(memory_space=pl.ANY)

    def feed(rows, grads, at, after=()):
        count = len(rows)
        return grid_call(
            feed_kernel,
            (count,),
            [whole_block] * 2
            + [pl.BlockSpec((length, width), lambda b: (b + at, 0))]
            + [anywhere] * 3,
            [row_spec(hidden)] * 3 + [row_spec(width)] * 2,
            [struct((count * length, hidden), bf16)] * 3 + [struct((count * length, width), bf16)] * 2,
            [rows[0], rows[-1], grads, swish_weight, up_weight, down_weight],
            scratch=[
                pltpu.VMEM((width, hidden), bf16),
                pltpu.VMEM((width, hidden), bf16),
                pltpu.VMEM((hidden, width), bf16),
                pltpu.SemaphoreType.DMA((3,)),
            ],
            after=after,
        )

    feed_near = feed(seconds[:2], grads_near, 0)
    seconds.append(second_third([feed_near[4]]))
    feed_two = feed(seconds[2:3], grads_far, 0, [feed_near[4]])
    feed_three = feed(seconds[3:4], grads_far, 1, [feed_two[4]])
    inner, swish_back, up_back = (
        [(feed_near[k], 0), (feed_near[k], 1), (feed_two[k], 0), (feed_three[k], 0)] for k in range(3)
    )

    bits = bits_of(devices)
    late_bits = [bits[1], bits[0], *bits[2:]]
    second_blocks = [(values, 0) for values in seconds]
    swish_grad = Scatter(second_blocks, [swish_back], bits)
    up_grad = Scatter(second_blocks, [up_back], bits)
    down_grad = Scatter(blocks(grads_near, grads_far), [inner], late_bits, True)
    swish_away = swish_grad.away()
    swish_grad.came[0] = swish_grad.hop(0, swish_away)

    def second_sum(near, far):
        parts, _ = tensor_reduce(near, far)
        down_away = down_grad.away([swish_away])
        return parts[1:], down_away, up_grad.away_halves([down_away])

    second_parts, down_away, up_away = region(
        second_sum, halves(feed_near[3]), (feed_two[3], feed_three[3])
    )
    second_parts = (feed_near[3], *second_parts)
    down_grad.came[0] = down_grad.hop(0, down_away)
    up_grad.came[0] = (up_grad.hop(0, up_away[0]), None)

    middle_grad, own_rows, mlp_norm_part = grid_call(
        middle_back_kernel,
        tiles,
        [own_spec] + [tile_spec] * 4 + [fixed((1, width))],
        [tile_spec, tile_spec, fixed((1, width))],
        [struct((length, width), f32), struct((length, width), bf16), struct((1, width), f32)],
        [place_index, cotangent, *second_parts, middle, gain_two],
        prefetch=1,
    )

    def branch_back(first, second, mixed, gates, queries, run, at, into=None):
        return grid_call(
            branch_back_kernel,
            (half,),
            [
                whole_block, whole_block, fixed((DK, width)), row_spec(DK), row_spec(DK), fixed((1, DK)),
                row_spec(DK), row_spec(DK),
            ],
            [row_spec(DK), row_spec(DK), line(1, DK), chunk_spec(devices, at)],
            [rows_of(DK, bf16), rows_of(DK, bf16), struct((half, 1, DK), f32), chunks],
            [first, second, out_weight, mixed, gates, gain, queries, run],
            into=() if into is None else [(into, 3)],
        )

    first_row = swap(own_rows, "tensor", 1)

    def gather_back(own_rows, first_row):
        second_row = swap(own_rows, "tensor", 2)
        *near, state_back = branch_back(
            own_rows, first_row, mixed_near, gates_near, queries_near, run_near, half
        )
        third_row = swap(hold(second_row, [near[0]]), "tensor", 1)
        *far, state_back = branch_back(
            second_row, third_row, mixed_far, gates_far, queries_far, run_far, 0, state_back
        )
        return second_row, third_row, near, far, state_back

    second_row, third_row, near, far, state_back = region(gather_back, own_rows, first_row)
    rows = [(values, 0) for values in (own_rows, first_row, second_row, third_row)]
    gate_back_near, mixed_back_near, gain_back_near = near
    gate_back_far, mixed_back_far, gain_back_far = far
    norms = blocks(norm_near, norm_far)

    far_bits = [bits[0], *bits[2:], bits[1]]
    out_grad = Scatter(rows, [blocks(branch_near, branch_far)], far_bits, True)
    gate_grad = Scatter(norms, [blocks(gate_back_near, gate_back_far)], bits)

    def states_back(state_back):
        swish_one = swish_grad.one([state_back])
        gate_away = gate_grad.away([swish_one])
        return (
            deal(state_back), swish_one, gate_away, out_grad.away([gate_away]),
            tensor_reduce(halves(feed_near[4]), (feed_two[4], feed_three[4]))[0],
        )

    came, swish_one, gate_away, out_away, output_parts = region(states_back, state_back)

    def states_out(came, swish_one, out_away, gate_away, output_parts):
        up_one = up_grad.one([came])
        own = sum((part.astype(f32) for part in output_parts), middle).astype(bf16)
        return (
            deal(carried(came, lines, True)), swish_grad.hop(1, swish_one), out_grad.hop(0, out_away),
            up_one, down_grad.one([up_one]), [own, swap(own, "tensor", 1), swap(own, "tensor", 2)],
            gate_grad.hop(0, gate_away),
        )

    (
        outgoing, swish_grad.came[1], out_grad.came[0], up_one, down_one, output_blocks,
        gate_grad.came[0],
    ) = region(states_out, came, swish_one, out_away, gate_away, output_parts)
    swish_two = swish_grad.two([outgoing])

    def mix_back(queries, keys, values, mixed_back, run, scores, incoming, at, rank_rows, after):
        return grid_call(
            mix_back_kernel,
            (half,),
            [row_spec(DK)] * 5
            + [square(length)]
            + [state_specs[1 if at else 0], chunk_spec(devices, at)]
            + [row_spec(rank), fixed((rank, DK)), fixed((1, DK))],
            [row_spec(DK)] * 3 + [line(rank, length), line(rank, DK), line(1, DK)],
            [rows_of(DK, bf16)] * 3
            + [
                struct((half, rank, length), f32),
                struct((half, rank, DK), f32),
                struct((half, 1, DK), f32),
            ],
            [
                queries, keys, values, mixed_back, run, scores, incoming, outgoing,
                rank_rows, rank_up, bias,
            ],
            after=after,
        )

    def first_part(query_back, key_back, value_back, gate_back, at, into=()):
        tile = 512
        pairs = [
            (query_back, query_weight),
            (key_back, key_weight),
            (value_back, value_weight),
            (gate_back, gate_weight),
        ]
        return grid_call(
            sum_kernel,
            (width // tile,),
            [pl.BlockSpec((half_rows, DK), lambda j: (0, 0))] * 4
            + [pl.BlockSpec((tile, DK), lambda j: (j, 0))] * 4,
            [pl.BlockSpec((1, length, tile), lambda j: (at, 0, j))] * 2,
            [struct((half, length, width), bf16)] * 2,
            [*[p[0] for p in pairs], *[p[1] for p in pairs]],
            into=into,
        )

    def in_order(blocks, after=()):
        whole = pl.BlockSpec((length, width), lambda k, order: (0, 0))
        return grid_call(
            place_kernel,
            (4,),
            [whole] * 4,
            pl.BlockSpec((1, length, width), lambda k, order: (order[k], 0, 0)),
            struct((seq_count, length, width), bf16),
            [order, *blocks],
            prefetch=1,
            after=after,
        )

    def mixed_pair(near, far):
        query_key = Scatter(norms, [blocks(near[0], far[0]), blocks(near[1], far[1])], bits)
        return query_key, Scatter(norms, [blocks(near[2], far[2])], late_bits)

    def mixes_back(up_one, swish_two, down_one):
        gate_one = gate_grad.one([swish_two])
        near = mix_back(
            queries_near, keys_near, values_near, mixed_back_near, run_near, scores_near,
            incoming_near, half, rank_near, [swish_two],
        )
        far = mix_back(
            queries_far, keys_far, values_far, mixed_back_far, run_far, scores_far,
            incoming_far, 0, rank_far, [near[5]],
        )
        query_key, value = mixed_pair(near, far)
        keep, send = first_part(*far[:3], gate_back_far, 1)
        keep, send = first_part(*near[:3], gate_back_near, 0, [(keep, 0), (send, 1)])
        query_key_away = query_key.away([send])
        value_away = value.away([query_key_away])
        return (
            up_grad.hop(1, up_one), swish_grad.hop(2, swish_two), down_grad.hop(1, down_one),
            gate_grad.hop(1, gate_one), near, far, query_key_away, value_away,
            keep, send, up_grad.hop_rest(up_away[1]),
        )

    (
        up_grad.came[1], swish_grad.came[2], down_grad.came[1], gate_grad.came[1], near, far, query_key_away,
        value_away, first_keep, first_send, up_rest,
    ) = region(mixes_back, up_one, swish_two, down_one)
    up_grad.came[0] = (up_grad.came[0][0], up_rest)

    def first_sum(keep, send, output_second):
        came = swap(send, "tensor", 1)
        output_third = swap(output_second, "tensor", 1)
        gate_two = gate_grad.two([send])
        down_two = down_grad.two([gate_two])
        second = (keep[1].astype(f32) + came[1].astype(f32)).astype(bf16)
        return came, second, gate_two, down_two, output_third

    first_came, first_second, gate_two, down_two, output_third = region(
        first_sum, first_keep, first_send, output_blocks[2]
    )
    output_blocks.append(output_third)
    rank_part_near, up_part_near, bias_part_near = near[3:]
    rank_part_far, up_part_far, bias_part_far = far[3:]
    query_key_grad, value_grad = mixed_pair(near, far)

    def third_window(query_key_away, value_away, gate_two, down_two, first_second):
        rank_part = jnp.concatenate([rank_part_near, rank_part_far], axis=0)
        rank_part = lax.all_to_all(jnp.take(rank_part, order, axis=0), "tensor", 0, 0)
        return (
            query_key_grad.hop(0, query_key_away), value_grad.hop(0, value_away),
            gate_grad.hop(2, gate_two), down_grad.hop(2, down_two), up_grad.two(),
            swish_grad.last(), jnp.sum(rank_part, axis=0).astype(bf16), swap(first_second, "tensor", 2),
            out_grad.one([down_two]), in_order(output_blocks, [down_two]),
        )

    (
        query_key_grad.came[0], value_grad.came[0], gate_grad.came[2], down_grad.came[2], up_two,
        swish_share, rank_back, first_last, out_one, layer_output,
    ) = region(third_window, query_key_away, value_away, gate_two, down_two, first_second)
    query_key_one = query_key_grad.one()
    value_one = value_grad.one([query_key_one])

    input_rows, attn_norm_part = grid_call(
        input_back_kernel,
        tiles,
        [own_spec]
        + [pl.BlockSpec((1, tile, width), lambda b, *_: (0, b, 0))] * 2
        + [
            tile_spec,
            pl.BlockSpec((rank, tile), lambda b, *_: (0, b)), fixed((width, rank)), tile_spec,
            fixed((1, width)),
        ],
        [tile_spec, fixed((1, width))],
        [struct((length, width), bf16), struct((1, width), f32)],
        [
            place_index, layer_input, first_keep, first_came, first_last, rank_back, rank_down, middle_grad,
            attn_norm.reshape(1, width),
        ],
        prefetch=1,
        after=[value_one],
    )
    rank_down_part = contract(rank_back, norm_near[:length], 1, 0)
    own_part = jnp.concatenate([rank_down_part, mlp_norm_part, attn_norm_part], axis=0)
    shared = jnp.concatenate(
        [
            sum(up_part_near) + sum(up_part_far),
            sum(bias_part_near) + sum(bias_part_far),
            sum(gain_back_near) + sum(gain_back_far),
        ],
        axis=0,
    )
    column = width // devices
    own_part = jnp.moveaxis(own_part.reshape(rank + 2, devices, column), 1, 0)
    own_size = (rank + 2) * column
    mail = jnp.concatenate(
        [
            own_part.reshape(devices, own_size),
            jnp.broadcast_to(shared.reshape(1, -1), (devices, shared.size)),
        ],
        axis=1,
    )

    def summed(mail):
        mail = mail.reshape(devices, 1, -1).astype(bf16)
        return jnp.sum(lax.all_to_all(mail, "seq", 0, 0).astype(f32), axis=0)

    def fourth_window(query_key_one, value_one, up_two, out_one, input_rows, mail):
        return (
            swap(input_rows, "tensor", 2),
            query_key_grad.hop(1, query_key_one), value_grad.hop(1, value_one), up_grad.hop(2, up_two),
            out_grad.hop(1, out_one), gate_grad.last(), down_grad.last(), summed(mail),
        )

    (
        second_rows, query_key_grad.came[1], value_grad.came[1], up_grad.came[2], out_grad.came[1],
        gate_share, down_share,
        mail,
    ) = region(fourth_window, query_key_one, value_one, up_two, out_one, input_rows, mail)

    out_two = out_grad.two([mail])
    query_key_two = query_key_grad.two([out_two])
    value_two = value_grad.two([query_key_two])

    def fifth_window(query_key_two, value_two, out_two, input_rows, second_rows):
        first_rows, third_rows = swap(input_rows, "tensor", 1), swap(second_rows, "tensor", 1)
        return (
            query_key_grad.hop(2, query_key_two), value_grad.hop(2, value_two), out_grad.hop(2, out_two),
            in_order([input_rows, first_rows, second_rows, third_rows]), up_grad.last(),
        )

    query_key_grad.came[2], value_grad.came[2], out_grad.came[2], input_grad, up_share = region(
        fifth_window, query_key_two, value_two, out_two, input_rows, second_rows
    )

    def sixth_window(mail):
        parts = mail.reshape(-1)[:own_size].reshape(rank + 2, column)
        return query_key_grad.last(), value_grad.last(), out_grad.last(), sum_over(parts, "tensor")

    query_key_share, value_share, out_share, own_part = region(sixth_window, mail)
    shared = mail.reshape(-1)[own_size:].reshape(rank + 2, DK)
    return (
        layer_output,
        input_grad,
        own_part[rank + 1],
        query_key_share[:, :DK],
        query_key_share[:, DK:],
        value_share,
        gate_share,
        own_part[:rank].T,
        shared[:rank],
        shared[rank],
        shared[rank + 1],
        out_share,
        own_part[rank],
        swish_share,
        up_share,
        down_share,
    )


def solution(mesh):
    return jax.shard_map(
        local,
        mesh=mesh,
        in_specs=(
            P(None, "seq", None),
            P(),
            P(None, "tensor"),
            P(None, "tensor"),
            P(None, "tensor"),
            P(None, "tensor"),
            P(),
            P(None, "tensor"),
            P("tensor"),
            P("tensor"),
            P("tensor", None),
            P(),
            P(None, "tensor"),
            P(None, "tensor"),
            P("tensor", None),
            P(None, "seq", None),
        ),
        out_specs=(
            P(None, "seq", None),
            P(None, "seq", None),
            P("seq"),
            P("seq", "tensor"),
            P("seq", "tensor"),
            P("seq", "tensor"),
            P("seq", "tensor"),
            P("seq", None),
            P(None, "tensor"),
            P("tensor"),
            P("tensor"),
            P("tensor", "seq"),
            P("seq"),
            P("seq", "tensor"),
            P("seq", "tensor"),
            P("tensor", "seq"),
        ),
        check_vma=False,
    )
```

```python
import functools

import jax
import jax.numpy as jnp
from jax import lax
from jax.experimental import pallas as pl
from jax.experimental.pallas import tpu as pltpu
from jax.sharding import PartitionSpec as P

DK = 512
BLOCK = 64
EXTRA = 16
ROWS = 256
COST = 1024
VMEM = 48 * 1024 * 1024

bf16 = jnp.bfloat16
f32 = jnp.float32
highest_precision = lax.Precision.HIGHEST
epsilon = 1e-06


def contract(left, right, left_dim, right_dim, precision=None):
    return lax.dot_general(
        left,
        right,
        (((left_dim,), (right_dim,)), ((), ())),
        preferred_element_type=f32,
        precision=precision,
    )


def product(left, right):
    return contract(left, right, 1, 0)


def across(left, right):
    return contract(left, right, 0, 0)


def against(left, right):
    return contract(left, right, 1, 1)


def forget_logits(rank_ref, up_ref, bias_ref):
    return product(rank_ref[...], up_ref[...]) + bias_ref[...].astype(f32)


def positions(count):
    rows = lax.broadcasted_iota(jnp.int32, (count, count), 0)
    cols = lax.broadcasted_iota(jnp.int32, (count, count), 1)
    return rows, cols


def spread(pieces, size):
    width = pieces[0].shape[1]
    return jnp.concatenate([jnp.broadcast_to(piece, (size, width)) for piece in pieces], axis=0)


def scaled_pair(level, query_scaled, key_rows, run):
    count = run.shape[0]
    if level == 0:
        starts = range(0, count, BLOCK)
        center = spread([run[s + BLOCK // 2 : s + BLOCK // 2 + 1] for s in starts], BLOCK)
        query_factor = jnp.exp(run - center)
        key_factor = jnp.exp(center - run)
        return query_scaled * query_factor, key_rows * key_factor, query_factor, key_factor
    group = BLOCK << level
    half = group // 2
    center = spread([run[s + half - 1 : s + half] for s in range(0, count, group)], group)
    place = lax.broadcasted_iota(jnp.int32, run.shape, 0)
    right = (place % group) >= half
    gap = run - center
    query_factor = jnp.where(right, jnp.exp(jnp.where(right, gap, 0.0)), 0.0)
    key_factor = jnp.where(right, 0.0, jnp.exp(jnp.where(right, 0.0, -gap)))
    return query_scaled * query_factor, key_rows * key_factor, query_factor, key_factor


def level_mask(level, rows, cols):
    if level == 0:
        return (rows // BLOCK == cols // BLOCK) & (cols <= rows)
    group = BLOCK << level
    half = group // 2
    return (rows // group == cols // group) & (rows % group >= half) & (cols % group < half)


def level_count(count):
    levels = 1
    while (BLOCK << (levels - 1)) < count:
        levels += 1
    return levels


def norm_kernel(order_ref, input_ref, grad_ref, gain_ref, norm_ref, rows_ref):
    values = input_ref[0].astype(f32)
    scale = lax.rsqrt(jnp.mean(values * values, axis=-1, keepdims=True) + epsilon)
    norm_ref[...] = (values * scale * gain_ref[...].astype(f32)).astype(bf16)
    rows_ref[...] = grad_ref[0]


def decay_kernel(rank_ref, up_ref, bias_ref, run_ref):
    logits = forget_logits(rank_ref, up_ref, bias_ref)
    decays = (jnp.minimum(logits, 0.0) - jnp.log1p(jnp.exp(-jnp.abs(logits)))) * (1.0 / 16.0)
    rows, cols = positions(decays.shape[0])
    run_ref[...] = contract((cols <= rows).astype(f32), decays, 1, 0, highest_precision)


def total_lines(run):
    return as_lines(run[run.shape[0] - 1 :])


def as_lines(*totals):
    place = lax.broadcasted_iota(jnp.int32, (EXTRA, DK), 0)
    lines = jnp.zeros((EXTRA, DK), f32)
    for first, total in enumerate(totals):
        high = total.astype(bf16)
        rest = total - high.astype(f32)
        middle = rest.astype(bf16)
        low = (rest - middle.astype(f32)).astype(bf16)
        for at, line in enumerate((high, middle, low)):
            lines = jnp.where(place == 3 * first + at, line.astype(f32), lines)
    return lines.astype(bf16)


def from_lines(lines, first=0):
    lines = lines.astype(f32)[3 * first : 3 * first + 3]
    return lines[0:1] + lines[1:2] + lines[2:3]


def state_of(key_ref, value_ref, run):
    left = (key_ref[...].astype(f32) * jnp.exp(run[run.shape[0] - 1 :] - run)).astype(bf16)
    return across(value_ref[...], left).astype(bf16)


def state_kernel(key_ref, value_ref, run_ref, state_ref, lines_ref):
    run = run_ref[...]
    state_ref[0] = state_of(key_ref, value_ref, run)
    lines_ref[0] = total_lines(run)


def cut_state_kernel(me_ref, key_ref, value_ref, run_ref, keep_ref, send_ref, lines_ref, held):
    run = run_ref[...]
    held[...] = state_of(key_ref, value_ref, run).reshape(held.shape)
    lines = total_lines(run)
    y, z = me_ref[0] % 2, me_ref[0] // 2
    for at in range(4):
        keep_ref[0, at] = held[y * 4 + (z ^ at)]
        send_ref[0, at] = held[(1 - y) * 4 + (z ^ at)]
    lines_ref[0] = lines
    send_ref[0, 4, :EXTRA] = lines


def pair_kernel(me_ref, keep_ref, lines_ref, came_ref, first_ref, *part_refs):
    lead = me_ref[0] % 2 == 0
    own, other = from_lines(lines_ref[0]), from_lines(came_ref[0, 4, :EXTRA])
    later = jnp.exp(jnp.where(lead, other, own))
    lines = as_lines(jnp.where(lead, own, other), jnp.where(lead, other, own))
    for at, part_ref in enumerate(part_refs):
        mine, came = keep_ref[0, at].astype(f32), came_ref[0, at].astype(f32)
        first = jnp.where(lead, mine, came)
        first_ref[0, at] = first.astype(bf16)
        rows = first.shape[0]
        part_ref[0, :rows] = (first * later + jnp.where(lead, came, mine)).astype(bf16)
        part_ref[0, rows:] = lines


def chain_kernel(me_ref, *refs):
    part_refs, out_refs, every_ref = refs[:4], refs[4:8], refs[8]
    held, lines, entered = refs[9:]
    z = me_ref[0] // 2
    rows = held.shape[1]
    for at in range(4):
        held[z ^ at] = part_refs[at][0, :rows]
        lines[z ^ at] = part_refs[at][0, rows:]
    carry = jnp.zeros(held.shape[1:], f32)
    for at in range(4):
        entered[at] = carry.astype(bf16)
        totals = from_lines(lines[at]), from_lines(lines[at], 1)
        for y in range(2):
            every_ref[2 * at + y, 0] = as_lines(totals[y])
        carry = carry * jnp.exp(totals[0] + totals[1]) + held[at].astype(f32)
    for at in range(4):
        out_refs[at][0] = entered[z ^ at]


def enter_kernel(me_ref, lines_ref, came_ref, first_ref, *refs):
    *part_refs, whole_ref, send_ref = refs
    y, z = me_ref[0] % 2, me_ref[0] // 2
    lead = y == 0
    earlier = jnp.exp(jnp.where(lead, from_lines(lines_ref[0]), from_lines(came_ref[0, 0, :EXTRA])))
    for at in range(4):
        pair = part_refs[at][0].astype(f32)
        inner = pair * earlier + first_ref[0, at].astype(f32)
        whole_ref[0, 0, z ^ at] = jnp.where(lead, pair, inner).astype(bf16)
        send_ref[0, z ^ at] = jnp.where(lead, inner, pair).astype(bf16)


def join_kernel(me_ref, came_ref, whole_ref):
    whole_ref[0, 0] = came_ref[0]


def score_kernel(query_ref, key_ref, run_ref, score_ref):
    run = run_ref[...]
    query_scaled = query_ref[...].astype(f32) * DK ** (-0.5)
    key_rows = key_ref[...].astype(f32)
    rows, cols = positions(run.shape[0])
    scores = jnp.zeros(rows.shape, f32)
    for level in range(level_count(run.shape[0])):
        left, right, _, _ = scaled_pair(level, query_scaled, key_rows, run)
        scores = jnp.where(
            level_mask(level, rows, cols), against(left.astype(bf16), right.astype(bf16)), scores
        )
    score_ref[0] = scores.astype(bf16)


def whole_state(ref):
    return ref[...].reshape(DK, DK)


def faded_queries(query_ref, run_ref):
    return (query_ref[...].astype(f32) * DK ** (-0.5) * jnp.exp(run_ref[...])).astype(bf16)


def mix_kernel(query_ref, value_ref, run_ref, score_ref, state_ref, gate_ref, gain_ref, mixed_ref, branch_ref):
    faded = faded_queries(query_ref, run_ref)
    mixed = product(score_ref[0], value_ref[...]) + against(faded, whole_state(state_ref))
    mixed_ref[...] = mixed
    scale = lax.rsqrt(jnp.mean(mixed * mixed, axis=-1, keepdims=True) + epsilon)
    gate = gate_ref[...]
    branch_ref[...] = (
        mixed * scale * gain_ref[...].astype(f32) * (gate * jax.nn.sigmoid(gate))
    ).astype(bf16)


def branch_back_kernel(
    first_ref, second_ref, weight_ref, mixed_ref, gate_ref, gain_ref, query_ref, run_ref,
    gate_back_ref, mixed_back_ref, gain_back_ref, state_back_ref,
):
    branch_grad = against(either(first_ref, second_ref), weight_ref[...])
    mixed = mixed_ref[...]
    scale = lax.rsqrt(jnp.mean(mixed * mixed, axis=-1, keepdims=True) + epsilon)
    unit = mixed * scale
    gate = gate_ref[...]
    gain = gain_ref[...].astype(f32)
    sig = jax.nn.sigmoid(gate)
    gate_back_ref[...] = (branch_grad * unit * gain * sig * (1.0 + gate * (1.0 - sig))).astype(bf16)
    shaped_grad = branch_grad * (gate * sig)
    gain_back_ref[0] = jnp.sum(shaped_grad * unit, axis=0, keepdims=True)
    unit_grad = shaped_grad * gain
    mixed_grad = scale * (unit_grad - unit * jnp.mean(unit_grad * unit, axis=-1, keepdims=True))
    mixed_back = mixed_grad.astype(bf16)
    mixed_back_ref[...] = mixed_back
    faded = faded_queries(query_ref, run_ref)
    state_back_ref[...] = across(mixed_back, faded).astype(bf16).reshape(state_back_ref.shape)


def ordered_sum(mask, values):
    high = values.astype(bf16)
    low = (values - high.astype(f32)).astype(bf16)
    ones = mask.astype(f32).astype(bf16)
    return product(ones, high) + product(ones, low)


def mix_back_kernel(
    query_ref, key_ref, value_ref, grad_ref, run_ref, score_ref, state_ref, state_back_ref,
    rank_ref, up_ref, bias_ref,
    query_back_ref, key_back_ref, value_back_ref, rank_back_ref, up_back_ref, bias_back_ref,
):
    run = run_ref[...]
    count = run.shape[0]
    query_scaled = query_ref[...].astype(f32) * DK ** (-0.5)
    key_rows = key_ref[...].astype(f32)
    values = value_ref[...]
    grads = grad_ref[...]
    state = whole_state(state_ref)
    state_back = whole_state(state_back_ref)
    rows, cols = positions(count)
    pairs = against(grads, values)

    closing = run[count - 1 : count]
    fade_in = jnp.exp(run)
    fade_out = jnp.exp(closing - run)
    kept = (key_rows * fade_out).astype(bf16)
    value_back_ref[...] = (across(score_ref[0], grads) + against(kept, state_back)).astype(bf16)

    from_state = product(grads, state)
    to_state = product(values, state_back)
    query_back = fade_in * from_state
    key_back = fade_out * to_state
    decay_back = jnp.exp(closing) * jnp.sum(
        state.astype(f32) * state_back.astype(f32), axis=0, keepdims=True
    )
    decay_back = decay_back + ordered_sum(cols >= rows, query_scaled * fade_in * from_state)
    decay_back = decay_back + ordered_sum(cols < rows, key_rows * fade_out * to_state)
    for level in range(level_count(count)):
        left, right, query_factor, key_factor = scaled_pair(level, query_scaled, key_rows, run)
        left, right = left.astype(bf16), right.astype(bf16)
        here = jnp.where(level_mask(level, rows, cols), pairs, 0.0).astype(bf16)
        to_query = product(here, right)
        to_key = across(here, left)
        query_back = query_back + query_factor * to_query
        key_back = key_back + key_factor * to_key
        left_part = left.astype(f32) * to_query
        right_part = right.astype(f32) * to_key
        if level == 0:
            mask = (rows // BLOCK == cols // BLOCK) & (cols >= rows)
            decay_back = decay_back + ordered_sum(mask, left_part - right_part)
        else:
            group = BLOCK << level
            half = group // 2
            same = rows // group == cols // group
            late = same & (rows % group >= half) & (cols >= rows)
            early = same & (rows % group < half) & (cols < rows)
            decay_back = decay_back + ordered_sum(late | early, left_part + right_part)
    query_back_ref[...] = (query_back * DK ** (-0.5)).astype(bf16)
    key_back_ref[...] = key_back.astype(bf16)
    logits = forget_logits(rank_ref, up_ref, bias_ref)
    logit_back = (decay_back * jax.nn.sigmoid(-logits) * (1.0 / 16.0)).astype(bf16)
    rank_back_ref[0] = against(up_ref[...], logit_back)
    up_back_ref[0] = across(rank_ref[...], logit_back)
    bias_back_ref[0] = jnp.sum(logit_back.astype(f32), axis=0, keepdims=True)


def prefix_kernel(reverse, lines_ref, parts_ref, out_ref):
    count = parts_ref.shape[0]
    rows = out_ref.shape[2]
    carry = jnp.zeros(out_ref.shape[2:], f32)
    for step in range(count):
        at = count - 1 - step if reverse else step
        out_ref[at, 0] = carry.astype(bf16)
        total = from_lines(lines_ref[at, 0])
        carry = carry * jnp.exp(total) + parts_ref[at, 0].astype(f32)


def hold_kernel(values_ref, out_ref):
    out_ref[...] = values_ref[...]


def either(first_ref, second_ref):
    return jnp.where(pl.program_id(0) == 0, first_ref[...], second_ref[...])


def middle_kernel(place_ref, input_ref, own_ref, first_ref, last_ref, gain_ref, middle_ref, second_ref):
    middle = input_ref[0].astype(f32) + (
        own_ref[...].astype(f32) + first_ref[...].astype(f32) + last_ref[...].astype(f32)
    )
    middle_ref[...] = middle
    scale = lax.rsqrt(jnp.mean(middle * middle, axis=-1, keepdims=True) + epsilon)
    second_ref[...] = (middle * scale * gain_ref[...].astype(f32)).astype(bf16)


def norm_back(values, grad, gain):
    scale = lax.rsqrt(jnp.mean(values * values, axis=-1, keepdims=True) + epsilon)
    unit = values * scale
    scaled = grad * gain
    back = scale * (scaled - unit * jnp.mean(scaled * unit, axis=-1, keepdims=True))
    return back, jnp.sum(grad * unit, axis=0, keepdims=True)


def add_part(out_ref, part):
    @pl.when(pl.program_id(0) == 0)
    def _():
        out_ref[...] = part

    @pl.when(pl.program_id(0) != 0)
    def _():
        out_ref[...] += part


def middle_back_kernel(
    place_ref, grad_ref, own_ref, first_ref, last_ref, middle_ref, gain_ref, back_ref, rows_ref, part_ref
):
    grad = own_ref[...].astype(f32) + first_ref[...].astype(f32) + last_ref[...].astype(f32)
    back, part = norm_back(middle_ref[...], grad, gain_ref[...].astype(f32))
    back = grad_ref[0].astype(f32) + back
    back_ref[...] = back
    rows_ref[...] = back.astype(bf16)
    add_part(part_ref, part)


def input_back_kernel(
    place_ref, input_ref, own_ref, first_ref, last_ref, rank_ref, down_ref, middle_ref, gain_ref, rows_ref, part_ref
):
    grad = own_ref[0].astype(f32) + first_ref[0].astype(f32) + last_ref[...].astype(f32)
    grad = grad + contract(rank_ref[...], down_ref[...], 0, 1)
    back, part = norm_back(input_ref[0].astype(f32), grad, gain_ref[...].astype(f32))
    rows_ref[...] = (middle_ref[...] + back).astype(bf16)
    add_part(part_ref, part)


def feed_kernel(
    first_ref, second_ref, grads_ref, swish_ref, up_ref, down_ref,
    inner_ref, swish_back_ref, up_back_ref, second_back_ref, out_ref,
    swish_held, up_held, down_held, semaphores,
):
    copies = [
        pltpu.make_async_copy(swish_ref, swish_held, semaphores.at[0]),
        pltpu.make_async_copy(up_ref, up_held, semaphores.at[1]),
        pltpu.make_async_copy(down_ref, down_held, semaphores.at[2]),
    ]
    start = pl.program_id(0) == 0

    @pl.when(start)
    def _():
        for copy in copies:
            copy.start()

    rows = either(first_ref, second_ref)

    @pl.when(start)
    def _():
        copies[0].wait()

    swish = product(rows, swish_held[...])

    @pl.when(start)
    def _():
        copies[1].wait()

    up = product(rows, up_held[...])
    sig = jax.nn.sigmoid(swish)
    act = swish * sig
    inner = (act * up).astype(bf16)
    inner_ref[...] = inner

    @pl.when(start)
    def _():
        copies[2].wait()

    inner_grad = against(grads_ref[...], down_held[...])
    swish_back = (inner_grad * up * sig * (1.0 + swish * (1.0 - sig))).astype(bf16)
    up_back = (inner_grad * act).astype(bf16)
    swish_back_ref[...] = swish_back
    up_back_ref[...] = up_back
    second_back_ref[...] = (against(swish_back, swish_held[...]) + against(up_back, up_held[...])).astype(bf16)
    out_ref[...] = product(inner, down_held[...]).astype(bf16)


def place_kernel(order_ref, *refs):
    out_ref = refs[-1]
    step = pl.program_id(0)
    for k in range(4):

        @pl.when(step == k)
        def _():
            out_ref[0] = refs[k][...]


def sum_kernel(*refs):
    *refs, keep_ref, send_ref = refs
    count = len(refs) // 2
    rows = keep_ref.shape[1]
    total = against(refs[0][...], refs[count][...])
    for k in range(1, count):
        total = total + against(refs[k][...], refs[count + k][...])
    total = total.astype(bf16)
    keep_ref[0] = total[:rows]
    send_ref[0] = total[rows:]


def grad_kernel(parts, groups, cut_groups, turned, pick_ref, *refs):
    cuts, refs = refs[: parts * cut_groups], refs[parts * cut_groups :]
    others, refs = refs[: parts * groups], refs[parts * groups :]
    arrived, out_ref = refs[:-1], refs[-1]
    for group in range(groups):
        total = None
        members = others[group * parts : (group + 1) * parts]
        width = members[0].shape[1]
        columns = slice(group * width, (group + 1) * width)
        first = group * parts if cut_groups > 1 else 0
        for cut, other in zip(cuts[first : first + parts], members):
            part = across(cut[...], other[...])
            total = part if total is None else total + part
        for ref in arrived:
            total = total + ref[0, :, columns].astype(f32)
        if turned:
            out_ref[...] = total.T
        else:
            out_ref[0, :, columns] = total.astype(out_ref.dtype)


def struct(shape, dtype):
    return jax.ShapeDtypeStruct(shape, dtype)


def grid_call(kernel, grid, in_specs, out_specs, out_shape, args, prefetch=0, after=(), scratch=(), into=()):
    first, last = len(args), len(args) + len(after)
    aliases = {}
    for array, at in into:
        aliases[last] = at
        after = (*after, array)
        last += 1

    def run(*refs):
        kernel(*refs[:first], *refs[last:])

    return pl.pallas_call(
        run,
        grid_spec=pltpu.PrefetchScalarGridSpec(
            num_scalar_prefetch=prefetch,
            grid=grid,
            in_specs=list(in_specs) + [pl.BlockSpec(memory_space=pl.ANY)] * len(after),
            out_specs=out_specs,
            scratch_shapes=list(scratch),
        ),
        out_shape=out_shape,
        input_output_aliases=aliases,
        compiler_params=pltpu.CompilerParams(vmem_limit_bytes=VMEM),
        cost_estimate=pl.CostEstimate(flops=COST, bytes_accessed=COST, transcendentals=0),
    )(*args, *after)


def swap(values, axis, distance):
    count = lax.axis_size(axis)
    return lax.ppermute(values, axis, [(i, i ^ distance) for i in range(count)])


def region(function, *args):
    shapes = jax.eval_shape(function, *args)

    def never(*_):
        return jax.tree.map(lambda a: jnp.zeros(a.shape, a.dtype), shapes)

    return lax.cond(lax.axis_index("seq") >= 0, function, never, *args)


def bits_of(count):
    return [1 << k for k in range(count.bit_length() - 1)]


def hold(values, after):
    spec = pl.BlockSpec(values.shape, lambda: (0,) * values.ndim)
    return grid_call(hold_kernel, (), [spec], spec, struct(values.shape, values.dtype), [values], after=after)


def chunk_spec(count, first=0):
    return pl.BlockSpec((count, 1, DK // count, DK), lambda b, *_: (0, b + first, 0, 0))


def carried(pieces, lines, reverse, after=()):
    count, seq_count, share, _ = pieces.shape
    return grid_call(
        functools.partial(prefix_kernel, reverse),
        (seq_count,),
        [pl.BlockSpec((count, 1, EXTRA, DK), lambda b: (0, b, 0, 0)), chunk_spec(count)],
        chunk_spec(count),
        struct((count, seq_count, share, DK), bf16),
        [lines, pieces],
        after=after,
    )


def deal(pieces):
    return lax.all_to_all(pieces, "seq", 0, 0)


def tensor_reduce(near, far):
    third = swap(far[1], "tensor", 1)
    second = (far[0].astype(f32) + third.astype(f32)).astype(bf16)
    first = swap(near[1], "tensor", 1)
    return (near[0], first, swap(second, "tensor", 2)), second


def tensor_gather(own):
    first = swap(own, "tensor", 1)
    second = swap(own, "tensor", 2)

    def third(after):
        return swap(hold(second, after) if after else second, "tensor", 1)

    return own, first, second, third


def grad_part(cuts, groups, picks, arrived, dtype, turned=False, after=()):
    rows = ROWS
    width = groups[0][0][0].shape[1]
    whole = width * len(groups)
    parts = len(groups[0])
    cut_groups = len(cuts)
    cuts = [block for group in cuts for block in group]
    share = cuts[0][0].shape[1] // lax.axis_size("seq")
    chunks = len(picks)
    me = lax.axis_index("seq")
    index = jnp.stack([me ^ r for r in picks]).astype(jnp.int32)
    others = [block for group in groups for block in group]
    in_specs = [pl.BlockSpec((rows, share), lambda k, pick, at=at: (at, pick[k])) for _, at in cuts]
    in_specs += [pl.BlockSpec((rows, width), lambda k, pick, at=at: (at, 0)) for _, at in others]
    for _, first in arrived:
        in_specs.append(pl.BlockSpec((1, share, whole), lambda k, pick, first=first: (k + first, 0, 0)))
    if turned:
        out_spec = pl.BlockSpec((whole, share), lambda k, pick: (0, 0))
        shape = (whole, share)
    else:
        out_spec = pl.BlockSpec((1, share, whole), lambda k, pick: (k, 0, 0))
        shape = (chunks, share, whole)
    return grid_call(
        functools.partial(grad_kernel, parts, len(groups), cut_groups, turned),
        (chunks,),
        in_specs,
        out_spec,
        struct(shape, dtype),
        [index, *[a for a, _ in cuts], *[a for a, _ in others], *[a for a, _ in arrived]],
        prefetch=1,
        after=after,
    )


class Scatter:
    def __init__(self, cuts, groups, order, turned=False):
        cuts = cuts if isinstance(cuts[0], list) else [cuts]
        self.cuts, self.groups, self.order, self.turned = cuts, groups, order, turned
        self.split = lax.axis_size("seq") == 8
        self.came = [None] * 3

    def part(self, picks, arrived, dtype, turned=False, after=()):
        return grad_part(self.cuts, self.groups, picks, arrived, dtype, turned, after)

    def hop(self, at, part):
        if self.split:
            return swap(part, "seq", self.order[at])
        return part if at else lax.psum_scatter(part, "seq", scatter_dimension=0, tiled=True)

    def whole(self):
        return jnp.concatenate(
            [
                sum(
                    across(a[i * ROWS : (i + 1) * ROWS], b[j * ROWS : (j + 1) * ROWS])
                    for (a, i), (b, j) in zip(cuts, group)
                ).astype(bf16)
                for cuts, group in zip(
                    self.cuts if len(self.cuts) > 1 else self.cuts * len(self.groups), self.groups
                )
            ],
            axis=1,
        )

    def away(self, after=()):
        if not self.split:
            return self.whole()
        a, b, c = self.order
        return self.part([a ^ b, a ^ b ^ c, a ^ c, a], [], bf16, after=after)

    def away_halves(self, after=()):
        if not self.split:
            return self.whole(), jnp.zeros((8, 128), bf16)
        a, b, c = self.order
        front = self.part([a ^ b, a ^ b ^ c], [], bf16, after=after)
        return front, self.part([a ^ c, a], [], bf16, after=[front])

    def hop_rest(self, part):
        return swap(part, "seq", self.order[0]) if self.split else part

    def arrived(self, at):
        came = self.came[0]
        if not isinstance(came, tuple):
            return came, at
        return (came[0], at) if at < 2 else (came[1], at - 2)

    def one(self, after=()):
        if not self.split:
            return self.arrived(0)[0]
        a, b, c = self.order
        return self.part([b, b ^ c], [self.arrived(0)], bf16, after=after)

    def two(self, after=()):
        if not self.split:
            return self.arrived(0)[0]
        c = self.order[2]
        return self.part([c], [self.arrived(2), (self.came[1], 1)], bf16, after=after)

    def last(self, after=()):
        if not self.split:
            total = self.arrived(0)[0].astype(f32)
            return total.T if self.turned else total
        arrived = [self.arrived(3), (self.came[1], 0), (self.came[2], 0)]
        total = self.part([0], arrived, f32, self.turned, after=after)
        return total if self.turned else total[0]


def sum_over(values, axis):
    for bit in bits_of(lax.axis_size(axis)):
        values = values + swap(values, axis, bit)
    return values


def local(
    layer_input,
    attn_norm,
    query_weight,
    key_weight,
    value_weight,
    gate_weight,
    rank_down,
    rank_up,
    decay_bias,
    head_gain,
    out_weight,
    mlp_norm,
    swish_weight,
    up_weight,
    down_weight,
    cotangent,
):
    seq_count, length, width = layer_input.shape
    place = lax.axis_index("tensor")
    devices = lax.axis_size("seq")
    half = seq_count // 2
    half_rows = half * length
    rank = rank_down.shape[1]
    bias = decay_bias.reshape(1, DK)
    gain = head_gain.reshape(1, DK)
    share = DK // devices

    def row_spec(size):
        return pl.BlockSpec((length, size), lambda b, *_: (b, 0))

    def fixed(shape):
        return pl.BlockSpec(shape, lambda b, *_: (0,) * len(shape))

    def square(size):
        return pl.BlockSpec((1, size, size), lambda b, *_: (b, 0, 0))

    def line(rows, size):
        return pl.BlockSpec((1, rows, size), lambda b, *_: (b, 0, 0))

    def rows_of(size, dtype):
        return struct((half_rows, size), dtype)

    chunks = struct((devices, seq_count, share, DK), bf16)
    whole_block = pl.BlockSpec((length, width), lambda b, *_: (0, 0))

    def blocks(near, far):
        return [(near, 0), (near, 1), (far, 0), (far, 1)]

    def halves(values):
        return values[:length], values[length:]

    def first_rows(order, after=()):
        spec = pl.BlockSpec((1, length, width), lambda b, order: (order[b], 0, 0))
        return grid_call(
            norm_kernel,
            (half,),
            [spec, spec, fixed((1, width))],
            [row_spec(width), row_spec(width)],
            [rows_of(width, bf16), rows_of(width, bf16)],
            [order, layer_input, cotangent, attn_norm.reshape(1, width)],
            prefetch=1,
            after=after,
        )

    def decays(norm):
        rank_rows = product(norm, rank_down).astype(bf16)
        run = grid_call(
            decay_kernel,
            (half,),
            [row_spec(rank), fixed((rank, DK)), fixed((1, DK))],
            row_spec(DK),
            rows_of(DK, f32),
            [rank_rows, rank_up, bias],
        )
        return rank_rows, run

    quarter = DK // 8
    me = lax.axis_index("seq").astype(jnp.int32).reshape(1)

    def quarters(count, size=quarter):
        return pl.BlockSpec((1, count, size, DK), lambda b, *_: (b, 0, 0, 0))

    def states(norm, run, after=()):
        keys = product(norm, key_weight).astype(bf16)
        values = product(norm, value_weight).astype(bf16)
        lines = struct((half, EXTRA, DK), bf16)
        if devices != 8:
            parts = grid_call(
                state_kernel,
                (half,),
                [row_spec(DK)] * 3,
                [square(DK), line(EXTRA, DK)],
                [struct((half, DK, DK), bf16), lines],
                [keys, values, run],
                after=after,
            )
        else:
            parts = grid_call(
                cut_state_kernel,
                (half,),
                [row_spec(DK)] * 3,
                [quarters(4), quarters(5), line(EXTRA, DK)],
                [struct((half, 4, quarter, DK), bf16), struct((half, 5, quarter, DK), bf16), lines],
                [me, keys, values, run],
                prefetch=1,
                after=after,
                scratch=[pltpu.VMEM((8, quarter, DK), bf16)],
            )
        return keys, values, parts

    def pairs(parts, came, after=()):
        keep, _, lines = parts
        return grid_call(
            pair_kernel,
            (half,),
            [quarters(4), line(EXTRA, DK), quarters(5)],
            [quarters(4)] + [line(quarter + EXTRA, DK)] * 4,
            [struct((half, 4, quarter, DK), bf16)] + [struct((half, quarter + EXTRA, DK), bf16)] * 4,
            [me, keep, lines, came],
            prefetch=1,
            after=after,
        )

    def chain(own, came, first, after=(), into=()):
        return grid_call(
            chain_kernel,
            (half,),
            [line(quarter + EXTRA, DK)] * 4,
            [line(quarter, DK)] * 4
            + [pl.BlockSpec((8, 1, EXTRA, DK), lambda b, *_: (0, b + first, 0, 0))],
            [struct((half, quarter, DK), bf16)] * 4 + [struct((8, seq_count, EXTRA, DK), bf16)],
            [me, own, *came],
            prefetch=1,
            after=after,
            into=into,
            scratch=[
                pltpu.VMEM((4, quarter, DK), bf16),
                pltpu.VMEM((4, EXTRA, DK), bf16),
                pltpu.VMEM((4, quarter, DK), bf16),
            ],
        )

    def enter(parts, came, first, own, others, after=()):
        return grid_call(
            enter_kernel,
            (half,),
            [line(EXTRA, DK), pl.BlockSpec((1, 1, quarter, DK), lambda b, *_: (b, 4, 0, 0)), quarters(4)]
            + [line(quarter, DK)] * 4,
            [pl.BlockSpec((1, 1, 4, quarter, DK), lambda b, me: (me[0] % 2, b, 0, 0, 0)), quarters(4)],
            [struct((2, half, 4, quarter, DK), bf16), struct((half, 4, quarter, DK), bf16)],
            [me, parts[2], came, first, own, *others],
            prefetch=1,
            after=after,
        )

    def join(whole, came):
        return grid_call(
            join_kernel,
            (half,),
            [quarters(4)],
            pl.BlockSpec((1, 1, 4, quarter, DK), lambda b, me: (1 - me[0] % 2, b, 0, 0, 0)),
            struct(whole.shape, bf16),
            [me, came],
            prefetch=1,
            into=[(whole, 0)],
        )

    def along(parts):
        return [swap(part, "seq", 2 * at) for at, part in enumerate(parts, 1)]

    def scored(norm, keys, run, after=()):
        queries = product(norm, query_weight).astype(bf16)
        gates = product(norm, gate_weight)
        scores = grid_call(
            score_kernel,
            (half,),
            [row_spec(DK)] * 3,
            square(length),
            struct((half, length, length), bf16),
            [queries, keys, run],
            after=after,
        )
        return queries, gates, scores

    def mix(queries, values, run, scores, incoming, at, gates, after=()):
        return grid_call(
            mix_kernel,
            (half,),
            [row_spec(DK)] * 3
            + [square(length), state_specs[at], row_spec(DK), fixed((1, DK))],
            [row_spec(DK), row_spec(DK)],
            [rows_of(DK, f32), rows_of(DK, bf16)],
            [queries, values, run, scores, incoming, gates, gain],
            after=after,
        )

    order = jnp.arange(seq_count, dtype=jnp.int32) ^ place
    place_index = order[:1]
    norm_far, grads_far = first_rows(order[half:])
    rank_far, run_far = decays(norm_far)
    keys_far, values_far, parts_far = states(norm_far, run_far)
    norm_near, grads_near = first_rows(order[:half], [parts_far[1]])
    rank_near, run_near = decays(norm_near)
    keys_near, values_near, parts_near = states(norm_near, run_near)
    queries_far, gates_far, scores_far = scored(norm_far, keys_far, run_far, [parts_near[1]])
    if devices != 8:
        queries_near, gates_near, scores_near = scored(norm_near, keys_near, run_near, [scores_far])
        state = jnp.concatenate([parts_far[0], parts_near[0]], axis=0)
        state = jnp.moveaxis(state.reshape(seq_count, devices, share, DK), 1, 0)
        every_line = jnp.concatenate([parts_far[1], parts_near[1]], axis=0)
        lines = deal(jnp.broadcast_to(every_line[None], (devices, *every_line.shape)))
        incoming = deal(carried(deal(state), lines, False))
        incoming_far = incoming_near = incoming
        state_specs = [chunk_spec(devices, at) for at in (0, half)]
    else:
        came_far = swap(parts_far[1], "seq", 1)
        came_near = swap(parts_near[1], "seq", 1)
        first_far, *pair_far = pairs(parts_far, came_far, [parts_near[1]])
        others_far = along(pair_far[1:])
        first_near, *pair_near = pairs(parts_near, came_near, [pair_far[0], scores_far])
        others_near = along(pair_near[1:])
        *chain_far, lines = chain(pair_far[0], others_far, 0, [pair_near[0]])
        back_far = along(chain_far[1:])
        queries_near, gates_near, scores_near = scored(norm_near, keys_near, run_near, [chain_far[0]])
        *chain_near, lines = chain(pair_near[0], others_near, half, [chain_far[0]], [(lines, 4)])
        back_near = along(chain_near[1:])
        whole_far, send_far = enter(parts_far, came_far, first_far, chain_far[0], back_far, [chain_near[0]])
        half_far = swap(send_far, "seq", 1)
        whole_near, send_near = enter(
            parts_near, came_near, first_near, chain_near[0], back_near, [send_far, scores_near]
        )
        half_near = swap(send_near, "seq", 1)
        incoming_far = join(whole_far, half_far)
        incoming_near = join(whole_near, half_near)
        state_specs = [
            pl.BlockSpec((2, 1, 4, quarter, DK), lambda b, *_: (0, b, 0, 0, 0)) for at in range(2)
        ]

    mixed_far, branch_far = mix(queries_far, values_far, run_far, scores_far, incoming_far, 0, gates_far)
    out_far = product(branch_far, out_weight).astype(bf16)
    out_third = swap(out_far[length:], "tensor", 1)
    out_second = (out_far[:length].astype(f32) + out_third.astype(f32)).astype(bf16)
    out_last = swap(out_second, "tensor", 2)
    mixed_near, branch_near = mix(
        queries_near, values_near, run_near, scores_near, incoming_near, 1, gates_near, [out_second]
    )
    out_near = product(branch_near, out_weight).astype(bf16)
    out_first = region(lambda values: swap(values[length:], "tensor", 1), out_near)
    out_parts = (out_near[:length], out_first, out_last)

    tile = 128
    tiles = (length // tile,)
    tile_spec = pl.BlockSpec((tile, width), lambda b, *_: (b, 0))
    own_spec = pl.BlockSpec((1, tile, width), lambda b, place: (place[0], b, 0))
    gain_two = mlp_norm.reshape(1, width)
    middle, second_own = grid_call(
        middle_kernel,
        tiles,
        [own_spec] + [tile_spec] * 3 + [fixed((1, width))],
        [tile_spec] * 2,
        [struct((length, width), f32), struct((length, width), bf16)],
        [place_index, layer_input, *out_parts, gain_two],
        prefetch=1,
    )
    *seconds, second_third = tensor_gather(second_own)

    hidden = swish_weight.shape[1]
    anywhere = pl.BlockSpec(memory_space=pl.ANY)

    def feed(rows, grads, at, after=()):
        count = len(rows)
        return grid_call(
            feed_kernel,
            (count,),
            [whole_block] * 2
            + [pl.BlockSpec((length, width), lambda b: (b + at, 0))]
            + [anywhere] * 3,
            [row_spec(hidden)] * 3 + [row_spec(width)] * 2,
            [struct((count * length, hidden), bf16)] * 3 + [struct((count * length, width), bf16)] * 2,
            [rows[0], rows[-1], grads, swish_weight, up_weight, down_weight],
            scratch=[
                pltpu.VMEM((width, hidden), bf16),
                pltpu.VMEM((width, hidden), bf16),
                pltpu.VMEM((hidden, width), bf16),
                pltpu.SemaphoreType.DMA((3,)),
            ],
            after=after,
        )

    feed_near = feed(seconds[:2], grads_near, 0)
    seconds.append(second_third([feed_near[4]]))
    feed_two = feed(seconds[2:3], grads_far, 0, [feed_near[4]])
    feed_three = feed(seconds[3:4], grads_far, 1, [feed_two[4]])
    inner, swish_back, up_back = (
        [(feed_near[k], 0), (feed_near[k], 1), (feed_two[k], 0), (feed_three[k], 0)] for k in range(3)
    )

    bits = bits_of(devices)
    late_bits = [bits[1], bits[0], *bits[2:]]
    second_blocks = [(values, 0) for values in seconds]
    swish_grad = Scatter(second_blocks, [swish_back], bits)
    up_grad = Scatter(second_blocks, [up_back], bits)
    down_grad = Scatter(blocks(grads_near, grads_far), [inner], late_bits, True)
    swish_away = swish_grad.away()
    swish_grad.came[0] = swish_grad.hop(0, swish_away)

    def second_sum(near, far):
        parts, _ = tensor_reduce(near, far)
        down_away = down_grad.away([swish_away])
        return parts[1:], down_away, up_grad.away_halves([down_away])

    second_parts, down_away, up_away = region(
        second_sum, halves(feed_near[3]), (feed_two[3], feed_three[3])
    )
    second_parts = (feed_near[3], *second_parts)
    down_grad.came[0] = down_grad.hop(0, down_away)
    up_grad.came[0] = (up_grad.hop(0, up_away[0]), None)

    middle_grad, own_rows, mlp_norm_part = grid_call(
        middle_back_kernel,
        tiles,
        [own_spec] + [tile_spec] * 4 + [fixed((1, width))],
        [tile_spec, tile_spec, fixed((1, width))],
        [struct((length, width), f32), struct((length, width), bf16), struct((1, width), f32)],
        [place_index, cotangent, *second_parts, middle, gain_two],
        prefetch=1,
    )

    def branch_back(first, second, mixed, gates, queries, run, at, into=None):
        return grid_call(
            branch_back_kernel,
            (half,),
            [
                whole_block, whole_block, fixed((DK, width)), row_spec(DK), row_spec(DK), fixed((1, DK)),
                row_spec(DK), row_spec(DK),
            ],
            [row_spec(DK), row_spec(DK), line(1, DK), chunk_spec(devices, at)],
            [rows_of(DK, bf16), rows_of(DK, bf16), struct((half, 1, DK), f32), chunks],
            [first, second, out_weight, mixed, gates, gain, queries, run],
            into=() if into is None else [(into, 3)],
        )

    first_row = swap(own_rows, "tensor", 1)

    def gather_back(own_rows, first_row):
        second_row = swap(own_rows, "tensor", 2)
        *near, state_back = branch_back(
            own_rows, first_row, mixed_near, gates_near, queries_near, run_near, half
        )
        third_row = swap(hold(second_row, [near[0]]), "tensor", 1)
        *far, state_back = branch_back(
            second_row, third_row, mixed_far, gates_far, queries_far, run_far, 0, state_back
        )
        return second_row, third_row, near, far, state_back

    second_row, third_row, near, far, state_back = region(gather_back, own_rows, first_row)
    rows = [(values, 0) for values in (own_rows, first_row, second_row, third_row)]
    gate_back_near, mixed_back_near, gain_back_near = near
    gate_back_far, mixed_back_far, gain_back_far = far
    norms = blocks(norm_near, norm_far)

    far_bits = [bits[0], *bits[2:], bits[1]]
    out_grad = Scatter(rows, [blocks(branch_near, branch_far)], far_bits, True)
    gate_grad = Scatter(norms, [blocks(gate_back_near, gate_back_far)], bits)

    def states_back(state_back):
        swish_one = swish_grad.one([state_back])
        gate_away = gate_grad.away([swish_one])
        return (
            deal(state_back), swish_one, gate_away, out_grad.away([gate_away]),
            tensor_reduce(halves(feed_near[4]), (feed_two[4], feed_three[4]))[0],
        )

    came, swish_one, gate_away, out_away, output_parts = region(states_back, state_back)

    def states_out(came, swish_one, out_away, gate_away, output_parts):
        up_one = up_grad.one([came])
        own = sum((part.astype(f32) for part in output_parts), middle).astype(bf16)
        return (
            deal(carried(came, lines, True)), swish_grad.hop(1, swish_one), out_grad.hop(0, out_away),
            up_one, down_grad.one([up_one]), [own, swap(own, "tensor", 1), swap(own, "tensor", 2)],
            gate_grad.hop(0, gate_away),
        )

    (
        outgoing, swish_grad.came[1], out_grad.came[0], up_one, down_one, output_blocks,
        gate_grad.came[0],
    ) = region(states_out, came, swish_one, out_away, gate_away, output_parts)

    def mix_back(queries, keys, values, mixed_back, run, scores, incoming, at, rank_rows, after):
        return grid_call(
            mix_back_kernel,
            (half,),
            [row_spec(DK)] * 5
            + [square(length)]
            + [state_specs[1 if at else 0], chunk_spec(devices, at)]
            + [row_spec(rank), fixed((rank, DK)), fixed((1, DK))],
            [row_spec(DK)] * 3 + [line(rank, length), line(rank, DK), line(1, DK)],
            [rows_of(DK, bf16)] * 3
            + [
                struct((half, rank, length), f32),
                struct((half, rank, DK), f32),
                struct((half, 1, DK), f32),
            ],
            [
                queries, keys, values, mixed_back, run, scores, incoming, outgoing,
                rank_rows, rank_up, bias,
            ],
            after=after,
        )

    def first_part(query_back, key_back, value_back, gate_back, at, into=()):
        tile = 512
        pairs = [
            (query_back, query_weight),
            (key_back, key_weight),
            (value_back, value_weight),
            (gate_back, gate_weight),
        ]
        return grid_call(
            sum_kernel,
            (width // tile,),
            [pl.BlockSpec((half_rows, DK), lambda j: (0, 0))] * 4
            + [pl.BlockSpec((tile, DK), lambda j: (j, 0))] * 4,
            [pl.BlockSpec((1, length, tile), lambda j: (at, 0, j))] * 2,
            [struct((half, length, width), bf16)] * 2,
            [*[p[0] for p in pairs], *[p[1] for p in pairs]],
            into=into,
        )

    def in_order(blocks, after=()):
        whole = pl.BlockSpec((length, width), lambda k, order: (0, 0))
        return grid_call(
            place_kernel,
            (4,),
            [whole] * 4,
            pl.BlockSpec((1, length, width), lambda k, order: (order[k], 0, 0)),
            struct((seq_count, length, width), bf16),
            [order, *blocks],
            prefetch=1,
            after=after,
        )

    def mixed_pair(near, far):
        query_key = Scatter(norms, [blocks(near[0], far[0]), blocks(near[1], far[1])], bits)
        return query_key, Scatter(norms, [blocks(near[2], far[2])], late_bits)

    def mixes_back(up_one, outgoing, down_one):
        swish_two = swish_grad.two([outgoing])
        gate_one = gate_grad.one([swish_two])
        near = mix_back(
            queries_near, keys_near, values_near, mixed_back_near, run_near, scores_near,
            incoming_near, half, rank_near, [swish_two],
        )
        far = mix_back(
            queries_far, keys_far, values_far, mixed_back_far, run_far, scores_far,
            incoming_far, 0, rank_far, [near[5]],
        )
        query_key, value = mixed_pair(near, far)
        keep, send = first_part(*far[:3], gate_back_far, 1)
        keep, send = first_part(*near[:3], gate_back_near, 0, [(keep, 0), (send, 1)])
        query_key_away = query_key.away([send])
        value_away = value.away([query_key_away])
        return (
            up_grad.hop(1, up_one), swish_grad.hop(2, swish_two), down_grad.hop(1, down_one),
            gate_grad.hop(1, gate_one), near, far, query_key_away, value_away,
            keep, send, up_grad.hop_rest(up_away[1]),
        )

    (
        up_grad.came[1], swish_grad.came[2], down_grad.came[1], gate_grad.came[1], near, far, query_key_away,
        value_away, first_keep, first_send, up_rest,
    ) = region(mixes_back, up_one, outgoing, down_one)
    up_grad.came[0] = (up_grad.came[0][0], up_rest)

    def first_sum(keep, send, output_second):
        came = swap(send, "tensor", 1)
        output_third = swap(output_second, "tensor", 1)
        gate_two = gate_grad.two([send])
        down_two = down_grad.two([gate_two])
        second = (keep[1].astype(f32) + came[1].astype(f32)).astype(bf16)
        return came, second, gate_two, down_two, output_third

    first_came, first_second, gate_two, down_two, output_third = region(
        first_sum, first_keep, first_send, output_blocks[2]
    )
    output_blocks.append(output_third)
    rank_part_near, up_part_near, bias_part_near = near[3:]
    rank_part_far, up_part_far, bias_part_far = far[3:]
    query_key_grad, value_grad = mixed_pair(near, far)

    def third_window(query_key_away, value_away, gate_two, down_two, first_second):
        rank_part = jnp.concatenate([rank_part_near, rank_part_far], axis=0)
        rank_part = lax.all_to_all(jnp.take(rank_part, order, axis=0), "tensor", 0, 0)
        return (
            query_key_grad.hop(0, query_key_away), value_grad.hop(0, value_away),
            gate_grad.hop(2, gate_two), down_grad.hop(2, down_two), up_grad.two(),
            swish_grad.last(), jnp.sum(rank_part, axis=0).astype(bf16), swap(first_second, "tensor", 2),
            out_grad.one([down_two]), in_order(output_blocks, [down_two]),
        )

    (
        query_key_grad.came[0], value_grad.came[0], gate_grad.came[2], down_grad.came[2], up_two,
        swish_share, rank_back, first_last, out_one, layer_output,
    ) = region(third_window, query_key_away, value_away, gate_two, down_two, first_second)
    query_key_one = query_key_grad.one()
    value_one = value_grad.one([query_key_one])

    input_rows, attn_norm_part = grid_call(
        input_back_kernel,
        tiles,
        [own_spec]
        + [pl.BlockSpec((1, tile, width), lambda b, *_: (0, b, 0))] * 2
        + [
            tile_spec,
            pl.BlockSpec((rank, tile), lambda b, *_: (0, b)), fixed((width, rank)), tile_spec,
            fixed((1, width)),
        ],
        [tile_spec, fixed((1, width))],
        [struct((length, width), bf16), struct((1, width), f32)],
        [
            place_index, layer_input, first_keep, first_came, first_last, rank_back, rank_down, middle_grad,
            attn_norm.reshape(1, width),
        ],
        prefetch=1,
        after=[value_one],
    )
    rank_down_part = contract(rank_back, norm_near[:length], 1, 0)
    own_part = jnp.concatenate([rank_down_part, mlp_norm_part, attn_norm_part], axis=0)
    shared = jnp.concatenate(
        [
            sum(up_part_near) + sum(up_part_far),
            sum(bias_part_near) + sum(bias_part_far),
            sum(gain_back_near) + sum(gain_back_far),
        ],
        axis=0,
    )
    column = width // devices
    own_part = jnp.moveaxis(own_part.reshape(rank + 2, devices, column), 1, 0)
    own_size = (rank + 2) * column
    mail = jnp.concatenate(
        [
            own_part.reshape(devices, own_size),
            jnp.broadcast_to(shared.reshape(1, -1), (devices, shared.size)),
        ],
        axis=1,
    )

    def summed(mail):
        mail = mail.reshape(devices, 1, -1).astype(bf16)
        return jnp.sum(lax.all_to_all(mail, "seq", 0, 0).astype(f32), axis=0)

    def fourth_window(query_key_one, value_one, up_two, out_one, input_rows):
        return (
            swap(input_rows, "tensor", 2),
            query_key_grad.hop(1, query_key_one), value_grad.hop(1, value_one), up_grad.hop(2, up_two),
            out_grad.hop(1, out_one), gate_grad.last(), down_grad.last(),
        )

    (
        second_rows, query_key_grad.came[1], value_grad.came[1], up_grad.came[2], out_grad.came[1],
        gate_share, down_share,
    ) = region(fourth_window, query_key_one, value_one, up_two, out_one, input_rows)


    def fifth_window(input_rows, second_rows, mail):
        query_key_two = query_key_grad.two([second_rows])
        value_two = value_grad.two([query_key_two])
        out_two = out_grad.two([value_two])
        first_rows, third_rows = swap(input_rows, "tensor", 1), swap(second_rows, "tensor", 1)
        return (
            query_key_grad.hop(2, query_key_two), value_grad.hop(2, value_two), out_grad.hop(2, out_two),
            in_order([input_rows, first_rows, second_rows, third_rows]), up_grad.last(), summed(mail),
        )

    query_key_grad.came[2], value_grad.came[2], out_grad.came[2], input_grad, up_share, mail = region(
        fifth_window, input_rows, second_rows, mail
    )

    def sixth_window(mail):
        parts = mail.reshape(-1)[:own_size].reshape(rank + 2, column)
        return query_key_grad.last(), value_grad.last(), out_grad.last(), sum_over(parts, "tensor")

    query_key_share, value_share, out_share, own_part = region(sixth_window, mail)
    shared = mail.reshape(-1)[own_size:].reshape(rank + 2, DK)
    return (
        layer_output,
        input_grad,
        own_part[rank + 1],
        query_key_share[:, :DK],
        query_key_share[:, DK:],
        value_share,
        gate_share,
        own_part[:rank].T,
        shared[:rank],
        shared[rank],
        shared[rank + 1],
        out_share,
        own_part[rank],
        swish_share,
        up_share,
        down_share,
    )


def solution(mesh):
    return jax.shard_map(
        local,
        mesh=mesh,
        in_specs=(
            P(None, "seq", None),
            P(),
            P(None, "tensor"),
            P(None, "tensor"),
            P(None, "tensor"),
            P(None, "tensor"),
            P(),
            P(None, "tensor"),
            P("tensor"),
            P("tensor"),
            P("tensor", None),
            P(),
            P(None, "tensor"),
            P(None, "tensor"),
            P("tensor", None),
            P(None, "seq", None),
        ),
        out_specs=(
            P(None, "seq", None),
            P(None, "seq", None),
            P("seq"),
            P("seq", "tensor"),
            P("seq", "tensor"),
            P("seq", "tensor"),
            P("seq", "tensor"),
            P("seq", None),
            P(None, "tensor"),
            P("tensor"),
            P("tensor"),
            P("tensor", "seq"),
            P("seq"),
            P("seq", "tensor"),
            P("seq", "tensor"),
            P("tensor", "seq"),
        ),
        check_vma=False,
    )
```

```python
import functools

import jax
import jax.numpy as jnp
from jax import lax
from jax.experimental import pallas as pl
from jax.experimental.pallas import tpu as pltpu
from jax.sharding import PartitionSpec as P

DK = 512
BLOCK = 64
EXTRA = 16
ROWS = 256
COST = 1024
VMEM = 48 * 1024 * 1024

bf16 = jnp.bfloat16
f32 = jnp.float32
highest_precision = lax.Precision.HIGHEST
epsilon = 1e-06


def contract(left, right, left_dim, right_dim, precision=None):
    return lax.dot_general(
        left,
        right,
        (((left_dim,), (right_dim,)), ((), ())),
        preferred_element_type=f32,
        precision=precision,
    )


def product(left, right):
    return contract(left, right, 1, 0)


def across(left, right):
    return contract(left, right, 0, 0)


def against(left, right):
    return contract(left, right, 1, 1)


def forget_logits(rank_ref, up_ref, bias_ref):
    return product(rank_ref[...], up_ref[...]) + bias_ref[...].astype(f32)


def positions(count):
    rows = lax.broadcasted_iota(jnp.int32, (count, count), 0)
    cols = lax.broadcasted_iota(jnp.int32, (count, count), 1)
    return rows, cols


def spread(pieces, size):
    width = pieces[0].shape[1]
    return jnp.concatenate([jnp.broadcast_to(piece, (size, width)) for piece in pieces], axis=0)


def scaled_pair(level, query_scaled, key_rows, run):
    count = run.shape[0]
    if level == 0:
        starts = range(0, count, BLOCK)
        center = spread([run[s + BLOCK // 2 : s + BLOCK // 2 + 1] for s in starts], BLOCK)
        query_factor = jnp.exp(run - center)
        key_factor = jnp.exp(center - run)
        return query_scaled * query_factor, key_rows * key_factor, query_factor, key_factor
    group = BLOCK << level
    half = group // 2
    center = spread([run[s + half - 1 : s + half] for s in range(0, count, group)], group)
    place = lax.broadcasted_iota(jnp.int32, run.shape, 0)
    right = (place % group) >= half
    gap = run - center
    query_factor = jnp.where(right, jnp.exp(jnp.where(right, gap, 0.0)), 0.0)
    key_factor = jnp.where(right, 0.0, jnp.exp(jnp.where(right, 0.0, -gap)))
    return query_scaled * query_factor, key_rows * key_factor, query_factor, key_factor


def level_mask(level, rows, cols):
    if level == 0:
        return (rows // BLOCK == cols // BLOCK) & (cols <= rows)
    group = BLOCK << level
    half = group // 2
    return (rows // group == cols // group) & (rows % group >= half) & (cols % group < half)


def level_count(count):
    levels = 1
    while (BLOCK << (levels - 1)) < count:
        levels += 1
    return levels


def norm_kernel(order_ref, input_ref, grad_ref, gain_ref, norm_ref, rows_ref):
    values = input_ref[0].astype(f32)
    scale = lax.rsqrt(jnp.mean(values * values, axis=-1, keepdims=True) + epsilon)
    norm_ref[...] = (values * scale * gain_ref[...].astype(f32)).astype(bf16)
    rows_ref[...] = grad_ref[0]


def decay_kernel(rank_ref, up_ref, bias_ref, run_ref):
    logits = forget_logits(rank_ref, up_ref, bias_ref)
    decays = (jnp.minimum(logits, 0.0) - jnp.log1p(jnp.exp(-jnp.abs(logits)))) * (1.0 / 16.0)
    rows, cols = positions(decays.shape[0])
    run_ref[...] = contract((cols <= rows).astype(f32), decays, 1, 0, highest_precision)


def total_lines(run):
    return as_lines(run[run.shape[0] - 1 :])


def as_lines(*totals):
    place = lax.broadcasted_iota(jnp.int32, (EXTRA, DK), 0)
    lines = jnp.zeros((EXTRA, DK), f32)
    for first, total in enumerate(totals):
        high = total.astype(bf16)
        rest = total - high.astype(f32)
        middle = rest.astype(bf16)
        low = (rest - middle.astype(f32)).astype(bf16)
        for at, line in enumerate((high, middle, low)):
            lines = jnp.where(place == 3 * first + at, line.astype(f32), lines)
    return lines.astype(bf16)


def from_lines(lines, first=0):
    lines = lines.astype(f32)[3 * first : 3 * first + 3]
    return lines[0:1] + lines[1:2] + lines[2:3]


def state_of(key_ref, value_ref, run):
    left = (key_ref[...].astype(f32) * jnp.exp(run[run.shape[0] - 1 :] - run)).astype(bf16)
    return across(value_ref[...], left).astype(bf16)


def state_kernel(key_ref, value_ref, run_ref, state_ref, lines_ref):
    run = run_ref[...]
    state_ref[0] = state_of(key_ref, value_ref, run)
    lines_ref[0] = total_lines(run)


def cut_state_kernel(me_ref, key_ref, value_ref, run_ref, keep_ref, send_ref, lines_ref, held):
    run = run_ref[...]
    held[...] = state_of(key_ref, value_ref, run).reshape(held.shape)
    lines = total_lines(run)
    y, z = me_ref[0] % 2, me_ref[0] // 2
    for at in range(4):
        keep_ref[0, at] = held[y * 4 + (z ^ at)]
        send_ref[0, at] = held[(1 - y) * 4 + (z ^ at)]
    lines_ref[0] = lines
    send_ref[0, 4, :EXTRA] = lines


def pair_kernel(me_ref, keep_ref, lines_ref, came_ref, first_ref, *part_refs):
    lead = me_ref[0] % 2 == 0
    own, other = from_lines(lines_ref[0]), from_lines(came_ref[0, 4, :EXTRA])
    later = jnp.exp(jnp.where(lead, other, own))
    lines = as_lines(jnp.where(lead, own, other), jnp.where(lead, other, own))
    for at, part_ref in enumerate(part_refs):
        mine, came = keep_ref[0, at].astype(f32), came_ref[0, at].astype(f32)
        first = jnp.where(lead, mine, came)
        first_ref[0, at] = first.astype(bf16)
        rows = first.shape[0]
        part_ref[0, :rows] = (first * later + jnp.where(lead, came, mine)).astype(bf16)
        part_ref[0, rows:] = lines


def chain_kernel(me_ref, *refs):
    part_refs, out_refs, every_ref = refs[:4], refs[4:8], refs[8]
    held, lines, entered = refs[9:]
    z = me_ref[0] // 2
    rows = held.shape[1]
    for at in range(4):
        held[z ^ at] = part_refs[at][0, :rows]
        lines[z ^ at] = part_refs[at][0, rows:]
    carry = jnp.zeros(held.shape[1:], f32)
    for at in range(4):
        entered[at] = carry.astype(bf16)
        totals = from_lines(lines[at]), from_lines(lines[at], 1)
        for y in range(2):
            every_ref[2 * at + y, 0] = as_lines(totals[y])
        carry = carry * jnp.exp(totals[0] + totals[1]) + held[at].astype(f32)
    for at in range(4):
        out_refs[at][0] = entered[z ^ at]


def enter_kernel(me_ref, lines_ref, came_ref, first_ref, *refs):
    *part_refs, whole_ref, send_ref = refs
    y, z = me_ref[0] % 2, me_ref[0] // 2
    lead = y == 0
    earlier = jnp.exp(jnp.where(lead, from_lines(lines_ref[0]), from_lines(came_ref[0, 0, :EXTRA])))
    for at in range(4):
        pair = part_refs[at][0].astype(f32)
        inner = pair * earlier + first_ref[0, at].astype(f32)
        whole_ref[0, 0, z ^ at] = jnp.where(lead, pair, inner).astype(bf16)
        send_ref[0, z ^ at] = jnp.where(lead, inner, pair).astype(bf16)


def join_kernel(me_ref, came_ref, whole_ref):
    whole_ref[0, 0] = came_ref[0]


def score_kernel(query_ref, key_ref, run_ref, score_ref):
    run = run_ref[...]
    query_scaled = query_ref[...].astype(f32) * DK ** (-0.5)
    key_rows = key_ref[...].astype(f32)
    rows, cols = positions(run.shape[0])
    scores = jnp.zeros(rows.shape, f32)
    for level in range(level_count(run.shape[0])):
        left, right, _, _ = scaled_pair(level, query_scaled, key_rows, run)
        scores = jnp.where(
            level_mask(level, rows, cols), against(left.astype(bf16), right.astype(bf16)), scores
        )
    score_ref[0] = scores.astype(bf16)


def whole_state(ref):
    return ref[...].reshape(DK, DK)


def faded_queries(query_ref, run_ref):
    return (query_ref[...].astype(f32) * DK ** (-0.5) * jnp.exp(run_ref[...])).astype(bf16)


def mix_kernel(query_ref, value_ref, run_ref, score_ref, state_ref, gate_ref, gain_ref, mixed_ref, branch_ref):
    faded = faded_queries(query_ref, run_ref)
    mixed = product(score_ref[0], value_ref[...]) + against(faded, whole_state(state_ref))
    mixed_ref[...] = mixed
    scale = lax.rsqrt(jnp.mean(mixed * mixed, axis=-1, keepdims=True) + epsilon)
    gate = gate_ref[...]
    branch_ref[...] = (
        mixed * scale * gain_ref[...].astype(f32) * (gate * jax.nn.sigmoid(gate))
    ).astype(bf16)


def branch_back_kernel(
    first_ref, second_ref, weight_ref, mixed_ref, gate_ref, gain_ref, query_ref, run_ref,
    gate_back_ref, mixed_back_ref, gain_back_ref, state_back_ref,
):
    branch_grad = against(either(first_ref, second_ref), weight_ref[...])
    mixed = mixed_ref[...]
    scale = lax.rsqrt(jnp.mean(mixed * mixed, axis=-1, keepdims=True) + epsilon)
    unit = mixed * scale
    gate = gate_ref[...]
    gain = gain_ref[...].astype(f32)
    sig = jax.nn.sigmoid(gate)
    gate_back_ref[...] = (branch_grad * unit * gain * sig * (1.0 + gate * (1.0 - sig))).astype(bf16)
    shaped_grad = branch_grad * (gate * sig)
    gain_back_ref[0] = jnp.sum(shaped_grad * unit, axis=0, keepdims=True)
    unit_grad = shaped_grad * gain
    mixed_grad = scale * (unit_grad - unit * jnp.mean(unit_grad * unit, axis=-1, keepdims=True))
    mixed_back = mixed_grad.astype(bf16)
    mixed_back_ref[...] = mixed_back
    faded = faded_queries(query_ref, run_ref)
    state_back_ref[...] = across(mixed_back, faded).astype(bf16).reshape(state_back_ref.shape)


def ordered_sum(mask, values):
    high = values.astype(bf16)
    low = (values - high.astype(f32)).astype(bf16)
    ones = mask.astype(f32).astype(bf16)
    return product(ones, high) + product(ones, low)


def mix_back_kernel(
    query_ref, key_ref, value_ref, grad_ref, run_ref, score_ref, state_ref, state_back_ref,
    rank_ref, up_ref, bias_ref,
    query_back_ref, key_back_ref, value_back_ref, rank_back_ref, up_back_ref, bias_back_ref,
):
    run = run_ref[...]
    count = run.shape[0]
    query_scaled = query_ref[...].astype(f32) * DK ** (-0.5)
    key_rows = key_ref[...].astype(f32)
    values = value_ref[...]
    grads = grad_ref[...]
    state = whole_state(state_ref)
    state_back = whole_state(state_back_ref)
    rows, cols = positions(count)
    pairs = against(grads, values)

    closing = run[count - 1 : count]
    fade_in = jnp.exp(run)
    fade_out = jnp.exp(closing - run)
    kept = (key_rows * fade_out).astype(bf16)
    value_back_ref[...] = (across(score_ref[0], grads) + against(kept, state_back)).astype(bf16)

    from_state = product(grads, state)
    to_state = product(values, state_back)
    query_back = fade_in * from_state
    key_back = fade_out * to_state
    decay_back = jnp.exp(closing) * jnp.sum(
        state.astype(f32) * state_back.astype(f32), axis=0, keepdims=True
    )
    decay_back = decay_back + ordered_sum(cols >= rows, query_scaled * fade_in * from_state)
    decay_back = decay_back + ordered_sum(cols < rows, key_rows * fade_out * to_state)
    for level in range(level_count(count)):
        left, right, query_factor, key_factor = scaled_pair(level, query_scaled, key_rows, run)
        left, right = left.astype(bf16), right.astype(bf16)
        here = jnp.where(level_mask(level, rows, cols), pairs, 0.0).astype(bf16)
        to_query = product(here, right)
        to_key = across(here, left)
        query_back = query_back + query_factor * to_query
        key_back = key_back + key_factor * to_key
        left_part = left.astype(f32) * to_query
        right_part = right.astype(f32) * to_key
        if level == 0:
            mask = (rows // BLOCK == cols // BLOCK) & (cols >= rows)
            decay_back = decay_back + ordered_sum(mask, left_part - right_part)
        else:
            group = BLOCK << level
            half = group // 2
            same = rows // group == cols // group
            late = same & (rows % group >= half) & (cols >= rows)
            early = same & (rows % group < half) & (cols < rows)
            decay_back = decay_back + ordered_sum(late | early, left_part + right_part)
    query_back_ref[...] = (query_back * DK ** (-0.5)).astype(bf16)
    key_back_ref[...] = key_back.astype(bf16)
    logits = forget_logits(rank_ref, up_ref, bias_ref)
    logit_back = (decay_back * jax.nn.sigmoid(-logits) * (1.0 / 16.0)).astype(bf16)
    rank_back_ref[0] = against(up_ref[...], logit_back)
    up_back_ref[0] = across(rank_ref[...], logit_back)
    bias_back_ref[0] = jnp.sum(logit_back.astype(f32), axis=0, keepdims=True)


def prefix_kernel(reverse, lines_ref, parts_ref, out_ref):
    count = parts_ref.shape[0]
    rows = out_ref.shape[2]
    carry = jnp.zeros(out_ref.shape[2:], f32)
    for step in range(count):
        at = count - 1 - step if reverse else step
        out_ref[at, 0] = carry.astype(bf16)
        total = from_lines(lines_ref[at, 0])
        carry = carry * jnp.exp(total) + parts_ref[at, 0].astype(f32)


def hold_kernel(values_ref, out_ref):
    out_ref[...] = values_ref[...]


def either(first_ref, second_ref):
    return jnp.where(pl.program_id(0) == 0, first_ref[...], second_ref[...])


def middle_kernel(place_ref, input_ref, own_ref, first_ref, last_ref, gain_ref, middle_ref, second_ref):
    middle = input_ref[0].astype(f32) + (
        own_ref[...].astype(f32) + first_ref[...].astype(f32) + last_ref[...].astype(f32)
    )
    middle_ref[...] = middle
    scale = lax.rsqrt(jnp.mean(middle * middle, axis=-1, keepdims=True) + epsilon)
    second_ref[...] = (middle * scale * gain_ref[...].astype(f32)).astype(bf16)


def norm_back(values, grad, gain):
    scale = lax.rsqrt(jnp.mean(values * values, axis=-1, keepdims=True) + epsilon)
    unit = values * scale
    scaled = grad * gain
    back = scale * (scaled - unit * jnp.mean(scaled * unit, axis=-1, keepdims=True))
    return back, jnp.sum(grad * unit, axis=0, keepdims=True)


def add_part(out_ref, part):
    @pl.when(pl.program_id(0) == 0)
    def _():
        out_ref[...] = part

    @pl.when(pl.program_id(0) != 0)
    def _():
        out_ref[...] += part


def middle_back_kernel(
    place_ref, grad_ref, own_ref, first_ref, last_ref, middle_ref, gain_ref, back_ref, rows_ref, part_ref
):
    grad = own_ref[...].astype(f32) + first_ref[...].astype(f32) + last_ref[...].astype(f32)
    back, part = norm_back(middle_ref[...], grad, gain_ref[...].astype(f32))
    back = grad_ref[0].astype(f32) + back
    back_ref[...] = back
    rows_ref[...] = back.astype(bf16)
    add_part(part_ref, part)


def input_back_kernel(
    place_ref, input_ref, own_ref, first_ref, last_ref, rank_ref, down_ref, middle_ref, gain_ref, rows_ref, part_ref
):
    grad = own_ref[0].astype(f32) + first_ref[0].astype(f32) + last_ref[...].astype(f32)
    grad = grad + contract(rank_ref[...], down_ref[...], 0, 1)
    back, part = norm_back(input_ref[0].astype(f32), grad, gain_ref[...].astype(f32))
    rows_ref[...] = (middle_ref[...] + back).astype(bf16)
    add_part(part_ref, part)


def feed_kernel(
    first_ref, second_ref, grads_ref, swish_ref, up_ref, down_ref,
    inner_ref, swish_back_ref, up_back_ref, second_back_ref, out_ref,
    swish_held, up_held, down_held, semaphores,
):
    copies = [
        pltpu.make_async_copy(swish_ref, swish_held, semaphores.at[0]),
        pltpu.make_async_copy(up_ref, up_held, semaphores.at[1]),
        pltpu.make_async_copy(down_ref, down_held, semaphores.at[2]),
    ]
    start = pl.program_id(0) == 0

    @pl.when(start)
    def _():
        for copy in copies:
            copy.start()

    rows = either(first_ref, second_ref)

    @pl.when(start)
    def _():
        copies[0].wait()

    swish = product(rows, swish_held[...])

    @pl.when(start)
    def _():
        copies[1].wait()

    up = product(rows, up_held[...])
    sig = jax.nn.sigmoid(swish)
    act = swish * sig
    inner = (act * up).astype(bf16)
    inner_ref[...] = inner

    @pl.when(start)
    def _():
        copies[2].wait()

    inner_grad = against(grads_ref[...], down_held[...])
    swish_back = (inner_grad * up * sig * (1.0 + swish * (1.0 - sig))).astype(bf16)
    up_back = (inner_grad * act).astype(bf16)
    swish_back_ref[...] = swish_back
    up_back_ref[...] = up_back
    second_back_ref[...] = (against(swish_back, swish_held[...]) + against(up_back, up_held[...])).astype(bf16)
    out_ref[...] = product(inner, down_held[...]).astype(bf16)


def place_kernel(order_ref, *refs):
    out_ref = refs[-1]
    step = pl.program_id(0)
    for k in range(4):

        @pl.when(step == k)
        def _():
            out_ref[0] = refs[k][...]


def sum_kernel(*refs):
    *refs, keep_ref, send_ref = refs
    count = len(refs) // 2
    rows = keep_ref.shape[1]
    total = against(refs[0][...], refs[count][...])
    for k in range(1, count):
        total = total + against(refs[k][...], refs[count + k][...])
    total = total.astype(bf16)
    keep_ref[0] = total[:rows]
    send_ref[0] = total[rows:]


def grad_kernel(parts, groups, cut_groups, turned, pick_ref, *refs):
    cuts, refs = refs[: parts * cut_groups], refs[parts * cut_groups :]
    others, refs = refs[: parts * groups], refs[parts * groups :]
    arrived, out_ref = refs[:-1], refs[-1]
    for group in range(groups):
        total = None
        members = others[group * parts : (group + 1) * parts]
        width = members[0].shape[1]
        columns = slice(group * width, (group + 1) * width)
        first = group * parts if cut_groups > 1 else 0
        for cut, other in zip(cuts[first : first + parts], members):
            part = across(cut[...], other[...])
            total = part if total is None else total + part
        for ref in arrived:
            total = total + ref[0, :, columns].astype(f32)
        if turned:
            out_ref[...] = total.T
        else:
            out_ref[0, :, columns] = total.astype(out_ref.dtype)


def struct(shape, dtype):
    return jax.ShapeDtypeStruct(shape, dtype)


def grid_call(kernel, grid, in_specs, out_specs, out_shape, args, prefetch=0, after=(), scratch=(), into=()):
    first, last = len(args), len(args) + len(after)
    aliases = {}
    for array, at in into:
        aliases[last] = at
        after = (*after, array)
        last += 1

    def run(*refs):
        kernel(*refs[:first], *refs[last:])

    return pl.pallas_call(
        run,
        grid_spec=pltpu.PrefetchScalarGridSpec(
            num_scalar_prefetch=prefetch,
            grid=grid,
            in_specs=list(in_specs) + [pl.BlockSpec(memory_space=pl.ANY)] * len(after),
            out_specs=out_specs,
            scratch_shapes=list(scratch),
        ),
        out_shape=out_shape,
        input_output_aliases=aliases,
        compiler_params=pltpu.CompilerParams(vmem_limit_bytes=VMEM),
        cost_estimate=pl.CostEstimate(flops=COST, bytes_accessed=COST, transcendentals=0),
    )(*args, *after)


def swap(values, axis, distance):
    count = lax.axis_size(axis)
    return lax.ppermute(values, axis, [(i, i ^ distance) for i in range(count)])


def region(function, *args):
    shapes = jax.eval_shape(function, *args)

    def never(*_):
        return jax.tree.map(lambda a: jnp.zeros(a.shape, a.dtype), shapes)

    return lax.cond(lax.axis_index("seq") >= 0, function, never, *args)


def bits_of(count):
    return [1 << k for k in range(count.bit_length() - 1)]


def hold(values, after):
    spec = pl.BlockSpec(values.shape, lambda: (0,) * values.ndim)
    return grid_call(hold_kernel, (), [spec], spec, struct(values.shape, values.dtype), [values], after=after)


def chunk_spec(count, first=0):
    return pl.BlockSpec((count, 1, DK // count, DK), lambda b, *_: (0, b + first, 0, 0))


def carried(pieces, lines, reverse, after=()):
    count, seq_count, share, _ = pieces.shape
    return grid_call(
        functools.partial(prefix_kernel, reverse),
        (seq_count,),
        [pl.BlockSpec((count, 1, EXTRA, DK), lambda b: (0, b, 0, 0)), chunk_spec(count)],
        chunk_spec(count),
        struct((count, seq_count, share, DK), bf16),
        [lines, pieces],
        after=after,
    )


def deal(pieces):
    return lax.all_to_all(pieces, "seq", 0, 0)


def tensor_reduce(near, far):
    third = swap(far[1], "tensor", 1)
    second = (far[0].astype(f32) + third.astype(f32)).astype(bf16)
    first = swap(near[1], "tensor", 1)
    return (near[0], first, swap(second, "tensor", 2)), second


def tensor_gather(own):
    first = swap(own, "tensor", 1)
    second = swap(own, "tensor", 2)

    def third(after):
        return swap(hold(second, after) if after else second, "tensor", 1)

    return own, first, second, third


def grad_part(cuts, groups, picks, arrived, dtype, turned=False, after=()):
    rows = ROWS
    width = groups[0][0][0].shape[1]
    whole = width * len(groups)
    parts = len(groups[0])
    cut_groups = len(cuts)
    cuts = [block for group in cuts for block in group]
    share = cuts[0][0].shape[1] // lax.axis_size("seq")
    chunks = len(picks)
    me = lax.axis_index("seq")
    index = jnp.stack([me ^ r for r in picks]).astype(jnp.int32)
    others = [block for group in groups for block in group]
    in_specs = [pl.BlockSpec((rows, share), lambda k, pick, at=at: (at, pick[k])) for _, at in cuts]
    in_specs += [pl.BlockSpec((rows, width), lambda k, pick, at=at: (at, 0)) for _, at in others]
    for _, first in arrived:
        in_specs.append(pl.BlockSpec((1, share, whole), lambda k, pick, first=first: (k + first, 0, 0)))
    if turned:
        out_spec = pl.BlockSpec((whole, share), lambda k, pick: (0, 0))
        shape = (whole, share)
    else:
        out_spec = pl.BlockSpec((1, share, whole), lambda k, pick: (k, 0, 0))
        shape = (chunks, share, whole)
    return grid_call(
        functools.partial(grad_kernel, parts, len(groups), cut_groups, turned),
        (chunks,),
        in_specs,
        out_spec,
        struct(shape, dtype),
        [index, *[a for a, _ in cuts], *[a for a, _ in others], *[a for a, _ in arrived]],
        prefetch=1,
        after=after,
    )


class Scatter:
    def __init__(self, cuts, groups, order, turned=False):
        cuts = cuts if isinstance(cuts[0], list) else [cuts]
        self.cuts, self.groups, self.order, self.turned = cuts, groups, order, turned
        self.split = lax.axis_size("seq") == 8
        self.came = [None] * 3

    def part(self, picks, arrived, dtype, turned=False, after=()):
        return grad_part(self.cuts, self.groups, picks, arrived, dtype, turned, after)

    def hop(self, at, part):
        if self.split:
            return swap(part, "seq", self.order[at])
        return part if at else lax.psum_scatter(part, "seq", scatter_dimension=0, tiled=True)

    def whole(self):
        return jnp.concatenate(
            [
                sum(
                    across(a[i * ROWS : (i + 1) * ROWS], b[j * ROWS : (j + 1) * ROWS])
                    for (a, i), (b, j) in zip(cuts, group)
                ).astype(bf16)
                for cuts, group in zip(
                    self.cuts if len(self.cuts) > 1 else self.cuts * len(self.groups), self.groups
                )
            ],
            axis=1,
        )

    def away(self, after=()):
        if not self.split:
            return self.whole()
        a, b, c = self.order
        return self.part([a ^ b, a ^ b ^ c, a ^ c, a], [], bf16, after=after)

    def away_halves(self, after=()):
        if not self.split:
            return self.whole(), jnp.zeros((8, 128), bf16)
        a, b, c = self.order
        front = self.part([a ^ b, a ^ b ^ c], [], bf16, after=after)
        return front, self.part([a ^ c, a], [], bf16, after=[front])

    def hop_rest(self, part):
        return swap(part, "seq", self.order[0]) if self.split else part

    def arrived(self, at):
        came = self.came[0]
        if not isinstance(came, tuple):
            return came, at
        return (came[0], at) if at < 2 else (came[1], at - 2)

    def one(self, after=()):
        if not self.split:
            return self.arrived(0)[0]
        a, b, c = self.order
        return self.part([b, b ^ c], [self.arrived(0)], bf16, after=after)

    def two(self, after=()):
        if not self.split:
            return self.arrived(0)[0]
        c = self.order[2]
        return self.part([c], [self.arrived(2), (self.came[1], 1)], bf16, after=after)

    def last(self, after=()):
        if not self.split:
            total = self.arrived(0)[0].astype(f32)
            return total.T if self.turned else total
        arrived = [self.arrived(3), (self.came[1], 0), (self.came[2], 0)]
        total = self.part([0], arrived, f32, self.turned, after=after)
        return total if self.turned else total[0]

    def most(self, after=()):
        if not self.split:
            return self.arrived(0)[0].astype(f32)
        return self.part([0], [self.arrived(3), (self.came[1], 0)], f32, after=after)

    def finish(self, most):
        total = most[0] + self.came[2][0].astype(f32) if self.split else most
        return total.T if self.turned else total


def sum_over(values, axis):
    for bit in bits_of(lax.axis_size(axis)):
        values = values + swap(values, axis, bit)
    return values


def local(
    layer_input,
    attn_norm,
    query_weight,
    key_weight,
    value_weight,
    gate_weight,
    rank_down,
    rank_up,
    decay_bias,
    head_gain,
    out_weight,
    mlp_norm,
    swish_weight,
    up_weight,
    down_weight,
    cotangent,
):
    seq_count, length, width = layer_input.shape
    place = lax.axis_index("tensor")
    devices = lax.axis_size("seq")
    half = seq_count // 2
    half_rows = half * length
    rank = rank_down.shape[1]
    bias = decay_bias.reshape(1, DK)
    gain = head_gain.reshape(1, DK)
    share = DK // devices

    def row_spec(size):
        return pl.BlockSpec((length, size), lambda b, *_: (b, 0))

    def fixed(shape):
        return pl.BlockSpec(shape, lambda b, *_: (0,) * len(shape))

    def square(size):
        return pl.BlockSpec((1, size, size), lambda b, *_: (b, 0, 0))

    def line(rows, size):
        return pl.BlockSpec((1, rows, size), lambda b, *_: (b, 0, 0))

    def rows_of(size, dtype):
        return struct((half_rows, size), dtype)

    chunks = struct((devices, seq_count, share, DK), bf16)
    whole_block = pl.BlockSpec((length, width), lambda b, *_: (0, 0))

    def blocks(near, far):
        return [(near, 0), (near, 1), (far, 0), (far, 1)]

    def halves(values):
        return values[:length], values[length:]

    def first_rows(order, after=()):
        spec = pl.BlockSpec((1, length, width), lambda b, order: (order[b], 0, 0))
        return grid_call(
            norm_kernel,
            (half,),
            [spec, spec, fixed((1, width))],
            [row_spec(width), row_spec(width)],
            [rows_of(width, bf16), rows_of(width, bf16)],
            [order, layer_input, cotangent, attn_norm.reshape(1, width)],
            prefetch=1,
            after=after,
        )

    def decays(norm):
        rank_rows = product(norm, rank_down).astype(bf16)
        run = grid_call(
            decay_kernel,
            (half,),
            [row_spec(rank), fixed((rank, DK)), fixed((1, DK))],
            row_spec(DK),
            rows_of(DK, f32),
            [rank_rows, rank_up, bias],
        )
        return rank_rows, run

    quarter = DK // 8
    me = lax.axis_index("seq").astype(jnp.int32).reshape(1)

    def quarters(count, size=quarter):
        return pl.BlockSpec((1, count, size, DK), lambda b, *_: (b, 0, 0, 0))

    def states(norm, run, after=()):
        keys = product(norm, key_weight).astype(bf16)
        values = product(norm, value_weight).astype(bf16)
        lines = struct((half, EXTRA, DK), bf16)
        if devices != 8:
            parts = grid_call(
                state_kernel,
                (half,),
                [row_spec(DK)] * 3,
                [square(DK), line(EXTRA, DK)],
                [struct((half, DK, DK), bf16), lines],
                [keys, values, run],
                after=after,
            )
        else:
            parts = grid_call(
                cut_state_kernel,
                (half,),
                [row_spec(DK)] * 3,
                [quarters(4), quarters(5), line(EXTRA, DK)],
                [struct((half, 4, quarter, DK), bf16), struct((half, 5, quarter, DK), bf16), lines],
                [me, keys, values, run],
                prefetch=1,
                after=after,
                scratch=[pltpu.VMEM((8, quarter, DK), bf16)],
            )
        return keys, values, parts

    def pairs(parts, came, after=()):
        keep, _, lines = parts
        return grid_call(
            pair_kernel,
            (half,),
            [quarters(4), line(EXTRA, DK), quarters(5)],
            [quarters(4)] + [line(quarter + EXTRA, DK)] * 4,
            [struct((half, 4, quarter, DK), bf16)] + [struct((half, quarter + EXTRA, DK), bf16)] * 4,
            [me, keep, lines, came],
            prefetch=1,
            after=after,
        )

    def chain(own, came, first, after=(), into=()):
        return grid_call(
            chain_kernel,
            (half,),
            [line(quarter + EXTRA, DK)] * 4,
            [line(quarter, DK)] * 4
            + [pl.BlockSpec((8, 1, EXTRA, DK), lambda b, *_: (0, b + first, 0, 0))],
            [struct((half, quarter, DK), bf16)] * 4 + [struct((8, seq_count, EXTRA, DK), bf16)],
            [me, own, *came],
            prefetch=1,
            after=after,
            into=into,
            scratch=[
                pltpu.VMEM((4, quarter, DK), bf16),
                pltpu.VMEM((4, EXTRA, DK), bf16),
                pltpu.VMEM((4, quarter, DK), bf16),
            ],
        )

    def enter(parts, came, first, own, others, after=()):
        return grid_call(
            enter_kernel,
            (half,),
            [line(EXTRA, DK), pl.BlockSpec((1, 1, quarter, DK), lambda b, *_: (b, 4, 0, 0)), quarters(4)]
            + [line(quarter, DK)] * 4,
            [pl.BlockSpec((1, 1, 4, quarter, DK), lambda b, me: (me[0] % 2, b, 0, 0, 0)), quarters(4)],
            [struct((2, half, 4, quarter, DK), bf16), struct((half, 4, quarter, DK), bf16)],
            [me, parts[2], came, first, own, *others],
            prefetch=1,
            after=after,
        )

    def join(whole, came):
        return grid_call(
            join_kernel,
            (half,),
            [quarters(4)],
            pl.BlockSpec((1, 1, 4, quarter, DK), lambda b, me: (1 - me[0] % 2, b, 0, 0, 0)),
            struct(whole.shape, bf16),
            [me, came],
            prefetch=1,
            into=[(whole, 0)],
        )

    def along(parts):
        return [swap(part, "seq", 2 * at) for at, part in enumerate(parts, 1)]

    def scored(norm, keys, run, after=()):
        queries = product(norm, query_weight).astype(bf16)
        gates = product(norm, gate_weight)
        scores = grid_call(
            score_kernel,
            (half,),
            [row_spec(DK)] * 3,
            square(length),
            struct((half, length, length), bf16),
            [queries, keys, run],
            after=after,
        )
        return queries, gates, scores

    def mix(queries, values, run, scores, incoming, at, gates, after=()):
        return grid_call(
            mix_kernel,
            (half,),
            [row_spec(DK)] * 3
            + [square(length), state_specs[at], row_spec(DK), fixed((1, DK))],
            [row_spec(DK), row_spec(DK)],
            [rows_of(DK, f32), rows_of(DK, bf16)],
            [queries, values, run, scores, incoming, gates, gain],
            after=after,
        )

    order = jnp.arange(seq_count, dtype=jnp.int32) ^ place
    place_index = order[:1]
    norm_far, grads_far = first_rows(order[half:])
    rank_far, run_far = decays(norm_far)
    keys_far, values_far, parts_far = states(norm_far, run_far)
    norm_near, grads_near = first_rows(order[:half], [parts_far[1]])
    rank_near, run_near = decays(norm_near)
    keys_near, values_near, parts_near = states(norm_near, run_near)
    queries_far, gates_far, scores_far = scored(norm_far, keys_far, run_far, [parts_near[1]])
    if devices != 8:
        queries_near, gates_near, scores_near = scored(norm_near, keys_near, run_near, [scores_far])
        state = jnp.concatenate([parts_far[0], parts_near[0]], axis=0)
        state = jnp.moveaxis(state.reshape(seq_count, devices, share, DK), 1, 0)
        every_line = jnp.concatenate([parts_far[1], parts_near[1]], axis=0)
        lines = deal(jnp.broadcast_to(every_line[None], (devices, *every_line.shape)))
        incoming = deal(carried(deal(state), lines, False))
        incoming_far = incoming_near = incoming
        state_specs = [chunk_spec(devices, at) for at in (0, half)]
    else:
        came_far = swap(parts_far[1], "seq", 1)
        came_near = swap(parts_near[1], "seq", 1)
        first_far, *pair_far = pairs(parts_far, came_far, [parts_near[1]])
        others_far = along(pair_far[1:])
        first_near, *pair_near = pairs(parts_near, came_near, [pair_far[0], scores_far])
        others_near = along(pair_near[1:])
        *chain_far, lines = chain(pair_far[0], others_far, 0, [pair_near[0]])
        back_far = along(chain_far[1:])
        queries_near, gates_near, scores_near = scored(norm_near, keys_near, run_near, [chain_far[0]])
        *chain_near, lines = chain(pair_near[0], others_near, half, [chain_far[0]], [(lines, 4)])
        back_near = along(chain_near[1:])
        whole_far, send_far = enter(parts_far, came_far, first_far, chain_far[0], back_far, [chain_near[0]])
        half_far = swap(send_far, "seq", 1)
        whole_near, send_near = enter(
            parts_near, came_near, first_near, chain_near[0], back_near, [send_far, scores_near]
        )
        half_near = swap(send_near, "seq", 1)
        incoming_far = join(whole_far, half_far)
        incoming_near = join(whole_near, half_near)
        state_specs = [
            pl.BlockSpec((2, 1, 4, quarter, DK), lambda b, *_: (0, b, 0, 0, 0)) for at in range(2)
        ]

    mixed_far, branch_far = mix(queries_far, values_far, run_far, scores_far, incoming_far, 0, gates_far)
    out_far = product(branch_far, out_weight).astype(bf16)
    out_third = swap(out_far[length:], "tensor", 1)
    out_second = (out_far[:length].astype(f32) + out_third.astype(f32)).astype(bf16)
    out_last = swap(out_second, "tensor", 2)
    mixed_near, branch_near = mix(
        queries_near, values_near, run_near, scores_near, incoming_near, 1, gates_near, [out_second]
    )
    out_near = product(branch_near, out_weight).astype(bf16)
    out_first = region(lambda values: swap(values[length:], "tensor", 1), out_near)
    out_parts = (out_near[:length], out_first, out_last)

    tile = 128
    tiles = (length // tile,)
    tile_spec = pl.BlockSpec((tile, width), lambda b, *_: (b, 0))
    own_spec = pl.BlockSpec((1, tile, width), lambda b, place: (place[0], b, 0))
    gain_two = mlp_norm.reshape(1, width)
    middle, second_own = grid_call(
        middle_kernel,
        tiles,
        [own_spec] + [tile_spec] * 3 + [fixed((1, width))],
        [tile_spec] * 2,
        [struct((length, width), f32), struct((length, width), bf16)],
        [place_index, layer_input, *out_parts, gain_two],
        prefetch=1,
    )
    *seconds, second_third = tensor_gather(second_own)

    hidden = swish_weight.shape[1]
    anywhere = pl.BlockSpec(memory_space=pl.ANY)

    def feed(rows, grads, at, after=()):
        count = len(rows)
        return grid_call(
            feed_kernel,
            (count,),
            [whole_block] * 2
            + [pl.BlockSpec((length, width), lambda b: (b + at, 0))]
            + [anywhere] * 3,
            [row_spec(hidden)] * 3 + [row_spec(width)] * 2,
            [struct((count * length, hidden), bf16)] * 3 + [struct((count * length, width), bf16)] * 2,
            [rows[0], rows[-1], grads, swish_weight, up_weight, down_weight],
            scratch=[
                pltpu.VMEM((width, hidden), bf16),
                pltpu.VMEM((width, hidden), bf16),
                pltpu.VMEM((hidden, width), bf16),
                pltpu.SemaphoreType.DMA((3,)),
            ],
            after=after,
        )

    feed_near = feed(seconds[:2], grads_near, 0)
    seconds.append(second_third([feed_near[4]]))
    feed_two = feed(seconds[2:3], grads_far, 0, [feed_near[4]])
    feed_three = feed(seconds[3:4], grads_far, 1, [feed_two[4]])
    inner, swish_back, up_back = (
        [(feed_near[k], 0), (feed_near[k], 1), (feed_two[k], 0), (feed_three[k], 0)] for k in range(3)
    )

    bits = bits_of(devices)
    late_bits = [bits[1], bits[0], *bits[2:]]
    second_blocks = [(values, 0) for values in seconds]
    swish_grad = Scatter(second_blocks, [swish_back], bits)
    up_grad = Scatter(second_blocks, [up_back], bits)
    down_grad = Scatter(blocks(grads_near, grads_far), [inner], late_bits, True)
    swish_away = swish_grad.away()
    swish_grad.came[0] = swish_grad.hop(0, swish_away)

    def second_sum(near, far):
        parts, _ = tensor_reduce(near, far)
        down_away = down_grad.away([swish_away])
        return parts[1:], down_away, up_grad.away_halves([down_away])

    second_parts, down_away, up_away = region(
        second_sum, halves(feed_near[3]), (feed_two[3], feed_three[3])
    )
    second_parts = (feed_near[3], *second_parts)
    down_grad.came[0] = down_grad.hop(0, down_away)
    up_grad.came[0] = (up_grad.hop(0, up_away[0]), None)

    middle_grad, own_rows, mlp_norm_part = grid_call(
        middle_back_kernel,
        tiles,
        [own_spec] + [tile_spec] * 4 + [fixed((1, width))],
        [tile_spec, tile_spec, fixed((1, width))],
        [struct((length, width), f32), struct((length, width), bf16), struct((1, width), f32)],
        [place_index, cotangent, *second_parts, middle, gain_two],
        prefetch=1,
    )

    def branch_back(first, second, mixed, gates, queries, run, at, into=None):
        return grid_call(
            branch_back_kernel,
            (half,),
            [
                whole_block, whole_block, fixed((DK, width)), row_spec(DK), row_spec(DK), fixed((1, DK)),
                row_spec(DK), row_spec(DK),
            ],
            [row_spec(DK), row_spec(DK), line(1, DK), chunk_spec(devices, at)],
            [rows_of(DK, bf16), rows_of(DK, bf16), struct((half, 1, DK), f32), chunks],
            [first, second, out_weight, mixed, gates, gain, queries, run],
            into=() if into is None else [(into, 3)],
        )

    first_row = swap(own_rows, "tensor", 1)

    def gather_back(own_rows, first_row):
        second_row = swap(own_rows, "tensor", 2)
        *near, state_back = branch_back(
            own_rows, first_row, mixed_near, gates_near, queries_near, run_near, half
        )
        third_row = swap(hold(second_row, [near[0]]), "tensor", 1)
        *far, state_back = branch_back(
            second_row, third_row, mixed_far, gates_far, queries_far, run_far, 0, state_back
        )
        return second_row, third_row, near, far, state_back

    second_row, third_row, near, far, state_back = region(gather_back, own_rows, first_row)
    rows = [(values, 0) for values in (own_rows, first_row, second_row, third_row)]
    gate_back_near, mixed_back_near, gain_back_near = near
    gate_back_far, mixed_back_far, gain_back_far = far
    norms = blocks(norm_near, norm_far)

    far_bits = [bits[0], *bits[2:], bits[1]]
    out_grad = Scatter(rows, [blocks(branch_near, branch_far)], far_bits, True)
    gate_grad = Scatter(norms, [blocks(gate_back_near, gate_back_far)], bits)

    def states_back(state_back):
        swish_one = swish_grad.one([state_back])
        gate_away = gate_grad.away([swish_one])
        return (
            deal(state_back), swish_one, gate_away, out_grad.away([gate_away]),
            tensor_reduce(halves(feed_near[4]), (feed_two[4], feed_three[4]))[0],
        )

    came, swish_one, gate_away, out_away, output_parts = region(states_back, state_back)

    def states_out(came, swish_one, out_away, gate_away, output_parts):
        up_one = up_grad.one([came])
        own = sum((part.astype(f32) for part in output_parts), middle).astype(bf16)
        return (
            deal(carried(came, lines, True)), swish_grad.hop(1, swish_one), out_grad.hop(0, out_away),
            up_one, down_grad.one([up_one]), [own, swap(own, "tensor", 1), swap(own, "tensor", 2)],
            gate_grad.hop(0, gate_away),
        )

    (
        outgoing, swish_grad.came[1], out_grad.came[0], up_one, down_one, output_blocks,
        gate_grad.came[0],
    ) = region(states_out, came, swish_one, out_away, gate_away, output_parts)

    def mix_back(queries, keys, values, mixed_back, run, scores, incoming, at, rank_rows, after):
        return grid_call(
            mix_back_kernel,
            (half,),
            [row_spec(DK)] * 5
            + [square(length)]
            + [state_specs[1 if at else 0], chunk_spec(devices, at)]
            + [row_spec(rank), fixed((rank, DK)), fixed((1, DK))],
            [row_spec(DK)] * 3 + [line(rank, length), line(rank, DK), line(1, DK)],
            [rows_of(DK, bf16)] * 3
            + [
                struct((half, rank, length), f32),
                struct((half, rank, DK), f32),
                struct((half, 1, DK), f32),
            ],
            [
                queries, keys, values, mixed_back, run, scores, incoming, outgoing,
                rank_rows, rank_up, bias,
            ],
            after=after,
        )

    def first_part(query_back, key_back, value_back, gate_back, at, into=()):
        tile = 512
        pairs = [
            (query_back, query_weight),
            (key_back, key_weight),
            (value_back, value_weight),
            (gate_back, gate_weight),
        ]
        return grid_call(
            sum_kernel,
            (width // tile,),
            [pl.BlockSpec((half_rows, DK), lambda j: (0, 0))] * 4
            + [pl.BlockSpec((tile, DK), lambda j: (j, 0))] * 4,
            [pl.BlockSpec((1, length, tile), lambda j: (at, 0, j))] * 2,
            [struct((half, length, width), bf16)] * 2,
            [*[p[0] for p in pairs], *[p[1] for p in pairs]],
            into=into,
        )

    def in_order(blocks, after=()):
        whole = pl.BlockSpec((length, width), lambda k, order: (0, 0))
        return grid_call(
            place_kernel,
            (4,),
            [whole] * 4,
            pl.BlockSpec((1, length, width), lambda k, order: (order[k], 0, 0)),
            struct((seq_count, length, width), bf16),
            [order, *blocks],
            prefetch=1,
            after=after,
        )

    def mixed_pair(near, far):
        query_key = Scatter(norms, [blocks(near[0], far[0]), blocks(near[1], far[1])], bits)
        return query_key, Scatter(norms, [blocks(near[2], far[2])], late_bits)

    def mixes_back(up_one, outgoing, down_one):
        swish_two = swish_grad.two([outgoing])
        gate_one = gate_grad.one([swish_two])
        near = mix_back(
            queries_near, keys_near, values_near, mixed_back_near, run_near, scores_near,
            incoming_near, half, rank_near, [swish_two],
        )
        far = mix_back(
            queries_far, keys_far, values_far, mixed_back_far, run_far, scores_far,
            incoming_far, 0, rank_far, [near[5]],
        )
        query_key, value = mixed_pair(near, far)
        keep, send = first_part(*far[:3], gate_back_far, 1)
        keep, send = first_part(*near[:3], gate_back_near, 0, [(keep, 0), (send, 1)])
        query_key_away = query_key.away([send])
        value_away = value.away([query_key_away])
        return (
            up_grad.hop(1, up_one), swish_grad.hop(2, swish_two), down_grad.hop(1, down_one),
            gate_grad.hop(1, gate_one), near, far, query_key_away, value_away,
            keep, send, up_grad.hop_rest(up_away[1]),
        )

    (
        up_grad.came[1], swish_grad.came[2], down_grad.came[1], gate_grad.came[1], near, far, query_key_away,
        value_away, first_keep, first_send, up_rest,
    ) = region(mixes_back, up_one, outgoing, down_one)
    up_grad.came[0] = (up_grad.came[0][0], up_rest)

    def first_sum(keep, send, output_second):
        came = swap(send, "tensor", 1)
        output_third = swap(output_second, "tensor", 1)
        gate_two = gate_grad.two([send])
        down_two = down_grad.two([gate_two])
        second = (keep[1].astype(f32) + came[1].astype(f32)).astype(bf16)
        return came, second, gate_two, down_two, output_third

    first_came, first_second, gate_two, down_two, output_third = region(
        first_sum, first_keep, first_send, output_blocks[2]
    )
    output_blocks.append(output_third)
    rank_part_near, up_part_near, bias_part_near = near[3:]
    rank_part_far, up_part_far, bias_part_far = far[3:]
    query_key_grad, value_grad = mixed_pair(near, far)

    def third_window(query_key_away, value_away, gate_two, down_two, first_second):
        rank_part = jnp.concatenate([rank_part_near, rank_part_far], axis=0)
        rank_part = lax.all_to_all(jnp.take(rank_part, order, axis=0), "tensor", 0, 0)
        return (
            query_key_grad.hop(0, query_key_away), value_grad.hop(0, value_away),
            gate_grad.hop(2, gate_two), down_grad.hop(2, down_two), up_grad.two(),
            swish_grad.last(), jnp.sum(rank_part, axis=0).astype(bf16), swap(first_second, "tensor", 2),
            out_grad.one([down_two]), in_order(output_blocks, [down_two]),
        )

    (
        query_key_grad.came[0], value_grad.came[0], gate_grad.came[2], down_grad.came[2], up_two,
        swish_share, rank_back, first_last, out_one, layer_output,
    ) = region(third_window, query_key_away, value_away, gate_two, down_two, first_second)
    query_key_one = query_key_grad.one()
    value_one = value_grad.one([query_key_one])

    input_rows, attn_norm_part = grid_call(
        input_back_kernel,
        tiles,
        [own_spec]
        + [pl.BlockSpec((1, tile, width), lambda b, *_: (0, b, 0))] * 2
        + [
            tile_spec,
            pl.BlockSpec((rank, tile), lambda b, *_: (0, b)), fixed((width, rank)), tile_spec,
            fixed((1, width)),
        ],
        [tile_spec, fixed((1, width))],
        [struct((length, width), bf16), struct((1, width), f32)],
        [
            place_index, layer_input, first_keep, first_came, first_last, rank_back, rank_down, middle_grad,
            attn_norm.reshape(1, width),
        ],
        prefetch=1,
        after=[value_one],
    )
    rank_down_part = contract(rank_back, norm_near[:length], 1, 0)
    own_part = jnp.concatenate([rank_down_part, mlp_norm_part, attn_norm_part], axis=0)
    shared = jnp.concatenate(
        [
            sum(up_part_near) + sum(up_part_far),
            sum(bias_part_near) + sum(bias_part_far),
            sum(gain_back_near) + sum(gain_back_far),
        ],
        axis=0,
    )
    column = width // devices
    own_part = jnp.moveaxis(own_part.reshape(rank + 2, devices, column), 1, 0)
    own_size = (rank + 2) * column
    mail = jnp.concatenate(
        [
            own_part.reshape(devices, own_size),
            jnp.broadcast_to(shared.reshape(1, -1), (devices, shared.size)),
        ],
        axis=1,
    )

    def summed(mail):
        mail = mail.reshape(devices, 1, -1).astype(bf16)
        return jnp.sum(lax.all_to_all(mail, "seq", 0, 0).astype(f32), axis=0)

    def fourth_window(query_key_one, value_one, up_two, out_one, input_rows):
        return (
            swap(input_rows, "tensor", 2),
            query_key_grad.hop(1, query_key_one), value_grad.hop(1, value_one), up_grad.hop(2, up_two),
            out_grad.hop(1, out_one), gate_grad.last(), down_grad.last(),
        )

    (
        second_rows, query_key_grad.came[1], value_grad.came[1], up_grad.came[2], out_grad.came[1],
        gate_share, down_share,
    ) = region(fourth_window, query_key_one, value_one, up_two, out_one, input_rows)


    def fifth_window(input_rows, second_rows, mail):
        query_key_two = query_key_grad.two([second_rows])
        value_two = value_grad.two([query_key_two])
        out_two = out_grad.two([value_two])
        first_rows, third_rows = swap(input_rows, "tensor", 1), swap(second_rows, "tensor", 1)
        return (
            query_key_grad.hop(2, query_key_two), value_grad.hop(2, value_two), out_grad.hop(2, out_two),
            in_order([input_rows, first_rows, second_rows, third_rows]), up_grad.last(), summed(mail),
            [query_key_grad.most([out_two]), value_grad.most([out_two]), out_grad.most([out_two])],
        )

    query_key_grad.came[2], value_grad.came[2], out_grad.came[2], input_grad, up_share, mail, mosts = region(
        fifth_window, input_rows, second_rows, mail
    )

    def sixth_window(mail):
        parts = mail.reshape(-1)[:own_size].reshape(rank + 2, column)
        query_key = query_key_grad.finish(mosts[0])
        return (
            query_key[:, :DK], query_key[:, DK:], value_grad.finish(mosts[1]), out_grad.finish(mosts[2]),
            sum_over(parts, "tensor"),
        )

    query_share, key_share, value_share, out_share, own_part = region(sixth_window, mail)
    shared = mail.reshape(-1)[own_size:].reshape(rank + 2, DK)
    return (
        layer_output,
        input_grad,
        own_part[rank + 1],
        query_share,
        key_share,
        value_share,
        gate_share,
        own_part[:rank].T,
        shared[:rank],
        shared[rank],
        shared[rank + 1],
        out_share,
        own_part[rank],
        swish_share,
        up_share,
        down_share,
    )


def solution(mesh):
    return jax.shard_map(
        local,
        mesh=mesh,
        in_specs=(
            P(None, "seq", None),
            P(),
            P(None, "tensor"),
            P(None, "tensor"),
            P(None, "tensor"),
            P(None, "tensor"),
            P(),
            P(None, "tensor"),
            P("tensor"),
            P("tensor"),
            P("tensor", None),
            P(),
            P(None, "tensor"),
            P(None, "tensor"),
            P("tensor", None),
            P(None, "seq", None),
        ),
        out_specs=(
            P(None, "seq", None),
            P(None, "seq", None),
            P("seq"),
            P("seq", "tensor"),
            P("seq", "tensor"),
            P("seq", "tensor"),
            P("seq", "tensor"),
            P("seq", None),
            P(None, "tensor"),
            P("tensor"),
            P("tensor"),
            P("tensor", "seq"),
            P("seq"),
            P("seq", "tensor"),
            P("seq", "tensor"),
            P("tensor", "seq"),
        ),
        check_vma=False,
    )
```
